32 devices in a mesh: tile: 16 (over z, y, x), sub: 2 (over core).
Axes of the slice: x: 2, y: 2, z: 4, core: 2. Of those that a mesh axis runs over, the one named last changes fastest.
Arguments:
- grid: bfloat16 [32768, 512], P(('tile', 'sub')), may hold values from -6 to 6
- g2m_owner: int32 [256], P(('tile', 'sub')), may hold values from 0 to 31, as said below
- g2m_weight: float32 [32768], P(('tile', 'sub')), may hold values from 0.1 to 1
- m2g_owner: int32 [256], P(('tile', 'sub')), may hold values from 0 to 31, as said below
- m2g_weight: float32 [32768], P(('tile', 'sub')), may hold values from 0.2 to 2
- mesh_feat: bfloat16 [4096, 512], P(('tile', 'sub')), may hold values from -6 to 6
- neighbours: int32 [32, 3], P(('tile', 'sub')), may hold values from 0 to 31, as said below
- enc_w1: bfloat16 [512, 2048], replicated, may hold values from -0.25 to 0.25
- enc_w2: bfloat16 [2048, 512], replicated, may hold values from -0.125 to 0.125
- attn_gain: float32 [1, 512], replicated, may hold values from 0.25 to 1.75
- w_qkv: bfloat16 [1, 512, 1536], replicated, may hold values from -1 to 1
- w_out: bfloat16 [1, 512, 512], replicated, may hold values from -0.25 to 0.25
- dec_w1: bfloat16 [512, 2048], replicated, may hold values from -0.25 to 0.25
- dec_w2: bfloat16 [2048, 512], replicated, may hold values from -0.125 to 0.125
Outputs:
- decoded: bfloat16 [32768, 512], P(('tile', 'sub'))
- mesh_out: bfloat16 [4096, 512], P(('tile', 'sub'))
The draws below stay inside these ranges and needn't reach their ends.
Inputs may be any that keep to these rules, and one draw needn't show every extreme that they name: g2m_owner[b] equals b // 8 + e modulo 32 with e between -2 and 2; both -2 and 2 occur. m2g_owner[b] equals b // 8 + e modulo 32 with e between -2 and 2; both -2 and 2 occur. `neighbours`: row m holds three distinct blocks among m - 2, m - 1, m + 1, m + 2 modulo 32.
All inputs are finite; a program needn't handle non-finite values.
Results may differ from the reference program's by a relative error of at most 0.015.
Values may be sent and summed in bfloat16 or wider, within the bound.
No kernel may reach another device: no remote copies, remote signals or barrier semaphores. Data moves between devices by JAX's collectives and lax.ppermute only.
A program may use at most 64 MiB of HBM per device.

```python
import math
import jax
import jax.numpy as jnp
from jax import lax

D = 512
FF = 2048
H = 4
HD = 128
BLK = 128
LAYERS = 1
GB = 8
MB = 32
GRID_BLOCKS = 256
GRID = 32768
MESH = 4096


def owner_common(key, salt):
    offset = jax.random.randint(jax.random.fold_in(key, salt), (GRID_BLOCKS,), -2, 3)
    offset = offset.at[0].set(2).at[1].set(-2)
    base = jnp.arange(GRID_BLOCKS, dtype=jnp.int32) // GB
    return ((base + offset) % MB).astype(jnp.int32)


def draw_g2m_owner(key, part):
    return owner_common(key, 11)


def draw_m2g_owner(key, part):
    return owner_common(key, 23)


def draw_neighbours(key, part):
    keyset = jax.random.split(jax.random.fold_in(key, 5), MB)
    orders = jax.vmap(lambda single: jax.random.permutation(single, 4))(keyset)[:, :3]
    choices_table = jnp.array([-2, -1, 1, 2], dtype=jnp.int32)
    offsets = choices_table[orders]
    base = jnp.arange(MB, dtype=jnp.int32)[:, None]
    return ((base + offsets) % MB).astype(jnp.int32)


def draw_mesh_feat(key, part):
    base_key = jax.random.fold_in(key, 31)
    result = jnp.clip(jax.random.normal(base_key, (MESH, D), jnp.float32), -6.0, 6.0)
    return result.astype(jnp.bfloat16)


def draw_w_qkv(key, part):
    base_key = jax.random.fold_in(key, 41)
    scale = jnp.float32(D) ** (-0.5)
    result = jnp.clip(jax.random.normal(base_key, (LAYERS, D, 3 * D), jnp.float32), -6.0, 6.0) * scale
    return result.astype(jnp.bfloat16)


def steps_of(stream_key, shape, shards, smallest, largest):
    level = 1.0
    for position, parts in shards:
        steps = jax.random.uniform(jax.random.fold_in(jax.random.fold_in(stream_key, 6), position), (parts,), jnp.float32, smallest / len(shards), largest / len(shards))
        level = level * jnp.repeat(jnp.exp(steps), shape[position] // parts).reshape((-1,) + (1,) * (len(shape) - 1 - position))
    return level


def centred(key, shape, width, most, pieces=(), kind=jnp.bfloat16):
    values = jax.random.normal(key, shape, jnp.float32) * width
    if len(pieces) > 0:
        values = steps_of(key, shape, pieces, -0.22, 0.18) * values
    return jnp.clip(values, min=-most, max=most).astype(kind)


def setup_inputs(seed: int = 0) -> dict:
    key_list = jax.random.split(jax.random.key(seed), 15)
    grid = centred(key_list[0], (GRID, D), 1.0, 6.0, ((0, 32),))
    g2m_owner = draw_g2m_owner(jax.random.fold_in(key_list[14], 71), 0)
    g2m_weight = jnp.clip(jnp.exp(math.log(1.0) - 2.3025851 * jax.random.uniform(key_list[2], (GRID,), jnp.float32) ** steps_of(key_list[2], (GRID,), ((0, 32),), -0.2, 0.2)), 0.1, 1.0)
    m2g_owner = draw_m2g_owner(jax.random.fold_in(key_list[14], 71), 0)
    m2g_weight = jnp.clip(jnp.exp(math.log(2.0) - 2.3025851 * jax.random.uniform(key_list[4], (GRID,), jnp.float32) ** steps_of(key_list[4], (GRID,), ((0, 32),), -0.2, 0.2)), 0.2, 2.0)
    mesh_feat = draw_mesh_feat(jax.random.fold_in(key_list[14], 71), 0)
    neighbours = draw_neighbours(jax.random.fold_in(key_list[14], 71), 0)
    enc_w1 = centred(key_list[7], (D, FF), D ** -0.5, 0.25)
    enc_w2 = centred(key_list[8], (FF, D), FF ** -0.5, 0.125)
    attn_gain = jnp.clip(1.0 + 0.15 * jax.random.normal(key_list[9], (LAYERS, D), jnp.float32), 0.25, 1.75)
    w_qkv = draw_w_qkv(jax.random.fold_in(key_list[14], 71), 0)
    w_out = centred(key_list[11], (LAYERS, D, D), D ** -0.5, 0.25)
    dec_w1 = centred(key_list[12], (D, FF), D ** -0.5, 0.25)
    dec_w2 = centred(key_list[13], (FF, D), FF ** -0.5, 0.125)
    return dict(grid=grid, g2m_owner=g2m_owner, g2m_weight=g2m_weight, m2g_owner=m2g_owner, m2g_weight=m2g_weight, mesh_feat=mesh_feat, neighbours=neighbours, enc_w1=enc_w1, enc_w2=enc_w2, attn_gain=attn_gain, w_qkv=w_qkv, w_out=w_out, dec_w1=dec_w1, dec_w2=dec_w2)


def feed(rows, first, second):
    hidden = jnp.dot(rows, first, preferred_element_type=jnp.float32)
    active = jax.nn.silu(hidden).astype(jnp.bfloat16)
    return (rows.astype(jnp.float32) + jnp.dot(active, second, preferred_element_type=jnp.float32)).astype(jnp.bfloat16)

def mlp_blocks(rows, first, second):
    grouped = rows.reshape(MB, GB * BLK, D)
    result = lax.map(lambda piece: feed(piece, first, second), grouped)
    return result.reshape(GRID, D)

def reference(grid, g2m_owner, g2m_weight, m2g_owner, m2g_weight, mesh_feat, neighbours, enc_w1, enc_w2, attn_gain, w_qkv, w_out, dec_w1, dec_w2):
    encoded = mlp_blocks(grid, enc_w1, enc_w2)
    contrib = (g2m_weight[:, None] * encoded.astype(jnp.float32)).reshape(GRID_BLOCKS, BLK, D)
    added = jax.ops.segment_sum(contrib, g2m_owner, num_segments=MB)
    state = mesh_feat.astype(jnp.float32).reshape(MB, BLK, D) + added
    for layer in range(LAYERS):
        mean_sq = lax.optimization_barrier(jnp.mean(state * state, axis=-1, keepdims=True))
        normed = (state * lax.rsqrt(mean_sq + 1e-06) * attn_gain[layer]).astype(jnp.bfloat16)
        qkv = jnp.dot(normed.reshape(MESH, D), w_qkv[layer], preferred_element_type=jnp.float32).astype(jnp.bfloat16)
        qkv = qkv.reshape(MB, BLK, 3 * D)
        query = qkv[:, :, :D]
        keys = qkv[:, :, D:2 * D]
        values = qkv[:, :, 2 * D:]

        def attend(block):
            listed = jnp.concatenate([block[None], neighbours[block]]).astype(jnp.int32)
            kk = keys[listed].reshape(4 * BLK, H, HD).astype(jnp.float32)
            vv = values[listed].reshape(4 * BLK, H, HD).astype(jnp.float32)
            qq = query[block].reshape(BLK, H, HD).astype(jnp.float32)
            scores = jnp.einsum('qhd,khd->hqk', qq, kk) / jnp.sqrt(jnp.float32(HD))
            probs = jax.nn.softmax(scores, axis=-1).astype(jnp.bfloat16)
            mixed = jnp.einsum('hqk,khd->qhd', probs.astype(jnp.float32), vv)
            return mixed.astype(jnp.bfloat16).reshape(BLK, D)
        attended = lax.map(attend, jnp.arange(MB, dtype=jnp.int32))
        state = state + jnp.dot(attended.reshape(MESH, D), w_out[layer], preferred_element_type=jnp.float32).reshape(MB, BLK, D)
    mesh_out = state.astype(jnp.bfloat16)
    picked = mesh_out[m2g_owner].reshape(GRID, D)
    dec_in = (encoded.astype(jnp.float32) + m2g_weight[:, None] * picked.astype(jnp.float32)).astype(jnp.bfloat16)
    decoded = mlp_blocks(dec_in, dec_w1, dec_w2)
    return (decoded, mesh_out.reshape(MESH, D))
```

```python
import functools

import jax
import jax.numpy as jnp
from jax import lax
from jax.experimental import pallas as pl
from jax.experimental.pallas import tpu as pltpu
from jax.sharding import PartitionSpec as P

HD = 128
REACH = 2
EXTRA = 16
AXES = ("tile", "sub")
BF16 = jnp.bfloat16
F32 = jnp.float32
VMEM = pl.BlockSpec(memory_space=pltpu.VMEM)
SMEM = pl.BlockSpec(memory_space=pltpu.SMEM)
ANY = pl.BlockSpec(memory_space=pl.ANY)


def swapped(block):
    count = lax.axis_size(AXES)
    return lax.ppermute(block, AXES, [(i, i ^ 1) for i in range(count)])


def from_outward(block, chips):
    count = lax.axis_size(AXES)
    route = []
    for i in range(count):
        step = 2 * chips - 1
        route.append((i, (i + step if i % 2 else i - step) % count))
    return lax.ppermute(block, AXES, route)


def tiles_of(rows, columns):
    return min(rows, 256), min(columns, 512)


def weight_copies(first_hbm, second_hbm, first, second, sems, part):
    parts = first.shape[1] // part
    ones, twos = [], []
    for j in range(parts):
        cut = pl.ds(j * part, part)
        ones.append(pltpu.make_async_copy(first_hbm.at[:, cut], first.at[:, cut], sems.at[0, j]))
        twos.append(pltpu.make_async_copy(second_hbm.at[cut], second.at[cut], sems.at[1, j]))
    return ones, twos


def hidden_layer(x_ref, first, act, ones, tile, part, arrive):
    for j, copy in enumerate(ones):
        copy.wait()
        cols = slice(j * part, (j + 1) * part)
        for r in range(x_ref.shape[0] // tile):
            if j == 0:
                arrive(r)
            cut = slice(r * tile, (r + 1) * tile)
            half = jnp.dot(x_ref[cut, :] * BF16(0.5), first[:, cols], preferred_element_type=F32)
            act[cut, cols] = (half * jnp.tanh(half) + half).astype(BF16)


def encode_kernel(
    slots, code, weight_ref, feat_ref, x_hbm, first_hbm, second_hbm,
    enc_hbm, msg_ref, base_ref, loc_ref,
    x_ref, first, second, act, total, sems, io_sems,
):
    rows = feat_ref.shape[0]
    depth = feat_ref.shape[1]
    tile, part = tiles_of(x_ref.shape[0], first.shape[1])
    tiles = x_ref.shape[0] // tile
    ones, twos = weight_copies(first_hbm, second_hbm, first, second, sems, part)
    loads = [
        pltpu.make_async_copy(x_hbm.at[pl.ds(r * tile, tile)], x_ref.at[pl.ds(r * tile, tile)], io_sems.at[0, r])
        for r in range(tiles)
    ]
    loads[0].start()
    ones[0].start()
    for copy in loads[1:] + ones[1:] + twos:
        copy.start()
    total[...] = jnp.zeros_like(total)
    columns = jnp.transpose(weight_ref[...])
    hidden_layer(x_ref, first, act, ones, tile, part, lambda r: loads[r].wait())
    for copy in twos:
        copy.wait()
    stores = []
    for r in range(tiles):
        cut = slice(r * tile, (r + 1) * tile)
        out = jnp.dot(act[cut, :], second[...], preferred_element_type=F32)
        x_ref[cut, :] = (x_ref[cut, :].astype(F32) + out).astype(BF16)
        copy = pltpu.make_async_copy(x_ref.at[pl.ds(r * tile, tile)], enc_hbm.at[pl.ds(r * tile, tile)], io_sems.at[1, r])
        copy.start()
        stores.append(copy)
        for b in range(r * tile // rows, (r + 1) * tile // rows):
            slot = slots[b]
            block = x_ref[b * rows:(b + 1) * rows, :].astype(F32)
            total[slot] += columns[:, b:b + 1] * block
    spot = lax.broadcasted_iota(jnp.int32, (EXTRA, depth), 1)
    row = lax.broadcasted_iota(jnp.int32, (EXTRA, depth), 0)
    value = code[0].astype(F32)
    msg_ref[:rows, :] = total[0].astype(BF16)
    msg_ref[rows:, :] = jnp.where((spot == 1) & (row == 0), value, 0.0).astype(BF16)
    base_ref[:rows, :] = total[4].astype(BF16)
    base_ref[rows:2 * rows, :] = total[3].astype(BF16)
    base_ref[2 * rows:, :] = jnp.where((spot == 0) & (row == 0), value, 0.0).astype(BF16)
    loc_ref[:rows, :] = total[1]
    loc_ref[rows:, :] = total[2] + feat_ref[...].astype(F32)
    for copy in stores:
        copy.wait()


def encode(slots, code, weights, feat, grid, first, second):
    cells, depth = grid.shape
    hidden = first.shape[1]
    rows = feat.shape[0]
    tile, part = tiles_of(cells, hidden)
    return pl.pallas_call(
        encode_kernel,
        out_shape=(
            jax.ShapeDtypeStruct((cells, depth), BF16),
            pltpu.VMEM((rows + EXTRA, depth), BF16),
            pltpu.VMEM((2 * rows + EXTRA, depth), BF16),
            pltpu.VMEM((2 * rows, depth), F32),
        ),
        in_specs=[SMEM, SMEM, VMEM, VMEM, ANY, ANY, ANY],
        out_specs=(ANY, VMEM, VMEM, VMEM),
        scratch_shapes=[
            pltpu.VMEM((cells, depth), BF16),
            pltpu.VMEM((depth, hidden), BF16),
            pltpu.VMEM((hidden, depth), BF16),
            pltpu.VMEM((cells, hidden), BF16),
            pltpu.VMEM((2 * REACH + 1, rows, depth), F32),
            pltpu.SemaphoreType.DMA((2, hidden // part)),
            pltpu.SemaphoreType.DMA((2, cells // tile)),
        ],
        compiler_params=pltpu.CompilerParams(vmem_limit_bytes=32 << 20),
        cost_estimate=pl.CostEstimate(
            flops=4 * cells * depth * hidden, bytes_accessed=4 * (cells + hidden) * depth, transcendentals=cells * hidden
        ),
        name="encode",
    )(slots, code, weights, feat, grid, first, second)


def attend_kernel(
    dropped, own_ref, pair_ref, near_ref, far_ref, behind_ref, gain_ref, qkv_hbm, out_hbm,
    mesh_ref, ring_ref,
    w_qkv, w_out, normed, query, key_value, mixed, sems,
):
    rows, depth = own_ref.shape
    heads = depth // HD
    span = 2 * REACH + 1
    copies = [
        pltpu.make_async_copy(qkv_hbm, w_qkv, sems.at[0]),
        pltpu.make_async_copy(out_hbm, w_out, sems.at[1]),
    ]
    for copy in copies:
        copy.start()
    blocks = [
        behind_ref[...], pair_ref[:rows, :], pair_ref[rows:, :],
        near_ref[rows:, :], near_ref[:rows, :], far_ref[rows:, :], far_ref[:rows, :],
    ]
    for n, block in enumerate(blocks):
        state = block.astype(F32)
        scale = lax.rsqrt(jnp.mean(state * state, axis=-1, keepdims=True) + 1e-6)
        normed[n * rows:(n + 1) * rows, :] = (state * scale * gain_ref[...]).astype(BF16)
    copies[0].wait()
    key_value[...] = jnp.dot(normed[...], w_qkv[:, depth:], preferred_element_type=F32).astype(BF16)
    query[...] = jnp.dot(
        normed[REACH * rows:(REACH + 3) * rows, :], w_qkv[:, :depth], preferred_element_type=F32
    ).astype(BF16)
    lane_block = lax.broadcasted_iota(jnp.int32, (rows, span * rows), 1) // rows
    for p in range(3):
        keep = lane_block != dropped[p]
        window = slice(p * rows, (p + span) * rows)
        for h in range(heads):
            cols = slice(h * HD, (h + 1) * HD)
            scores = lax.dot_general(
                query[p * rows:(p + 1) * rows, cols], key_value[window, cols],
                (((1,), (1,)), ((), ())), preferred_element_type=F32,
            ) * (HD ** -0.5)
            scores = jnp.where(keep, scores, -jnp.inf)
            grown = jnp.exp(scores - jnp.max(scores, axis=-1, keepdims=True))
            share = 1.0 / jnp.sum(grown, axis=-1, keepdims=True)
            value = key_value[window, depth + h * HD:depth + (h + 1) * HD]
            mixed[p * rows:(p + 1) * rows, cols] = (
                jnp.dot(grown.astype(BF16), value, preferred_element_type=F32) * share
            ).astype(BF16)
    copies[1].wait()
    added = jnp.dot(mixed[...], w_out[...], preferred_element_type=F32)
    mesh_own = (own_ref[...] + added[:rows, :]).astype(BF16)
    mesh_ref[...] = mesh_own
    ring_ref[:rows, :] = mesh_own
    ring_ref[rows:2 * rows, :] = (near_ref[rows:, :].astype(F32) + added[rows:2 * rows, :]).astype(BF16)
    ring_ref[2 * rows:, :] = (near_ref[:rows, :].astype(F32) + added[2 * rows:, :]).astype(BF16)


def attend(dropped, own, pair, near, far, behind, gain, w_qkv, w_out):
    rows, depth = own.shape
    count = 2 * REACH + 3
    return pl.pallas_call(
        attend_kernel,
        out_shape=(
            jax.ShapeDtypeStruct((rows, depth), BF16),
            pltpu.VMEM((3 * rows, depth), BF16),
        ),
        in_specs=[SMEM, VMEM, VMEM, VMEM, VMEM, VMEM, VMEM, ANY, ANY],
        out_specs=(VMEM, VMEM),
        scratch_shapes=[
            pltpu.VMEM(w_qkv.shape, BF16),
            pltpu.VMEM(w_out.shape, BF16),
            pltpu.VMEM((count * rows, depth), BF16),
            pltpu.VMEM((3 * rows, depth), BF16),
            pltpu.VMEM((count * rows, 2 * depth), BF16),
            pltpu.VMEM((3 * rows, depth), BF16),
            pltpu.SemaphoreType.DMA((2,)),
        ],
        compiler_params=pltpu.CompilerParams(vmem_limit_bytes=32 << 20),
        name="attend",
    )(dropped, own, pair, near, far, behind, gain, w_qkv, w_out)


def decode_kernel(
    slots, weight_ref, ring_ref, back_ref, enc_hbm, first_hbm, second_hbm,
    out_hbm,
    x_ref, first, second, act, mesh, sems, io_sems,
):
    rows = back_ref.shape[0] // 2
    tile, part = tiles_of(x_ref.shape[0], first.shape[1])
    tiles = x_ref.shape[0] // tile
    ones, twos = weight_copies(first_hbm, second_hbm, first, second, sems, part)
    loads = [
        pltpu.make_async_copy(enc_hbm.at[pl.ds(r * tile, tile)], x_ref.at[pl.ds(r * tile, tile)], io_sems.at[0, r])
        for r in range(tiles)
    ]
    loads[0].start()
    ones[0].start()
    for copy in loads[1:] + ones[1:] + twos:
        copy.start()
    mesh[0] = back_ref[rows:, :]
    mesh[1] = back_ref[:rows, :]
    for n in range(3):
        mesh[2 + n] = ring_ref[n * rows:(n + 1) * rows, :]
    columns = jnp.transpose(weight_ref[...])

    def arrive(r):
        loads[r].wait()
        for b in range(r * tile // rows, (r + 1) * tile // rows):
            cut = slice(b * rows, (b + 1) * rows)
            read = mesh[slots[b]].astype(F32)
            x_ref[cut, :] = (x_ref[cut, :].astype(F32) + columns[:, b:b + 1] * read).astype(BF16)

    hidden_layer(x_ref, first, act, ones, tile, part, arrive)
    for copy in twos:
        copy.wait()
    stores = []
    for r in range(tiles):
        cut = slice(r * tile, (r + 1) * tile)
        out = jnp.dot(act[cut, :], second[...], preferred_element_type=F32)
        x_ref[cut, :] = (x_ref[cut, :].astype(F32) + out).astype(BF16)
        copy = pltpu.make_async_copy(x_ref.at[pl.ds(r * tile, tile)], out_hbm.at[pl.ds(r * tile, tile)], io_sems.at[1, r])
        copy.start()
        stores.append(copy)
    for copy in stores:
        copy.wait()


def decode(slots, weights, ring, back, encoded, first, second):
    cells, depth = encoded.shape
    hidden = first.shape[1]
    rows = back.shape[0] // 2
    tile, part = tiles_of(cells, hidden)
    return pl.pallas_call(
        decode_kernel,
        out_shape=jax.ShapeDtypeStruct((cells, depth), BF16),
        in_specs=[SMEM, VMEM, VMEM, VMEM, ANY, ANY, ANY],
        out_specs=ANY,
        scratch_shapes=[
            pltpu.VMEM((cells, depth), BF16),
            pltpu.VMEM((depth, hidden), BF16),
            pltpu.VMEM((hidden, depth), BF16),
            pltpu.VMEM((cells, hidden), BF16),
            pltpu.VMEM((2 * REACH + 1, rows, depth), BF16),
            pltpu.SemaphoreType.DMA((2, hidden // part)),
            pltpu.SemaphoreType.DMA((2, cells // tile)),
        ],
        compiler_params=pltpu.CompilerParams(vmem_limit_bytes=32 << 20),
        cost_estimate=pl.CostEstimate(
            flops=4 * cells * depth * hidden, bytes_accessed=4 * (cells + hidden) * depth, transcendentals=cells * hidden
        ),
        name="decode",
    )(slots, weights, ring, back, encoded, first, second)


def on_device(
    grid, g2m_owner, g2m_weight, m2g_owner, m2g_weight, mesh_feat, neighbours,
    enc_w1, enc_w2, attn_gain, w_qkv, w_out, dec_w1, dec_w2,
):
    mine = lax.axis_index(AXES)
    count = lax.axis_size(AXES)
    rows, depth = mesh_feat.shape
    nblocks = g2m_owner.shape[0]
    outward = 2 * lax.axis_index("sub") - 1

    def offset(owner):
        return (owner - mine + REACH) % count - REACH

    absent = -jnp.sum(offset(neighbours[0]))
    loc_slots = outward * offset(g2m_owner) + REACH
    read_slots = outward * offset(m2g_owner) + REACH

    encoded, message, base, local = encode(
        loc_slots, absent[None], g2m_weight.reshape(nblocks, rows), mesh_feat, grid, enc_w1, enc_w2
    )
    arrived = swapped(message)
    outgoing = (
        base.astype(F32) + jnp.pad(arrived.astype(F32), ((rows, 0), (0, 0)))
    ).astype(BF16)
    arrived = from_outward(outgoing, 1)
    shares = local + arrived[:2 * rows].astype(F32)
    absents = arrived[2 * rows, :2].astype(F32).astype(jnp.int32)
    dropped = outward * jnp.concatenate([absent[None], absents]) + REACH
    halves = shares.reshape(2, rows, depth)
    other = swapped(halves[::-1].astype(BF16).reshape(2 * rows, depth))
    state = shares + other.astype(F32)
    pair = state.astype(BF16)
    near = from_outward(pair, 1)
    far = from_outward(pair, 2)
    behind = swapped(near[rows:])
    mesh_out, ring = attend(
        dropped, state[rows:], pair, near, far, behind, attn_gain, w_qkv[0], w_out[0]
    )
    back = swapped(ring[:2 * rows])
    decoded = decode(
        read_slots, m2g_weight.reshape(nblocks, rows), ring, back, encoded, dec_w1, dec_w2
    )
    return (decoded, mesh_out)


def solution(mesh):
    split = P(AXES, None)
    flat = P(AXES)
    in_specs = (split, flat, flat, flat, flat, split, split) + (P(),) * 7
    return jax.shard_map(
        on_device, mesh=mesh, in_specs=in_specs, out_specs=(split, split), check_vma=False
    )
```

```python
import functools

import jax
import jax.numpy as jnp
from jax import lax
from jax.experimental import pallas as pl
from jax.experimental.pallas import tpu as pltpu
from jax.sharding import PartitionSpec as P

HD = 128
REACH = 2
EXTRA = 16
AXES = ("tile", "sub")
BF16 = jnp.bfloat16
F32 = jnp.float32
VMEM = pl.BlockSpec(memory_space=pltpu.VMEM)
SMEM = pl.BlockSpec(memory_space=pltpu.SMEM)
ANY = pl.BlockSpec(memory_space=pl.ANY)


def swapped(block):
    count = lax.axis_size(AXES)
    return lax.ppermute(block, AXES, [(i, i ^ 1) for i in range(count)])


def from_outward(block, chips):
    count = lax.axis_size(AXES)
    route = []
    for i in range(count):
        step = 2 * chips - 1
        route.append((i, (i + step if i % 2 else i - step) % count))
    return lax.ppermute(block, AXES, route)


def tiles_of(rows, columns):
    return min(rows, 256), min(columns, 512)


def outward_of():
    return 2 * lax.axis_index("sub") - 1


def offset_of(owner, mine, count):
    return lax.rem(owner - mine + REACH + count, count) - REACH


def kept(shape, dtype=BF16):
    return pltpu.VMEM(shape, dtype)


def in_hbm(*arrays):
    return [pltpu.with_memory_space_constraint(a, pltpu.HBM) for a in arrays]


def hidden_layer(x_ref, first, act, tile, part, arrive, before):
    for j in range(first.shape[1] // part):
        before(j)
        cols = slice(j * part, (j + 1) * part)
        for r in range(x_ref.shape[0] // tile):
            if j == 0:
                arrive(r)
            cut = slice(r * tile, (r + 1) * tile)
            half = jnp.dot(x_ref[cut, :] * BF16(0.5), first[:, cols], preferred_element_type=F32)
            act[cut, cols] = (half * jnp.tanh(half) + half).astype(BF16)


def encode_kernel(
    owner, listed, weight_hbm, feat_hbm, x_hbm, first_hbm, second_hbm,
    enc_ref, msg_ref, base_ref, loc_ref,
    weight_ref, feat_ref, first, second, act, total, sems, io_sems,
):
    rows, depth = feat_ref.shape
    tile, part = tiles_of(enc_ref.shape[0], first.shape[1])
    tiles, parts = enc_ref.shape[0] // tile, first.shape[1] // part
    loads = [
        pltpu.make_async_copy(x_hbm.at[pl.ds(r * tile, tile)], enc_ref.at[pl.ds(r * tile, tile)], io_sems.at[r])
        for r in range(tiles)
    ]
    ones, twos = [], []
    for j in range(parts):
        cut = pl.ds(j * part, part)
        ones.append(pltpu.make_async_copy(first_hbm.at[:, cut], first.at[:, cut], sems.at[0, j]))
        twos.append(pltpu.make_async_copy(second_hbm.at[cut], second.at[cut], sems.at[1, j]))
    small = [
        pltpu.make_async_copy(weight_hbm, weight_ref, io_sems.at[tiles]),
        pltpu.make_async_copy(feat_hbm, feat_ref, io_sems.at[tiles + 1]),
    ]
    for copy in [loads[0], ones[0]] + loads[1:] + ones[1:] + twos + small:
        copy.start()
    mine, count = lax.axis_index(AXES), lax.axis_size(AXES)
    outward = outward_of()
    total[...] = jnp.zeros_like(total)
    hidden_layer(
        enc_ref, first, act, tile, part, lambda r: loads[r].wait(), lambda j: ones[j].wait()
    )
    for copy in twos + small:
        copy.wait()
    columns = jnp.transpose(weight_ref[...])
    for r in range(tiles):
        cut = slice(r * tile, (r + 1) * tile)
        out = jnp.dot(act[cut, :], second[...], preferred_element_type=F32)
        enc_ref[cut, :] = (enc_ref[cut, :].astype(F32) + out).astype(BF16)
        for b in range(r * tile // rows, (r + 1) * tile // rows):
            slot = outward * offset_of(owner[b], mine, count) + REACH
            block = enc_ref[b * rows:(b + 1) * rows, :].astype(F32)
            total[slot] += columns[:, b:b + 1] * block
    absent = sum(-offset_of(listed[0, n], mine, count) for n in range(listed.shape[1])).astype(F32)
    spot = lax.broadcasted_iota(jnp.int32, (EXTRA, depth), 1)
    msg_ref[:rows, :] = total[0].astype(BF16)
    msg_ref[rows:, :] = jnp.where(spot == 1, absent, 0.0).astype(BF16)
    base_ref[:rows, :] = total[4].astype(BF16)
    base_ref[rows:2 * rows, :] = total[3].astype(BF16)
    base_ref[2 * rows:, :] = jnp.where(spot == 0, absent, 0.0).astype(BF16)
    loc_ref[:rows, :] = total[1]
    loc_ref[rows:, :] = total[2] + feat_ref[...].astype(F32)


def encode(owner, listed, weights, feat, grid, first, second):
    cells, depth = grid.shape
    hidden = first.shape[1]
    rows = feat.shape[0]
    tile, part = tiles_of(cells, hidden)
    return pl.pallas_call(
        encode_kernel,
        out_shape=(
            kept((cells, depth)),
            kept((rows + EXTRA, depth)),
            kept((2 * rows + EXTRA, depth)),
            kept((2 * rows, depth), F32),
        ),
        in_specs=[SMEM, SMEM] + [ANY] * 5,
        out_specs=(VMEM,) * 4,
        scratch_shapes=[
            pltpu.VMEM(weights.shape, F32),
            pltpu.VMEM(feat.shape, BF16),
            pltpu.VMEM((depth, hidden), BF16),
            pltpu.VMEM((hidden, depth), BF16),
            pltpu.VMEM((cells, hidden), BF16),
            pltpu.VMEM((2 * REACH + 1, rows, depth), F32),
            pltpu.SemaphoreType.DMA((2, hidden // part)),
            pltpu.SemaphoreType.DMA((cells // tile + 2,)),
        ],
        compiler_params=pltpu.CompilerParams(vmem_limit_bytes=24 << 20),
        cost_estimate=pl.CostEstimate(
            flops=4 * cells * depth * hidden, bytes_accessed=4 * (cells + hidden) * depth, transcendentals=cells * hidden
        ),
        name="encode",
    )(owner, listed, *in_hbm(weights, feat, grid, first, second))


def outgoing_kernel(base_ref, arrived_ref, out_ref):
    rows = arrived_ref.shape[0] - EXTRA
    out_ref[:rows, :] = base_ref[:rows, :]
    out_ref[rows:, :] = (base_ref[rows:, :].astype(F32) + arrived_ref[...].astype(F32)).astype(BF16)


def outgoing_sums(base, arrived):
    return pl.pallas_call(
        outgoing_kernel, out_shape=kept(base.shape), in_specs=[VMEM] * 2, out_specs=VMEM, name="outgoing_sums"
    )(base, arrived)


def share_kernel(loc_ref, arrived_ref, share_ref, msg_ref):
    rows = loc_ref.shape[0] // 2
    share_ref[...] = loc_ref[...] + arrived_ref[:2 * rows, :].astype(F32)
    msg_ref[:rows, :] = share_ref[rows:, :].astype(BF16)
    msg_ref[rows:, :] = share_ref[:rows, :].astype(BF16)


def chip_share(local, arrived):
    return pl.pallas_call(
        share_kernel,
        out_shape=(kept(local.shape, F32), kept(local.shape)),
        in_specs=[VMEM] * 2,
        out_specs=(VMEM,) * 2,
        name="chip_share",
    )(local, arrived)


def state_kernel(share_ref, other_ref, own_ref, pair_ref):
    rows = own_ref.shape[0]
    own_ref[...] = share_ref[rows:, :] + other_ref[rows:, :].astype(F32)
    pair_ref[:rows, :] = (share_ref[:rows, :] + other_ref[:rows, :].astype(F32)).astype(BF16)
    pair_ref[rows:, :] = own_ref[...].astype(BF16)


def chip_states(share, other):
    rows, depth = share.shape[0] // 2, share.shape[1]
    return pl.pallas_call(
        state_kernel,
        out_shape=(kept((rows, depth), F32), kept(share.shape)),
        in_specs=[VMEM] * 2,
        out_specs=(VMEM,) * 2,
        name="chip_states",
    )(share, other)


def normal(block, gain):
    state = block.astype(F32)
    scale = lax.rsqrt(jnp.mean(state * state, axis=-1, keepdims=True) + 1e-6)
    return (state * scale * gain).astype(BF16)


def project_kernel(state_ref, gain_ref, w_qkv, out_ref):
    rows = normal(state_ref[...], gain_ref[...])
    out_ref[...] = jnp.dot(rows, w_qkv[...], preferred_element_type=F32).astype(BF16)


def project(states, gain, w_qkv):
    rows, depth = states.shape
    return pl.pallas_call(
        project_kernel,
        out_shape=kept((rows, w_qkv.shape[1])),
        in_specs=[VMEM] * 3,
        out_specs=VMEM,
        compiler_params=pltpu.CompilerParams(vmem_limit_bytes=16 << 20),
        cost_estimate=pl.CostEstimate(
            flops=2 * rows * depth * w_qkv.shape[1], bytes_accessed=2 * rows * depth, transcendentals=0
        ),
        name="project",
    )(states, gain, w_qkv)


def attend_kernel(
    listed, code_ref, own_ref, qkv_pair, near_ref, qkv_near, far_ref, behind_ref, gain_ref, w_qkv, w_out,
    ring_ref,
    kv_far, kv_behind, mixed,
):
    rows, depth = own_ref.shape
    heads = depth // HD
    span = 2 * REACH + 1
    mine, count = lax.axis_index(AXES), lax.axis_size(AXES)
    outward = outward_of()
    gain = gain_ref[...]
    kv_far[...] = jnp.dot(normal(far_ref[...], gain), w_qkv[:, depth:], preferred_element_type=F32).astype(BF16)
    kv_behind[...] = jnp.dot(normal(behind_ref[...], gain), w_qkv[:, depth:], preferred_element_type=F32).astype(BF16)
    window = [
        (kv_behind, 0, 0), (qkv_pair, 0, depth), (qkv_pair, 1, depth), (qkv_near, 1, depth),
        (qkv_near, 0, depth), (kv_far, 1, 0), (kv_far, 0, 0),
    ]
    absent = sum(-offset_of(listed[0, n], mine, count) for n in range(listed.shape[1]))
    dropped = [
        (outward * absent + REACH).astype(F32),
        outward.astype(F32) * code_ref[0:1, 0:1].astype(F32) + REACH,
        outward.astype(F32) * code_ref[0:1, 1:2].astype(F32) + REACH,
    ]
    lane_block = (lax.broadcasted_iota(jnp.int32, (rows, span * rows), 1) // rows).astype(F32)
    queries = [(qkv_pair, 1), (qkv_near, 1), (qkv_near, 0)]
    for p, (q_ref, q_block) in enumerate(queries):
        keep = lane_block != dropped[p]
        for h in range(heads):
            cols = slice(h * HD, (h + 1) * HD)
            query = q_ref[q_block * rows:(q_block + 1) * rows, cols]
            parts = []
            for ref, block, start in window[p:p + span]:
                key = ref[block * rows:(block + 1) * rows, start + h * HD:start + (h + 1) * HD]
                parts.append(lax.dot_general(
                    query, key, (((1,), (1,)), ((), ())), preferred_element_type=F32
                ))
            scores = jnp.concatenate(parts, axis=1) * (HD ** -0.5)
            scores = jnp.where(keep, scores, -jnp.inf)
            grown = jnp.exp(scores - jnp.max(scores, axis=-1, keepdims=True))
            share = 1.0 / jnp.sum(grown, axis=-1, keepdims=True)
            grown = grown.astype(BF16)
            taken = None
            for n, (ref, block, start) in enumerate(window[p:p + span]):
                left = start + depth + h * HD
                value = ref[block * rows:(block + 1) * rows, left:left + HD]
                term = jnp.dot(grown[:, n * rows:(n + 1) * rows], value, preferred_element_type=F32)
                taken = term if taken is None else taken + term
            mixed[p * rows:(p + 1) * rows, cols] = (taken * share).astype(BF16)
    added = jnp.dot(mixed[...], w_out[...], preferred_element_type=F32)
    ring_ref[:rows, :] = (own_ref[...] + added[:rows, :]).astype(BF16)
    ring_ref[rows:2 * rows, :] = (near_ref[rows:, :].astype(F32) + added[rows:2 * rows, :]).astype(BF16)
    ring_ref[2 * rows:, :] = (near_ref[:rows, :].astype(F32) + added[2 * rows:, :]).astype(BF16)


def attend(listed, codes, own, qkv_pair, near, qkv_near, far, behind, gain, w_qkv, w_out):
    rows, depth = own.shape
    return pl.pallas_call(
        attend_kernel,
        out_shape=kept((3 * rows, depth)),
        in_specs=[SMEM] + [VMEM] * 10,
        out_specs=VMEM,
        scratch_shapes=[
            pltpu.VMEM((2 * rows, 2 * depth), BF16),
            pltpu.VMEM((rows, 2 * depth), BF16),
            pltpu.VMEM((3 * rows, depth), BF16),
        ],
        compiler_params=pltpu.CompilerParams(vmem_limit_bytes=16 << 20),
        name="attend",
    )(listed, codes, own, qkv_pair, near, qkv_near, far, behind, gain, w_qkv, w_out)


def decode_kernel(
    owner, weight_ref, ring_ref, back_ref, enc_ref, first, second,
    out_hbm, mesh_hbm,
    x_ref, act, mesh, io_sems,
):
    rows = back_ref.shape[0] // 2
    tile, part = tiles_of(x_ref.shape[0], first.shape[1])
    tiles = x_ref.shape[0] // tile
    stores = [pltpu.make_async_copy(ring_ref.at[pl.ds(0, rows)], mesh_hbm, io_sems.at[tiles])]
    stores[0].start()
    mine, count = lax.axis_index(AXES), lax.axis_size(AXES)
    outward = outward_of()
    mesh[0] = back_ref[rows:, :]
    mesh[1] = back_ref[:rows, :]
    for n in range(3):
        mesh[2 + n] = ring_ref[n * rows:(n + 1) * rows, :]
    columns = jnp.transpose(weight_ref[...])

    def arrive(r):
        for b in range(r * tile // rows, (r + 1) * tile // rows):
            cut = slice(b * rows, (b + 1) * rows)
            slot = outward * offset_of(owner[b], mine, count) + REACH
            read = mesh[slot].astype(F32)
            x_ref[cut, :] = (enc_ref[cut, :].astype(F32) + columns[:, b:b + 1] * read).astype(BF16)

    hidden_layer(x_ref, first, act, tile, part, arrive, lambda j: None)
    for r in range(tiles):
        cut = slice(r * tile, (r + 1) * tile)
        out = jnp.dot(act[cut, :], second[...], preferred_element_type=F32)
        x_ref[cut, :] = (x_ref[cut, :].astype(F32) + out).astype(BF16)
        copy = pltpu.make_async_copy(x_ref.at[pl.ds(r * tile, tile)], out_hbm.at[pl.ds(r * tile, tile)], io_sems.at[r])
        copy.start()
        stores.append(copy)
    for copy in stores:
        copy.wait()


def decode(owner, weights, ring, back, encoded, first, second):
    cells, depth = encoded.shape
    hidden = first.shape[1]
    rows = back.shape[0] // 2
    tile, part = tiles_of(cells, hidden)
    return pl.pallas_call(
        decode_kernel,
        out_shape=(jax.ShapeDtypeStruct((cells, depth), BF16), jax.ShapeDtypeStruct((rows, depth), BF16)),
        in_specs=[SMEM] + [VMEM] * 6,
        out_specs=(ANY, ANY),
        scratch_shapes=[
            pltpu.VMEM((cells, depth), BF16),
            pltpu.VMEM((cells, hidden), BF16),
            pltpu.VMEM((2 * REACH + 1, rows, depth), BF16),
            pltpu.SemaphoreType.DMA((cells // tile + 1,)),
        ],
        compiler_params=pltpu.CompilerParams(vmem_limit_bytes=24 << 20),
        cost_estimate=pl.CostEstimate(
            flops=4 * cells * depth * hidden, bytes_accessed=4 * (cells + hidden) * depth, transcendentals=cells * hidden
        ),
        name="decode",
    )(owner, weights, ring, back, encoded, first, second)


def on_device(
    grid, g2m_owner, g2m_weight, m2g_owner, m2g_weight, mesh_feat, neighbours,
    enc_w1, enc_w2, attn_gain, w_qkv, w_out, dec_w1, dec_w2,
):
    rows = mesh_feat.shape[0]
    nblocks = g2m_owner.shape[0]
    encoded, message, base, local = encode(
        g2m_owner, neighbours, g2m_weight.reshape(nblocks, rows), mesh_feat, grid, enc_w1, enc_w2
    )
    sums = from_outward(outgoing_sums(base, swapped(message)), 1)
    share, message = chip_share(local, sums)
    own, pair = chip_states(share, swapped(message))
    near = from_outward(pair, 1)
    far = from_outward(pair, 2)
    behind = swapped(near[rows:])
    qkv_pair = project(pair, attn_gain, w_qkv[0])
    qkv_near = project(near, attn_gain, w_qkv[0])
    ring = attend(
        neighbours, sums[2 * rows:], own, qkv_pair, near, qkv_near, far, behind, attn_gain, w_qkv[0], w_out[0]
    )
    back = swapped(ring[:2 * rows])
    return decode(m2g_owner, m2g_weight.reshape(nblocks, rows), ring, back, encoded, dec_w1, dec_w2)


def solution(mesh):
    split = P(AXES, None)
    flat = P(AXES)
    in_specs = (split, flat, flat, flat, flat, split, split) + (P(),) * 7
    return jax.shard_map(
        on_device, mesh=mesh, in_specs=in_specs, out_specs=(split, split), check_vma=False
    )
```

```python
import functools

import jax
import jax.numpy as jnp
from jax import lax
from jax.experimental import pallas as pl
from jax.experimental.pallas import tpu as pltpu
from jax.sharding import PartitionSpec as P

HD = 128
REACH = 2
EXTRA = 16
AXES = ("tile", "sub")
BF16 = jnp.bfloat16
F32 = jnp.float32
VMEM = pl.BlockSpec(memory_space=pltpu.VMEM)
SMEM = pl.BlockSpec(memory_space=pltpu.SMEM)
ANY = pl.BlockSpec(memory_space=pl.ANY)


def swapped(block):
    count = lax.axis_size(AXES)
    return lax.ppermute(block, AXES, [(i, i ^ 1) for i in range(count)])


def from_outward(block, chips):
    count = lax.axis_size(AXES)
    route = []
    for i in range(count):
        step = 2 * chips - 1
        route.append((i, (i + step if i % 2 else i - step) % count))
    return lax.ppermute(block, AXES, route)


def tiles_of(rows, columns):
    return min(rows, 256), min(columns, 512)


def outward_of():
    return 2 * lax.axis_index("sub") - 1


def offset_of(owner, mine, count):
    return lax.rem(owner - mine + REACH + count, count) - REACH


def kept(shape, dtype=BF16):
    return pltpu.VMEM(shape, dtype)


def in_hbm(*arrays):
    return [pltpu.with_memory_space_constraint(a, pltpu.HBM) for a in arrays]


def hidden_layer(x_ref, first, act, tile, part, arrive, before):
    for j in range(first.shape[1] // part):
        before(j)
        cols = slice(j * part, (j + 1) * part)
        for r in range(x_ref.shape[0] // tile):
            if j == 0:
                arrive(r)
            cut = slice(r * tile, (r + 1) * tile)
            half = jnp.dot(x_ref[cut, :] * BF16(0.5), first[:, cols], preferred_element_type=F32)
            act[cut, cols] = (half * jnp.tanh(half) + half).astype(BF16)


def encode_kernel(
    owner, listed, weight_hbm, feat_hbm, x_hbm, first_hbm, second_hbm,
    enc_ref, msg_ref, base_ref, loc_ref,
    weight_ref, feat_ref, first, second, act, total, sems, io_sems,
):
    rows, depth = feat_ref.shape
    tile, part = tiles_of(enc_ref.shape[0], first.shape[1])
    tiles, parts = enc_ref.shape[0] // tile, first.shape[1] // part
    loads = [
        pltpu.make_async_copy(x_hbm.at[pl.ds(r * tile, tile)], enc_ref.at[pl.ds(r * tile, tile)], io_sems.at[r])
        for r in range(tiles)
    ]
    ones, twos = [], []
    for j in range(parts):
        cut = pl.ds(j * part, part)
        ones.append(pltpu.make_async_copy(first_hbm.at[:, cut], first.at[:, cut], sems.at[0, j]))
        twos.append(pltpu.make_async_copy(second_hbm.at[cut], second.at[cut], sems.at[1, j]))
    small = [
        pltpu.make_async_copy(weight_hbm, weight_ref, io_sems.at[tiles]),
        pltpu.make_async_copy(feat_hbm, feat_ref, io_sems.at[tiles + 1]),
    ]
    for copy in [loads[0], ones[0]] + loads[1:] + ones[1:] + twos + small:
        copy.start()
    mine, count = lax.axis_index(AXES), lax.axis_size(AXES)
    outward = outward_of()
    total[...] = jnp.zeros_like(total)
    hidden_layer(
        enc_ref, first, act, tile, part, lambda r: loads[r].wait(), lambda j: ones[j].wait()
    )
    for copy in twos + small:
        copy.wait()
    columns = jnp.transpose(weight_ref[...])
    for r in range(tiles):
        cut = slice(r * tile, (r + 1) * tile)
        out = jnp.dot(act[cut, :], second[...], preferred_element_type=F32)
        enc_ref[cut, :] = (enc_ref[cut, :].astype(F32) + out).astype(BF16)
        for b in range(r * tile // rows, (r + 1) * tile // rows):
            slot = outward * offset_of(owner[b], mine, count) + REACH
            block = enc_ref[b * rows:(b + 1) * rows, :].astype(F32)
            total[slot] += columns[:, b:b + 1] * block
    absent = sum(-offset_of(listed[0, n], mine, count) for n in range(listed.shape[1])).astype(F32)
    spot = lax.broadcasted_iota(jnp.int32, (EXTRA, depth), 1)
    msg_ref[:rows, :] = total[0].astype(BF16)
    msg_ref[rows:, :] = jnp.where(spot == 1, absent, 0.0).astype(BF16)
    base_ref[:rows, :] = total[4].astype(BF16)
    base_ref[rows:2 * rows, :] = total[3].astype(BF16)
    base_ref[2 * rows:, :] = jnp.where(spot == 0, absent, 0.0).astype(BF16)
    loc_ref[:rows, :] = total[1]
    loc_ref[rows:, :] = total[2] + feat_ref[...].astype(F32)


def encode(owner, listed, weights, feat, grid, first, second):
    cells, depth = grid.shape
    hidden = first.shape[1]
    rows = feat.shape[0]
    tile, part = tiles_of(cells, hidden)
    return pl.pallas_call(
        encode_kernel,
        out_shape=(
            kept((cells, depth)),
            kept((rows + EXTRA, depth)),
            kept((2 * rows + EXTRA, depth)),
            kept((2 * rows, depth), F32),
        ),
        in_specs=[SMEM, SMEM] + [ANY] * 5,
        out_specs=(VMEM,) * 4,
        scratch_shapes=[
            pltpu.VMEM(weights.shape, F32),
            pltpu.VMEM(feat.shape, BF16),
            pltpu.VMEM((depth, hidden), BF16),
            pltpu.VMEM((hidden, depth), BF16),
            pltpu.VMEM((cells, hidden), BF16),
            pltpu.VMEM((2 * REACH + 1, rows, depth), F32),
            pltpu.SemaphoreType.DMA((2, hidden // part)),
            pltpu.SemaphoreType.DMA((cells // tile + 2,)),
        ],
        compiler_params=pltpu.CompilerParams(vmem_limit_bytes=24 << 20),
        cost_estimate=pl.CostEstimate(
            flops=4 * cells * depth * hidden, bytes_accessed=4 * (cells + hidden) * depth, transcendentals=cells * hidden
        ),
        name="encode",
    )(owner, listed, *in_hbm(weights, feat, grid, first, second))


def outgoing_kernel(base_ref, arrived_ref, out_ref):
    rows = arrived_ref.shape[0] - EXTRA
    out_ref[:rows, :] = base_ref[:rows, :]
    out_ref[rows:, :] = (base_ref[rows:, :].astype(F32) + arrived_ref[...].astype(F32)).astype(BF16)


def outgoing_sums(base, arrived):
    return pl.pallas_call(
        outgoing_kernel, out_shape=kept(base.shape), in_specs=[VMEM] * 2, out_specs=VMEM,
        compiler_params=pltpu.CompilerParams(vmem_limit_bytes=4 << 20), name="outgoing_sums"
    )(base, arrived)


def share_kernel(loc_ref, arrived_ref, share_ref, msg_ref):
    rows = loc_ref.shape[0] // 2
    share_ref[...] = loc_ref[...] + arrived_ref[:2 * rows, :].astype(F32)
    msg_ref[:rows, :] = share_ref[rows:, :].astype(BF16)
    msg_ref[rows:, :] = share_ref[:rows, :].astype(BF16)


def chip_share(local, arrived):
    return pl.pallas_call(
        share_kernel,
        out_shape=(kept(local.shape, F32), kept(local.shape)),
        in_specs=[VMEM] * 2,
        out_specs=(VMEM,) * 2,
        compiler_params=pltpu.CompilerParams(vmem_limit_bytes=4 << 20),
        name="chip_share",
    )(local, arrived)


def state_kernel(share_ref, other_ref, own_ref, pair_ref):
    rows = own_ref.shape[0]
    own_ref[...] = share_ref[rows:, :] + other_ref[rows:, :].astype(F32)
    pair_ref[:rows, :] = (share_ref[:rows, :] + other_ref[:rows, :].astype(F32)).astype(BF16)
    pair_ref[rows:, :] = own_ref[...].astype(BF16)


def chip_states(share, other):
    rows, depth = share.shape[0] // 2, share.shape[1]
    return pl.pallas_call(
        state_kernel,
        out_shape=(kept((rows, depth), F32), kept(share.shape)),
        in_specs=[VMEM] * 2,
        out_specs=(VMEM,) * 2,
        compiler_params=pltpu.CompilerParams(vmem_limit_bytes=4 << 20),
        name="chip_states",
    )(share, other)


def normal(block, gain):
    state = block.astype(F32)
    scale = lax.rsqrt(jnp.mean(state * state, axis=-1, keepdims=True) + 1e-6)
    return (state * scale * gain).astype(BF16)


def project_kernel(state_ref, gain_ref, w_qkv, out_ref):
    rows = normal(state_ref[...], gain_ref[...])
    out_ref[...] = jnp.dot(rows, w_qkv[...], preferred_element_type=F32).astype(BF16)


def project(states, gain, w_qkv):
    rows, depth = states.shape
    return pl.pallas_call(
        project_kernel,
        out_shape=kept((rows, w_qkv.shape[1])),
        in_specs=[VMEM] * 3,
        out_specs=VMEM,
        compiler_params=pltpu.CompilerParams(vmem_limit_bytes=16 << 20),
        cost_estimate=pl.CostEstimate(
            flops=2 * rows * depth * w_qkv.shape[1], bytes_accessed=2 * rows * depth, transcendentals=0
        ),
        name="project",
    )(states, gain, w_qkv)


def attend_kernel(
    listed, code_ref, own_ref, qkv_pair, near_ref, qkv_near, far_ref, behind_ref, gain_ref, w_qkv, w_out,
    ring_ref,
    kv_far, kv_behind, mixed,
):
    rows, depth = own_ref.shape
    heads = depth // HD
    span = 2 * REACH + 1
    mine, count = lax.axis_index(AXES), lax.axis_size(AXES)
    outward = outward_of()
    gain = gain_ref[...]
    kv_far[...] = jnp.dot(normal(far_ref[...], gain), w_qkv[:, depth:], preferred_element_type=F32).astype(BF16)
    kv_behind[...] = jnp.dot(normal(behind_ref[...], gain), w_qkv[:, depth:], preferred_element_type=F32).astype(BF16)
    window = [
        (kv_behind, 0, 0), (qkv_pair, 0, depth), (qkv_pair, 1, depth), (qkv_near, 1, depth),
        (qkv_near, 0, depth), (kv_far, 1, 0), (kv_far, 0, 0),
    ]
    absent = sum(-offset_of(listed[0, n], mine, count) for n in range(listed.shape[1]))
    dropped = [
        (outward * absent + REACH).astype(F32),
        outward.astype(F32) * code_ref[0:1, 0:1].astype(F32) + REACH,
        outward.astype(F32) * code_ref[0:1, 1:2].astype(F32) + REACH,
    ]
    lane_block = (lax.broadcasted_iota(jnp.int32, (rows, span * rows), 1) // rows).astype(F32)
    queries = [(qkv_pair, 1), (qkv_near, 1), (qkv_near, 0)]
    for p, (q_ref, q_block) in enumerate(queries):
        keep = lane_block != dropped[p]
        for h in range(heads):
            cols = slice(h * HD, (h + 1) * HD)
            query = q_ref[q_block * rows:(q_block + 1) * rows, cols]
            parts = []
            for ref, block, start in window[p:p + span]:
                key = ref[block * rows:(block + 1) * rows, start + h * HD:start + (h + 1) * HD]
                parts.append(lax.dot_general(
                    query, key, (((1,), (1,)), ((), ())), preferred_element_type=F32
                ))
            scores = jnp.concatenate(parts, axis=1) * (HD ** -0.5)
            scores = jnp.where(keep, scores, -jnp.inf)
            grown = jnp.exp(scores - jnp.max(scores, axis=-1, keepdims=True))
            share = 1.0 / jnp.sum(grown, axis=-1, keepdims=True)
            grown = grown.astype(BF16)
            taken = None
            for n, (ref, block, start) in enumerate(window[p:p + span]):
                left = start + depth + h * HD
                value = ref[block * rows:(block + 1) * rows, left:left + HD]
                term = jnp.dot(grown[:, n * rows:(n + 1) * rows], value, preferred_element_type=F32)
                taken = term if taken is None else taken + term
            mixed[p * rows:(p + 1) * rows, cols] = (taken * share).astype(BF16)
    added = jnp.dot(mixed[...], w_out[...], preferred_element_type=F32)
    ring_ref[:rows, :] = (own_ref[...] + added[:rows, :]).astype(BF16)
    ring_ref[rows:2 * rows, :] = (near_ref[rows:, :].astype(F32) + added[rows:2 * rows, :]).astype(BF16)
    ring_ref[2 * rows:, :] = (near_ref[:rows, :].astype(F32) + added[2 * rows:, :]).astype(BF16)


def attend(listed, codes, own, qkv_pair, near, qkv_near, far, behind, gain, w_qkv, w_out):
    rows, depth = own.shape
    return pl.pallas_call(
        attend_kernel,
        out_shape=kept((3 * rows, depth)),
        in_specs=[SMEM] + [VMEM] * 10,
        out_specs=VMEM,
        scratch_shapes=[
            pltpu.VMEM((2 * rows, 2 * depth), BF16),
            pltpu.VMEM((rows, 2 * depth), BF16),
            pltpu.VMEM((3 * rows, depth), BF16),
        ],
        compiler_params=pltpu.CompilerParams(vmem_limit_bytes=16 << 20),
        name="attend",
    )(listed, codes, own, qkv_pair, near, qkv_near, far, behind, gain, w_qkv, w_out)


def decode_kernel(
    owner, weight_ref, ring_ref, back_ref, enc_ref, first, second,
    out_hbm, mesh_hbm,
    x_ref, act, mesh, io_sems,
):
    rows = back_ref.shape[0] // 2
    tile, part = tiles_of(x_ref.shape[0], first.shape[1])
    tiles = x_ref.shape[0] // tile
    stores = [pltpu.make_async_copy(ring_ref.at[pl.ds(0, rows)], mesh_hbm, io_sems.at[tiles])]
    stores[0].start()
    mine, count = lax.axis_index(AXES), lax.axis_size(AXES)
    outward = outward_of()
    mesh[0] = back_ref[rows:, :]
    mesh[1] = back_ref[:rows, :]
    for n in range(3):
        mesh[2 + n] = ring_ref[n * rows:(n + 1) * rows, :]
    columns = jnp.transpose(weight_ref[...])

    def arrive(r):
        for b in range(r * tile // rows, (r + 1) * tile // rows):
            cut = slice(b * rows, (b + 1) * rows)
            slot = outward * offset_of(owner[b], mine, count) + REACH
            read = mesh[slot].astype(F32)
            x_ref[cut, :] = (enc_ref[cut, :].astype(F32) + columns[:, b:b + 1] * read).astype(BF16)

    hidden_layer(x_ref, first, act, tile, part, arrive, lambda j: None)
    for r in range(tiles):
        cut = slice(r * tile, (r + 1) * tile)
        out = jnp.dot(act[cut, :], second[...], preferred_element_type=F32)
        x_ref[cut, :] = (x_ref[cut, :].astype(F32) + out).astype(BF16)
        copy = pltpu.make_async_copy(x_ref.at[pl.ds(r * tile, tile)], out_hbm.at[pl.ds(r * tile, tile)], io_sems.at[r])
        copy.start()
        stores.append(copy)
    for copy in stores:
        copy.wait()


def decode(owner, weights, ring, back, encoded, first, second):
    cells, depth = encoded.shape
    hidden = first.shape[1]
    rows = back.shape[0] // 2
    tile, part = tiles_of(cells, hidden)
    return pl.pallas_call(
        decode_kernel,
        out_shape=(jax.ShapeDtypeStruct((cells, depth), BF16), jax.ShapeDtypeStruct((rows, depth), BF16)),
        in_specs=[SMEM] + [VMEM] * 6,
        out_specs=(ANY, ANY),
        scratch_shapes=[
            pltpu.VMEM((cells, depth), BF16),
            pltpu.VMEM((cells, hidden), BF16),
            pltpu.VMEM((2 * REACH + 1, rows, depth), BF16),
            pltpu.SemaphoreType.DMA((cells // tile + 1,)),
        ],
        compiler_params=pltpu.CompilerParams(vmem_limit_bytes=24 << 20),
        cost_estimate=pl.CostEstimate(
            flops=4 * cells * depth * hidden, bytes_accessed=4 * (cells + hidden) * depth, transcendentals=cells * hidden
        ),
        name="decode",
    )(owner, weights, ring, back, encoded, first, second)


def on_device(
    grid, g2m_owner, g2m_weight, m2g_owner, m2g_weight, mesh_feat, neighbours,
    enc_w1, enc_w2, attn_gain, w_qkv, w_out, dec_w1, dec_w2,
):
    rows = mesh_feat.shape[0]
    nblocks = g2m_owner.shape[0]
    encoded, message, base, local = encode(
        g2m_owner, neighbours, g2m_weight.reshape(nblocks, rows), mesh_feat, grid, enc_w1, enc_w2
    )
    sums = from_outward(outgoing_sums(base, swapped(message)), 1)
    share, message = chip_share(local, sums)
    own, pair = chip_states(share, swapped(message))
    near = from_outward(pair, 1)
    far = from_outward(pair, 2)
    behind = swapped(near[rows:])
    qkv_pair = project(pair, attn_gain, w_qkv[0])
    qkv_near = project(near, attn_gain, w_qkv[0])
    ring = attend(
        neighbours, sums[2 * rows:], own, qkv_pair, near, qkv_near, far, behind, attn_gain, w_qkv[0], w_out[0]
    )
    back = swapped(ring[:2 * rows])
    return decode(m2g_owner, m2g_weight.reshape(nblocks, rows), ring, back, encoded, dec_w1, dec_w2)


def solution(mesh):
    split = P(AXES, None)
    flat = P(AXES)
    in_specs = (split, flat, flat, flat, flat, split, split) + (P(),) * 7
    return jax.shard_map(
        on_device, mesh=mesh, in_specs=in_specs, out_specs=(split, split), check_vma=False
    )
```

```python
import functools

import jax
import jax.numpy as jnp
from jax import lax
from jax.experimental import pallas as pl
from jax.experimental.pallas import tpu as pltpu
from jax.sharding import PartitionSpec as P

HD = 128
REACH = 2
EXTRA = 16
AXES = ("tile", "sub")
BF16 = jnp.bfloat16
F32 = jnp.float32
VMEM = pl.BlockSpec(memory_space=pltpu.VMEM)
SMEM = pl.BlockSpec(memory_space=pltpu.SMEM)
ANY = pl.BlockSpec(memory_space=pl.ANY)


def swapped(block):
    count = lax.axis_size(AXES)
    return lax.ppermute(block, AXES, [(i, i ^ 1) for i in range(count)])


def from_outward(block, chips):
    count = lax.axis_size(AXES)
    route = []
    for i in range(count):
        step = 2 * chips - 1
        route.append((i, (i + step if i % 2 else i - step) % count))
    return lax.ppermute(block, AXES, route)


def tiles_of(rows, columns):
    return min(rows, 512), min(columns, 1024)


def outward_of():
    return 2 * lax.axis_index("sub") - 1


def offset_of(owner, mine, count):
    return lax.rem(owner - mine + REACH + count, count) - REACH


def kept(shape, dtype=BF16):
    return pltpu.VMEM(shape, dtype)


def in_hbm(*arrays):
    return [pltpu.with_memory_space_constraint(a, pltpu.HBM) for a in arrays]


def hidden_layer(x_ref, first, act, tile, part, arrive, before):
    for j in range(first.shape[1] // part):
        before(j)
        cols = slice(j * part, (j + 1) * part)
        for r in range(x_ref.shape[0] // tile):
            if j == 0:
                arrive(r)
            cut = slice(r * tile, (r + 1) * tile)
            half = jnp.dot(x_ref[cut, :] * BF16(0.5), first[:, cols], preferred_element_type=F32)
            act[cut, cols] = (half * jnp.tanh(half) + half).astype(BF16)


def encode_kernel(
    owner_hbm, listed_hbm, weight_hbm, feat_hbm, x_hbm, first_hbm, second_hbm,
    enc_ref, msg_ref, base_ref, loc_ref,
    owner, listed, weight_ref, feat_ref, first, second, act, total, sems, io_sems,
):
    rows, depth = feat_ref.shape
    tile, part = tiles_of(enc_ref.shape[0], first.shape[1])
    tiles, parts = enc_ref.shape[0] // tile, first.shape[1] // part
    loads = [
        pltpu.make_async_copy(x_hbm.at[pl.ds(r * tile, tile)], enc_ref.at[pl.ds(r * tile, tile)], io_sems.at[r])
        for r in range(tiles)
    ]
    ones, twos = [], []
    for j in range(parts):
        cut = pl.ds(j * part, part)
        ones.append(pltpu.make_async_copy(first_hbm.at[:, cut], first.at[:, cut], sems.at[0, j]))
        twos.append(pltpu.make_async_copy(second_hbm.at[cut], second.at[cut], sems.at[1, j]))
    small = [
        pltpu.make_async_copy(weight_hbm, weight_ref, io_sems.at[tiles]),
        pltpu.make_async_copy(feat_hbm, feat_ref, io_sems.at[tiles + 1]),
        pltpu.make_async_copy(owner_hbm, owner, io_sems.at[tiles + 2]),
        pltpu.make_async_copy(listed_hbm, listed, io_sems.at[tiles + 3]),
    ]
    for copy in loads + ones:
        copy.start()

    def arrive(r):
        if r == 0:
            for copy in loads:
                copy.wait()
            for copy in twos + small:
                copy.start()

    mine, count = lax.axis_index(AXES), lax.axis_size(AXES)
    outward = outward_of()
    total[...] = jnp.zeros_like(total)
    hidden_layer(enc_ref, first, act, tile, part, arrive, lambda j: ones[j].wait())
    for copy in twos + small:
        copy.wait()
    columns = jnp.transpose(weight_ref[...])
    for r in range(tiles):
        cut = slice(r * tile, (r + 1) * tile)
        out = jnp.dot(act[cut, :], second[...], preferred_element_type=F32)
        enc_ref[cut, :] = (enc_ref[cut, :].astype(F32) + out).astype(BF16)
        for b in range(r * tile // rows, (r + 1) * tile // rows):
            slot = outward * offset_of(owner[b], mine, count) + REACH
            block = enc_ref[b * rows:(b + 1) * rows, :].astype(F32)
            total[slot] += columns[:, b:b + 1] * block
    absent = sum(-offset_of(listed[0, n], mine, count) for n in range(listed.shape[1])).astype(F32)
    spot = lax.broadcasted_iota(jnp.int32, (EXTRA, depth), 1)
    msg_ref[:rows, :] = total[0].astype(BF16)
    msg_ref[rows:, :] = jnp.where(spot == 1, absent, 0.0).astype(BF16)
    base_ref[:rows, :] = total[4].astype(BF16)
    base_ref[rows:2 * rows, :] = total[3].astype(BF16)
    base_ref[2 * rows:, :] = jnp.where(spot == 0, absent, 0.0).astype(BF16)
    loc_ref[:rows, :] = total[1]
    loc_ref[rows:, :] = total[2] + feat_ref[...].astype(F32)


def encode(owner, listed, weights, feat, grid, first, second):
    cells, depth = grid.shape
    hidden = first.shape[1]
    rows = feat.shape[0]
    tile, part = tiles_of(cells, hidden)
    return pl.pallas_call(
        encode_kernel,
        out_shape=(
            kept((cells, depth)),
            kept((rows + EXTRA, depth)),
            kept((2 * rows + EXTRA, depth)),
            kept((2 * rows, depth), F32),
        ),
        in_specs=[ANY] * 7,
        out_specs=(VMEM,) * 4,
        scratch_shapes=[
            pltpu.SMEM(owner.shape, jnp.int32),
            pltpu.SMEM(listed.shape, jnp.int32),
            pltpu.VMEM(weights.shape, F32),
            pltpu.VMEM(feat.shape, BF16),
            pltpu.VMEM((depth, hidden), BF16),
            pltpu.VMEM((hidden, depth), BF16),
            pltpu.VMEM((cells, hidden), BF16),
            pltpu.VMEM((2 * REACH + 1, rows, depth), F32),
            pltpu.SemaphoreType.DMA((2, hidden // part)),
            pltpu.SemaphoreType.DMA((cells // tile + 4,)),
        ],
        compiler_params=pltpu.CompilerParams(vmem_limit_bytes=24 << 20),
        cost_estimate=pl.CostEstimate(
            flops=4 * cells * depth * hidden, bytes_accessed=4 * (cells + hidden) * depth, transcendentals=cells * hidden
        ),
        name="encode",
    )(*in_hbm(owner, listed, weights, feat, grid, first, second))


def outgoing_kernel(base_ref, arrived_ref, out_ref):
    rows = arrived_ref.shape[0] - EXTRA
    out_ref[:rows, :] = base_ref[:rows, :]
    out_ref[rows:, :] = (base_ref[rows:, :].astype(F32) + arrived_ref[...].astype(F32)).astype(BF16)


def outgoing_sums(base, arrived):
    return pl.pallas_call(
        outgoing_kernel, out_shape=kept(base.shape), in_specs=[VMEM] * 2, out_specs=VMEM,
        compiler_params=pltpu.CompilerParams(vmem_limit_bytes=4 << 20), name="outgoing_sums"
    )(base, arrived)


def share_kernel(loc_ref, arrived_ref, after, share_ref, msg_ref):
    del after
    rows = loc_ref.shape[0] // 2
    share_ref[...] = loc_ref[...] + arrived_ref[:2 * rows, :].astype(F32)
    msg_ref[:rows, :] = share_ref[rows:, :].astype(BF16)
    msg_ref[rows:, :] = share_ref[:rows, :].astype(BF16)


def chip_share(local, arrived, after):
    return pl.pallas_call(
        share_kernel,
        out_shape=(kept(local.shape, F32), kept(local.shape)),
        in_specs=[VMEM] * 2 + [ANY],
        out_specs=(VMEM,) * 2,
        compiler_params=pltpu.CompilerParams(vmem_limit_bytes=4 << 20),
        name="chip_share",
    )(local, arrived, after)


def state_kernel(share_ref, other_ref, own_ref, pair_ref, msg_ref):
    rows = own_ref.shape[0]
    own_ref[...] = share_ref[rows:, :] + other_ref[rows:, :].astype(F32)
    pair_ref[:rows, :] = (share_ref[:rows, :] + other_ref[:rows, :].astype(F32)).astype(BF16)
    pair_ref[rows:, :] = own_ref[...].astype(BF16)
    msg_ref[:rows, :] = pair_ref[rows:, :]
    msg_ref[rows:, :] = pair_ref[:rows, :]


def chip_states(share, other):
    rows, depth = share.shape[0] // 2, share.shape[1]
    return pl.pallas_call(
        state_kernel,
        out_shape=(kept((rows, depth), F32), kept(share.shape), kept(share.shape)),
        in_specs=[VMEM] * 2,
        out_specs=(VMEM,) * 3,
        compiler_params=pltpu.CompilerParams(vmem_limit_bytes=4 << 20),
        name="chip_states",
    )(share, other)


def normal(block, gain):
    state = block.astype(F32)
    scale = lax.rsqrt(jnp.mean(state * state, axis=-1, keepdims=True) + 1e-6)
    return (state * scale * gain).astype(BF16)


def project_kernel(pair_ref, near_ref, gain_ref, w_qkv, query_ref, kv_ref, normed):
    rows, depth = pair_ref.shape[0] // 2, pair_ref.shape[1]
    gain = gain_ref[...]
    normed[:2 * rows, :] = normal(pair_ref[...], gain)
    normed[2 * rows:, :] = normal(near_ref[...], gain)
    kv_ref[...] = jnp.dot(normed[...], w_qkv[:, depth:], preferred_element_type=F32).astype(BF16)
    query_ref[...] = jnp.dot(normed[rows:, :], w_qkv[:, :depth], preferred_element_type=F32).astype(BF16)


def project(pair, near, gain, w_qkv):
    rows, depth = pair.shape[0] // 2, pair.shape[1]
    return pl.pallas_call(
        project_kernel,
        out_shape=(kept((3 * rows, depth)), kept((4 * rows, 2 * depth))),
        in_specs=[VMEM] * 4,
        out_specs=(VMEM,) * 2,
        scratch_shapes=[pltpu.VMEM((4 * rows, depth), BF16)],
        compiler_params=pltpu.CompilerParams(vmem_limit_bytes=8 << 20),
        cost_estimate=pl.CostEstimate(
            flops=22 * rows * depth * depth, bytes_accessed=2 * rows * depth, transcendentals=0
        ),
        name="project",
    )(pair, near, gain, w_qkv)


def attention(query, window, keep):
    depth = query.shape[1]
    heads = []
    for h in range(depth // HD):
        cols = slice(h * HD, (h + 1) * HD)
        value_cols = slice(depth + h * HD, depth + (h + 1) * HD)
        scores = jnp.concatenate([
            lax.dot_general(
                query[:, cols], ref[first:first + size, cols], (((1,), (1,)), ((), ())), preferred_element_type=F32
            )
            for ref, first, size in window
        ], axis=1)
        scores = jnp.where(keep, scores, -jnp.inf) * (HD ** -0.5)
        grown = jnp.exp(scores - jnp.max(scores, axis=-1, keepdims=True))
        share = 1.0 / jnp.sum(grown, axis=-1, keepdims=True)
        grown = grown.astype(BF16)
        start, taken = 0, None
        for ref, first, size in window:
            term = jnp.dot(
                grown[:, start:start + size], ref[first:first + size, value_cols], preferred_element_type=F32
            )
            taken = term if taken is None else taken + term
            start += size
        heads.append((taken * share).astype(BF16))
    return jnp.concatenate(heads, axis=1)


def kept_lanes(rows, absent):
    block = (lax.broadcasted_iota(jnp.int32, (rows, (2 * REACH + 1) * rows), 1) // rows).astype(F32)
    return block != outward_of().astype(F32) * absent.astype(F32) + REACH


def attend_own_kernel(base_ref, own_ref, query_ref, kv_ref, behind_ref, gain_ref, w_qkv, w_out, ring_ref, kv_behind):
    rows, depth = own_ref.shape
    kv_behind[...] = jnp.dot(
        normal(behind_ref[...], gain_ref[...]), w_qkv[:, depth:], preferred_element_type=F32
    ).astype(BF16)
    keep = kept_lanes(rows, base_ref[2 * rows:2 * rows + 1, 0:1])
    mixed = attention(query_ref[:rows, :], [(kv_behind, 0, rows), (kv_ref, 0, 4 * rows)], keep)
    ring_ref[...] = (own_ref[...] + jnp.dot(mixed, w_out[...], preferred_element_type=F32)).astype(BF16)


def attend_near_kernel(
    sums_ref, near_ref, query_ref, kv_ref, far_ref, gain_ref, w_qkv, w_out, after, ring_ref, kv_far, mixed
):
    del after
    rows, depth = near_ref.shape[0] // 2, near_ref.shape[1]
    kv_far[...] = jnp.dot(
        normal(far_ref[...], gain_ref[...]), w_qkv[:, depth:], preferred_element_type=F32
    ).astype(BF16)
    windows = [
        [(kv_ref, 0, 4 * rows), (kv_far, 0, rows)],
        [(kv_ref, rows, 3 * rows), (kv_far, 0, 2 * rows)],
    ]
    for n, window in enumerate(windows):
        keep = kept_lanes(rows, sums_ref[2 * rows:2 * rows + 1, n:n + 1])
        mixed[n * rows:(n + 1) * rows, :] = attention(query_ref[(n + 1) * rows:(n + 2) * rows, :], window, keep)
    added = jnp.dot(mixed[...], w_out[...], preferred_element_type=F32)
    ring_ref[...] = (near_ref[...].astype(F32) + added).astype(BF16)


def attend_own(base, own, query, kv, behind, gain, w_qkv, w_out):
    rows, depth = own.shape
    return pl.pallas_call(
        attend_own_kernel,
        out_shape=kept((rows, depth)),
        in_specs=[VMEM] * 8,
        out_specs=VMEM,
        scratch_shapes=[pltpu.VMEM((rows, 2 * depth), BF16)],
        compiler_params=pltpu.CompilerParams(vmem_limit_bytes=12 << 20),
        cost_estimate=pl.CostEstimate(
            flops=20 * rows * depth * depth, bytes_accessed=2 * rows * depth, transcendentals=0
        ),
        name="attend_own",
    )(base, own, query, kv, behind, gain, w_qkv, w_out)


def attend_near(sums, near, query, kv, far, gain, w_qkv, w_out, after):
    rows, depth = near.shape[0] // 2, near.shape[1]
    return pl.pallas_call(
        attend_near_kernel,
        out_shape=kept((2 * rows, depth)),
        in_specs=[VMEM] * 8 + [ANY],
        out_specs=VMEM,
        scratch_shapes=[pltpu.VMEM((2 * rows, 2 * depth), BF16), pltpu.VMEM((2 * rows, depth), BF16)],
        compiler_params=pltpu.CompilerParams(vmem_limit_bytes=12 << 20),
        cost_estimate=pl.CostEstimate(
            flops=40 * rows * depth * depth, bytes_accessed=2 * rows * depth, transcendentals=0
        ),
        name="attend_near",
    )(sums, near, query, kv, far, gain, w_qkv, w_out, after)


def halved(rows, first):
    return jnp.dot(rows * BF16(0.5), first, preferred_element_type=F32)


def grid_hidden_kernel(enc_ref, first, after, out_ref):
    del after
    tile, part = tiles_of(*out_ref.shape)
    for j in range(out_ref.shape[1] // part):
        cols = slice(j * part, (j + 1) * part)
        for r in range(out_ref.shape[0] // tile):
            cut = slice(r * tile, (r + 1) * tile)
            out_ref[cut, cols] = halved(enc_ref[cut, :], first[:, cols]).astype(BF16)


def grid_hidden(encoded, first, after):
    cells, depth = encoded.shape
    hidden = first.shape[1]
    return pl.pallas_call(
        grid_hidden_kernel,
        out_shape=kept((cells, hidden)),
        in_specs=[VMEM] * 2 + [ANY],
        out_specs=VMEM,
        compiler_params=pltpu.CompilerParams(vmem_limit_bytes=12 << 20),
        cost_estimate=pl.CostEstimate(
            flops=2 * cells * depth * hidden, bytes_accessed=2 * (cells + hidden) * depth, transcendentals=0
        ),
        name="grid_hidden",
    )(encoded, first, after)


def mesh_hidden_kernel(ring_own, ring_near, first, out_ref):
    rows = ring_own.shape[0]
    out_ref[REACH * rows:(REACH + 1) * rows, :] = halved(ring_own[...], first[...])
    out_ref[(REACH + 1) * rows:, :] = halved(ring_near[...], first[...])


def mesh_hidden(ring_own, ring_near, first):
    rows, depth = ring_own.shape
    return pl.pallas_call(
        mesh_hidden_kernel,
        out_shape=kept(((2 * REACH + 1) * rows, first.shape[1]), F32),
        in_specs=[VMEM] * 3,
        out_specs=VMEM,
        compiler_params=pltpu.CompilerParams(vmem_limit_bytes=12 << 20),
        cost_estimate=pl.CostEstimate(
            flops=6 * rows * depth * first.shape[1], bytes_accessed=2 * rows * depth, transcendentals=0
        ),
        name="mesh_hidden",
    )(ring_own, ring_near, first)


def decode_kernel(
    owner, weight_ref, ring_own, ring_near, back_own, back_near, grid_ref, mesh_in, enc_ref, first, second,
    out_hbm, mesh_hbm, mesh_ref,
    x_ref, act, ring, io_sems,
):
    del mesh_in
    rows = ring_own.shape[0]
    tile, part = tiles_of(x_ref.shape[0], first.shape[1])
    tile = min(tile, 256)
    tiles, parts = x_ref.shape[0] // tile, first.shape[1] // part
    stores = [pltpu.make_async_copy(ring_own, mesh_hbm, io_sems.at[tiles])]
    stores[0].start()
    mine, count = lax.axis_index(AXES), lax.axis_size(AXES)
    outward = outward_of()
    mesh_ref[:rows, :] = halved(back_near[...], first[...])
    mesh_ref[rows:2 * rows, :] = halved(back_own[...], first[...])
    ring[:rows, :] = back_near[...]
    ring[rows:2 * rows, :] = back_own[...]
    ring[2 * rows:3 * rows, :] = ring_own[...]
    ring[3 * rows:, :] = ring_near[...]
    columns = jnp.transpose(weight_ref[...])
    for r in range(tiles):
        cut = slice(r * tile, (r + 1) * tile)
        for b in range(r * tile // rows, (r + 1) * tile // rows):
            slot = outward * offset_of(owner[b], mine, count) + REACH
            lines = pl.ds(pl.multiple_of(slot * rows, rows), rows)
            block = slice(b * rows, (b + 1) * rows)
            weight = columns[:, b:b + 1]
            for j in range(parts):
                cols = slice(j * part, (j + 1) * part)
                half = grid_ref[block, cols].astype(F32) + weight * mesh_ref[lines, cols]
                act[block, cols] = (half * jnp.tanh(half) + half).astype(BF16)
            x_ref[block, :] = (enc_ref[block, :].astype(F32) + weight * ring[lines, :].astype(F32)).astype(BF16)
        out = jnp.dot(act[cut, :], second[...], preferred_element_type=F32)
        x_ref[cut, :] = (x_ref[cut, :].astype(F32) + out).astype(BF16)
        copy = pltpu.make_async_copy(x_ref.at[pl.ds(r * tile, tile)], out_hbm.at[pl.ds(r * tile, tile)], io_sems.at[r])
        copy.start()
        stores.append(copy)
    for copy in stores:
        copy.wait()


def decode(owner, weights, ring_own, ring_near, back_own, back_near, grid_part, mesh_part, encoded, first, second):
    cells, depth = encoded.shape
    hidden = first.shape[1]
    rows = ring_own.shape[0]
    return pl.pallas_call(
        decode_kernel,
        out_shape=(
            jax.ShapeDtypeStruct((cells, depth), BF16),
            jax.ShapeDtypeStruct((rows, depth), BF16),
            kept(mesh_part.shape, F32),
        ),
        in_specs=[SMEM] + [VMEM] * 10,
        out_specs=(ANY, ANY, VMEM),
        input_output_aliases={7: 2},
        scratch_shapes=[
            pltpu.VMEM((cells, depth), BF16),
            pltpu.VMEM((cells, hidden), BF16),
            pltpu.VMEM(((2 * REACH + 1) * rows, depth), BF16),
            pltpu.SemaphoreType.DMA((cells // min(cells, 256) + 1,)),
        ],
        compiler_params=pltpu.CompilerParams(vmem_limit_bytes=16 << 20),
        cost_estimate=pl.CostEstimate(
            flops=2 * cells * depth * hidden, bytes_accessed=4 * (cells + hidden) * depth, transcendentals=cells * hidden
        ),
        name="decode",
    )(owner, weights, ring_own, ring_near, back_own, back_near, grid_part, mesh_part, encoded, first, second)[:2]


def on_device(
    grid, g2m_owner, g2m_weight, m2g_owner, m2g_weight, mesh_feat, neighbours,
    enc_w1, enc_w2, attn_gain, w_qkv, w_out, dec_w1, dec_w2,
):
    rows = mesh_feat.shape[0]
    nblocks = g2m_owner.shape[0]
    encoded, message, base, local = encode(
        g2m_owner, neighbours, g2m_weight.reshape(nblocks, rows), mesh_feat, grid, enc_w1, enc_w2
    )
    outgoing = outgoing_sums(base, swapped(message))
    sums = from_outward(outgoing, 1)
    grid_part = grid_hidden(encoded, dec_w1, outgoing)
    share, message = chip_share(local, sums, grid_part)
    own, pair, message = chip_states(share, swapped(message))
    near = from_outward(message, 1)
    far = from_outward(message, 2)
    behind = swapped(near[:rows])
    query, kv = project(pair, near, attn_gain, w_qkv[0])
    ring_own = attend_own(base, own, query, kv, behind, attn_gain, w_qkv[0], w_out[0])
    ring_near = attend_near(sums, near, query, kv, far, attn_gain, w_qkv[0], w_out[0], ring_own)
    back_own = swapped(ring_own)
    back_near = swapped(ring_near[:rows])
    mesh_part = mesh_hidden(ring_own, ring_near, dec_w1)
    return decode(
        m2g_owner, m2g_weight.reshape(nblocks, rows), ring_own, ring_near, back_own, back_near,
        grid_part, mesh_part, encoded, dec_w1, dec_w2,
    )


def solution(mesh):
    split = P(AXES, None)
    flat = P(AXES)
    in_specs = (split, flat, flat, flat, flat, split, split) + (P(),) * 7
    return jax.shard_map(
        on_device, mesh=mesh, in_specs=in_specs, out_specs=(split, split), check_vma=False
    )
```

```python
import functools

import jax
import jax.numpy as jnp
from jax import lax
from jax.experimental import pallas as pl
from jax.experimental.pallas import tpu as pltpu
from jax.sharding import PartitionSpec as P

HD = 128
REACH = 2
EXTRA = 16
AXES = ("tile", "sub")
BF16 = jnp.bfloat16
F32 = jnp.float32
VMEM = pl.BlockSpec(memory_space=pltpu.VMEM)
SMEM = pl.BlockSpec(memory_space=pltpu.SMEM)
ANY = pl.BlockSpec(memory_space=pl.ANY)


def swapped(block):
    count = lax.axis_size(AXES)
    return lax.ppermute(block, AXES, [(i, i ^ 1) for i in range(count)])


def from_outward(block, chips):
    count = lax.axis_size(AXES)
    route = []
    for i in range(count):
        step = 2 * chips - 1
        route.append((i, (i + step if i % 2 else i - step) % count))
    return lax.ppermute(block, AXES, route)


def tiles_of(rows, columns):
    return min(rows, 512), min(columns, 1024)


def outward_of():
    return 2 * lax.axis_index("sub") - 1


def offset_of(owner, mine, count):
    return lax.rem(owner - mine + REACH + count, count) - REACH


def kept(shape, dtype=BF16):
    return pltpu.VMEM(shape, dtype)


def in_hbm(*arrays):
    return [pltpu.with_memory_space_constraint(a, pltpu.HBM) for a in arrays]


def hidden_layer(x_ref, first, act, tile, part, arrive, before):
    for j in range(first.shape[1] // part):
        before(j)
        cols = slice(j * part, (j + 1) * part)
        for r in range(x_ref.shape[0] // tile):
            if j == 0:
                arrive(r)
            cut = slice(r * tile, (r + 1) * tile)
            half = jnp.dot(x_ref[cut, :] * BF16(0.5), first[:, cols], preferred_element_type=F32)
            act[cut, cols] = (half * jnp.tanh(half) + half).astype(BF16)


def encode_kernel(
    owner_hbm, listed_hbm, weight_hbm, feat_hbm, x_hbm, first_hbm, second_hbm,
    enc_ref, msg_ref, base_ref, loc_ref,
    owner, listed, weight_ref, feat_ref, first, second, act, total, sems, io_sems,
):
    rows, depth = feat_ref.shape
    tile, part = tiles_of(enc_ref.shape[0], first.shape[1])
    tiles, parts = enc_ref.shape[0] // tile, first.shape[1] // part
    loads = [
        pltpu.make_async_copy(x_hbm.at[pl.ds(r * tile, tile)], enc_ref.at[pl.ds(r * tile, tile)], io_sems.at[r])
        for r in range(tiles)
    ]
    ones, twos = [], []
    for j in range(parts):
        cut = pl.ds(j * part, part)
        ones.append(pltpu.make_async_copy(first_hbm.at[:, cut], first.at[:, cut], sems.at[0, j]))
        twos.append(pltpu.make_async_copy(second_hbm.at[cut], second.at[cut], sems.at[1, j]))
    small = [
        pltpu.make_async_copy(weight_hbm, weight_ref, io_sems.at[tiles]),
        pltpu.make_async_copy(feat_hbm, feat_ref, io_sems.at[tiles + 1]),
        pltpu.make_async_copy(owner_hbm, owner, io_sems.at[tiles + 2]),
        pltpu.make_async_copy(listed_hbm, listed, io_sems.at[tiles + 3]),
    ]
    for copy in loads + ones:
        copy.start()

    def arrive(r):
        if r == 0:
            for copy in loads:
                copy.wait()
            for copy in twos + small:
                copy.start()

    mine, count = lax.axis_index(AXES), lax.axis_size(AXES)
    outward = outward_of()
    total[...] = jnp.zeros_like(total)
    hidden_layer(enc_ref, first, act, tile, part, arrive, lambda j: ones[j].wait())
    for copy in twos + small:
        copy.wait()
    columns = jnp.transpose(weight_ref[...])
    tile = min(tile, 256)
    for r in range(enc_ref.shape[0] // tile):
        cut = slice(r * tile, (r + 1) * tile)
        out = jnp.dot(act[cut, :], second[...], preferred_element_type=F32)
        enc_ref[cut, :] = (enc_ref[cut, :].astype(F32) + out).astype(BF16)
        for b in range(r * tile // rows, (r + 1) * tile // rows):
            slot = outward * offset_of(owner[b], mine, count) + REACH
            block = enc_ref[b * rows:(b + 1) * rows, :].astype(F32)
            total[slot] += columns[:, b:b + 1] * block
    absent = sum(-offset_of(listed[0, n], mine, count) for n in range(listed.shape[1])).astype(F32)
    spot = lax.broadcasted_iota(jnp.int32, (EXTRA, depth), 1)
    msg_ref[:rows, :] = total[0].astype(BF16)
    msg_ref[rows:, :] = jnp.where(spot == 1, absent, 0.0).astype(BF16)
    base_ref[:rows, :] = total[4].astype(BF16)
    base_ref[rows:2 * rows, :] = total[3].astype(BF16)
    base_ref[2 * rows:, :] = jnp.where(spot == 0, absent, 0.0).astype(BF16)
    loc_ref[:rows, :] = total[1]
    loc_ref[rows:, :] = total[2] + feat_ref[...].astype(F32)


def encode(owner, listed, weights, feat, grid, first, second):
    cells, depth = grid.shape
    hidden = first.shape[1]
    rows = feat.shape[0]
    tile, part = tiles_of(cells, hidden)
    return pl.pallas_call(
        encode_kernel,
        out_shape=(
            kept((cells, depth)),
            kept((rows + EXTRA, depth)),
            kept((2 * rows + EXTRA, depth)),
            kept((2 * rows, depth), F32),
        ),
        in_specs=[ANY] * 7,
        out_specs=(VMEM,) * 4,
        scratch_shapes=[
            pltpu.SMEM(owner.shape, jnp.int32),
            pltpu.SMEM(listed.shape, jnp.int32),
            pltpu.VMEM(weights.shape, F32),
            pltpu.VMEM(feat.shape, BF16),
            pltpu.VMEM((depth, hidden), BF16),
            pltpu.VMEM((hidden, depth), BF16),
            pltpu.VMEM((cells, hidden), BF16),
            pltpu.VMEM((2 * REACH + 1, rows, depth), F32),
            pltpu.SemaphoreType.DMA((2, hidden // part)),
            pltpu.SemaphoreType.DMA((cells // tile + 4,)),
        ],
        compiler_params=pltpu.CompilerParams(vmem_limit_bytes=24 << 20),
        cost_estimate=pl.CostEstimate(
            flops=4 * cells * depth * hidden, bytes_accessed=4 * (cells + hidden) * depth, transcendentals=cells * hidden
        ),
        name="encode",
    )(*in_hbm(owner, listed, weights, feat, grid, first, second))


def outgoing_kernel(base_ref, arrived_ref, out_ref):
    rows = arrived_ref.shape[0] - EXTRA
    out_ref[:rows, :] = base_ref[:rows, :]
    out_ref[rows:, :] = (base_ref[rows:, :].astype(F32) + arrived_ref[...].astype(F32)).astype(BF16)


def outgoing_sums(base, arrived):
    return pl.pallas_call(
        outgoing_kernel, out_shape=kept(base.shape), in_specs=[VMEM] * 2, out_specs=VMEM,
        compiler_params=pltpu.CompilerParams(vmem_limit_bytes=4 << 20), name="outgoing_sums"
    )(base, arrived)


def share_kernel(loc_ref, arrived_ref, after, share_ref, msg_ref):
    del after
    rows = loc_ref.shape[0] // 2
    share_ref[...] = loc_ref[...] + arrived_ref[:2 * rows, :].astype(F32)
    msg_ref[:rows, :] = share_ref[rows:, :].astype(BF16)
    msg_ref[rows:, :] = share_ref[:rows, :].astype(BF16)


def chip_share(local, arrived, after):
    return pl.pallas_call(
        share_kernel,
        out_shape=(kept(local.shape, F32), kept(local.shape)),
        in_specs=[VMEM] * 2 + [ANY],
        out_specs=(VMEM,) * 2,
        compiler_params=pltpu.CompilerParams(vmem_limit_bytes=4 << 20),
        name="chip_share",
    )(local, arrived, after)


def state_kernel(share_ref, other_ref, own_ref, pair_ref, msg_ref):
    rows = own_ref.shape[0]
    own_ref[...] = share_ref[rows:, :] + other_ref[rows:, :].astype(F32)
    pair_ref[:rows, :] = (share_ref[:rows, :] + other_ref[:rows, :].astype(F32)).astype(BF16)
    pair_ref[rows:, :] = own_ref[...].astype(BF16)
    msg_ref[:rows, :] = pair_ref[rows:, :]
    msg_ref[rows:, :] = pair_ref[:rows, :]


def chip_states(share, other):
    rows, depth = share.shape[0] // 2, share.shape[1]
    return pl.pallas_call(
        state_kernel,
        out_shape=(kept((rows, depth), F32), kept(share.shape), kept(share.shape)),
        in_specs=[VMEM] * 2,
        out_specs=(VMEM,) * 3,
        compiler_params=pltpu.CompilerParams(vmem_limit_bytes=4 << 20),
        name="chip_states",
    )(share, other)


def normal(block, gain):
    state = block.astype(F32)
    scale = lax.rsqrt(jnp.mean(state * state, axis=-1, keepdims=True) + 1e-6)
    return (state * scale * gain).astype(BF16)


def project_kernel(pair_ref, near_ref, gain_ref, w_qkv, query_ref, kv_ref, normed):
    rows, depth = pair_ref.shape[0] // 2, pair_ref.shape[1]
    gain = gain_ref[...]
    normed[:2 * rows, :] = normal(pair_ref[...], gain)
    normed[2 * rows:, :] = normal(near_ref[...], gain)
    kv_ref[...] = jnp.dot(normed[...], w_qkv[:, depth:], preferred_element_type=F32).astype(BF16)
    query_ref[...] = jnp.dot(normed[rows:, :], w_qkv[:, :depth], preferred_element_type=F32).astype(BF16)


def project(pair, near, gain, w_qkv):
    rows, depth = pair.shape[0] // 2, pair.shape[1]
    return pl.pallas_call(
        project_kernel,
        out_shape=(kept((3 * rows, depth)), kept((4 * rows, 2 * depth))),
        in_specs=[VMEM] * 4,
        out_specs=(VMEM,) * 2,
        scratch_shapes=[pltpu.VMEM((4 * rows, depth), BF16)],
        compiler_params=pltpu.CompilerParams(vmem_limit_bytes=8 << 20),
        cost_estimate=pl.CostEstimate(
            flops=22 * rows * depth * depth, bytes_accessed=2 * rows * depth, transcendentals=0
        ),
        name="project",
    )(pair, near, gain, w_qkv)


def attention(query, window, keep):
    depth = query.shape[1]
    heads = []
    for h in range(depth // HD):
        cols = slice(h * HD, (h + 1) * HD)
        value_cols = slice(depth + h * HD, depth + (h + 1) * HD)
        scores = jnp.concatenate([
            lax.dot_general(
                query[:, cols], ref[first:first + size, cols], (((1,), (1,)), ((), ())), preferred_element_type=F32
            )
            for ref, first, size in window
        ], axis=1)
        scores = jnp.where(keep, scores, -jnp.inf)
        below = (scores - jnp.max(scores, axis=-1, keepdims=True)) * (HD ** -0.5)
        grown = jnp.exp(below.astype(BF16))
        start, taken = 0, None
        for ref, first, size in window:
            value = jnp.concatenate([ref[first:first + size, value_cols], jnp.ones((size, HD), BF16)], axis=1)
            term = jnp.dot(grown[:, start:start + size], value, preferred_element_type=F32)
            taken = term if taken is None else taken + term
            start += size
        heads.append((taken[:, :HD] / taken[:, HD:]).astype(BF16))
    return jnp.concatenate(heads, axis=1)


def kept_lanes(rows, absent):
    block = (lax.broadcasted_iota(jnp.int32, (rows, (2 * REACH + 1) * rows), 1) // rows).astype(F32)
    return block != outward_of().astype(F32) * absent.astype(F32) + REACH


def attend_own_kernel(base_ref, own_ref, query_ref, kv_ref, behind_ref, gain_ref, w_qkv, w_out, ring_ref, kv_behind):
    rows, depth = own_ref.shape
    kv_behind[...] = jnp.dot(
        normal(behind_ref[...], gain_ref[...]), w_qkv[:, depth:], preferred_element_type=F32
    ).astype(BF16)
    keep = kept_lanes(rows, base_ref[2 * rows:2 * rows + 1, 0:1])
    mixed = attention(query_ref[:rows, :], [(kv_behind, 0, rows), (kv_ref, 0, 4 * rows)], keep)
    ring_ref[...] = (own_ref[...] + jnp.dot(mixed, w_out[...], preferred_element_type=F32)).astype(BF16)


def attend_near_kernel(
    sums_ref, near_ref, query_ref, kv_ref, far_ref, gain_ref, w_qkv, w_out, after, ring_ref, kv_far, mixed
):
    del after
    rows, depth = near_ref.shape[0] // 2, near_ref.shape[1]
    kv_far[...] = jnp.dot(
        normal(far_ref[...], gain_ref[...]), w_qkv[:, depth:], preferred_element_type=F32
    ).astype(BF16)
    windows = [
        [(kv_ref, 0, 4 * rows), (kv_far, 0, rows)],
        [(kv_ref, rows, 3 * rows), (kv_far, 0, 2 * rows)],
    ]
    for n, window in enumerate(windows):
        keep = kept_lanes(rows, sums_ref[2 * rows:2 * rows + 1, n:n + 1])
        mixed[n * rows:(n + 1) * rows, :] = attention(query_ref[(n + 1) * rows:(n + 2) * rows, :], window, keep)
    added = jnp.dot(mixed[...], w_out[...], preferred_element_type=F32)
    ring_ref[...] = (near_ref[...].astype(F32) + added).astype(BF16)


def attend_own(base, own, query, kv, behind, gain, w_qkv, w_out):
    rows, depth = own.shape
    return pl.pallas_call(
        attend_own_kernel,
        out_shape=kept((rows, depth)),
        in_specs=[VMEM] * 8,
        out_specs=VMEM,
        scratch_shapes=[pltpu.VMEM((rows, 2 * depth), BF16)],
        compiler_params=pltpu.CompilerParams(vmem_limit_bytes=12 << 20),
        cost_estimate=pl.CostEstimate(
            flops=20 * rows * depth * depth, bytes_accessed=2 * rows * depth, transcendentals=0
        ),
        name="attend_own",
    )(base, own, query, kv, behind, gain, w_qkv, w_out)


def attend_near(sums, near, query, kv, far, gain, w_qkv, w_out, after):
    rows, depth = near.shape[0] // 2, near.shape[1]
    return pl.pallas_call(
        attend_near_kernel,
        out_shape=kept((2 * rows, depth)),
        in_specs=[VMEM] * 8 + [ANY],
        out_specs=VMEM,
        scratch_shapes=[pltpu.VMEM((2 * rows, 2 * depth), BF16), pltpu.VMEM((2 * rows, depth), BF16)],
        compiler_params=pltpu.CompilerParams(vmem_limit_bytes=12 << 20),
        cost_estimate=pl.CostEstimate(
            flops=40 * rows * depth * depth, bytes_accessed=2 * rows * depth, transcendentals=0
        ),
        name="attend_near",
    )(sums, near, query, kv, far, gain, w_qkv, w_out, after)


def halved(rows, first):
    return jnp.dot(rows * BF16(0.5), first, preferred_element_type=F32)


def grid_hidden_kernel(enc_ref, first, after, out_ref):
    del after
    tile, part = tiles_of(*out_ref.shape)
    for j in range(out_ref.shape[1] // part):
        cols = slice(j * part, (j + 1) * part)
        for r in range(out_ref.shape[0] // tile):
            cut = slice(r * tile, (r + 1) * tile)
            out_ref[cut, cols] = halved(enc_ref[cut, :], first[:, cols]).astype(BF16)


def grid_hidden(encoded, first, after):
    cells, depth = encoded.shape
    hidden = first.shape[1]
    return pl.pallas_call(
        grid_hidden_kernel,
        out_shape=kept((cells, hidden)),
        in_specs=[VMEM] * 2 + [ANY],
        out_specs=VMEM,
        compiler_params=pltpu.CompilerParams(vmem_limit_bytes=12 << 20),
        cost_estimate=pl.CostEstimate(
            flops=2 * cells * depth * hidden, bytes_accessed=2 * (cells + hidden) * depth, transcendentals=0
        ),
        name="grid_hidden",
    )(encoded, first, after)


def mesh_hidden_kernel(ring_own, ring_near, first, out_ref):
    rows = ring_own.shape[0]
    out_ref[REACH * rows:(REACH + 1) * rows, :] = halved(ring_own[...], first[...]).astype(BF16)
    out_ref[(REACH + 1) * rows:, :] = halved(ring_near[...], first[...]).astype(BF16)


def mesh_hidden(ring_own, ring_near, first):
    rows, depth = ring_own.shape
    return pl.pallas_call(
        mesh_hidden_kernel,
        out_shape=kept(((2 * REACH + 1) * rows, first.shape[1])),
        in_specs=[VMEM] * 3,
        out_specs=VMEM,
        compiler_params=pltpu.CompilerParams(vmem_limit_bytes=12 << 20),
        cost_estimate=pl.CostEstimate(
            flops=6 * rows * depth * first.shape[1], bytes_accessed=2 * rows * depth, transcendentals=0
        ),
        name="mesh_hidden",
    )(ring_own, ring_near, first)


def decode_kernel(
    owner, weight_ref, ring_own, ring_near, back_own, back_near, grid_ref, mesh_in, enc_ref, first, second,
    out_hbm, mesh_hbm, mesh_ref,
    x_ref, act, ring, io_sems,
):
    del mesh_in
    rows = ring_own.shape[0]
    tile, part = tiles_of(x_ref.shape[0], first.shape[1])
    tile = min(tile, 256)
    tiles, parts = x_ref.shape[0] // tile, first.shape[1] // part
    stores = [pltpu.make_async_copy(ring_own, mesh_hbm, io_sems.at[tiles])]
    stores[0].start()
    mine, count = lax.axis_index(AXES), lax.axis_size(AXES)
    outward = outward_of()
    mesh_ref[:rows, :] = halved(back_near[...], first[...]).astype(BF16)
    mesh_ref[rows:2 * rows, :] = halved(back_own[...], first[...]).astype(BF16)
    ring[:rows, :] = back_near[...]
    ring[rows:2 * rows, :] = back_own[...]
    ring[2 * rows:3 * rows, :] = ring_own[...]
    ring[3 * rows:, :] = ring_near[...]
    columns = jnp.transpose(weight_ref[...])
    for r in range(tiles):
        cut = slice(r * tile, (r + 1) * tile)
        for b in range(r * tile // rows, (r + 1) * tile // rows):
            slot = outward * offset_of(owner[b], mine, count) + REACH
            lines = pl.ds(pl.multiple_of(slot * rows, rows), rows)
            block = slice(b * rows, (b + 1) * rows)
            weight = columns[:, b:b + 1]
            narrow = weight.astype(BF16)
            for j in range(parts):
                cols = slice(j * part, (j + 1) * part)
                half = grid_ref[block, cols] + narrow * mesh_ref[lines, cols]
                act[block, cols] = half * jnp.tanh(half) + half
            x_ref[block, :] = (enc_ref[block, :].astype(F32) + weight * ring[lines, :].astype(F32)).astype(BF16)
        out = jnp.dot(act[cut, :], second[...], preferred_element_type=F32)
        x_ref[cut, :] = (x_ref[cut, :].astype(F32) + out).astype(BF16)
        copy = pltpu.make_async_copy(x_ref.at[pl.ds(r * tile, tile)], out_hbm.at[pl.ds(r * tile, tile)], io_sems.at[r])
        copy.start()
        stores.append(copy)
    for copy in stores:
        copy.wait()


def decode(owner, weights, ring_own, ring_near, back_own, back_near, grid_part, mesh_part, encoded, first, second):
    cells, depth = encoded.shape
    hidden = first.shape[1]
    rows = ring_own.shape[0]
    return pl.pallas_call(
        decode_kernel,
        out_shape=(
            jax.ShapeDtypeStruct((cells, depth), BF16),
            jax.ShapeDtypeStruct((rows, depth), BF16),
            kept(mesh_part.shape),
        ),
        in_specs=[SMEM] + [VMEM] * 10,
        out_specs=(ANY, ANY, VMEM),
        input_output_aliases={7: 2},
        scratch_shapes=[
            pltpu.VMEM((cells, depth), BF16),
            pltpu.VMEM((cells, hidden), BF16),
            pltpu.VMEM(((2 * REACH + 1) * rows, depth), BF16),
            pltpu.SemaphoreType.DMA((cells // min(cells, 256) + 1,)),
        ],
        compiler_params=pltpu.CompilerParams(vmem_limit_bytes=16 << 20),
        cost_estimate=pl.CostEstimate(
            flops=2 * cells * depth * hidden, bytes_accessed=4 * (cells + hidden) * depth, transcendentals=cells * hidden
        ),
        name="decode",
    )(owner, weights, ring_own, ring_near, back_own, back_near, grid_part, mesh_part, encoded, first, second)[:2]


def on_device(
    grid, g2m_owner, g2m_weight, m2g_owner, m2g_weight, mesh_feat, neighbours,
    enc_w1, enc_w2, attn_gain, w_qkv, w_out, dec_w1, dec_w2,
):
    rows = mesh_feat.shape[0]
    nblocks = g2m_owner.shape[0]
    encoded, message, base, local = encode(
        g2m_owner, neighbours, g2m_weight.reshape(nblocks, rows), mesh_feat, grid, enc_w1, enc_w2
    )
    outgoing = outgoing_sums(base, swapped(message))
    sums = from_outward(outgoing, 1)
    grid_part = grid_hidden(encoded, dec_w1, outgoing)
    share, message = chip_share(local, sums, grid_part)
    own, pair, message = chip_states(share, swapped(message))
    near = from_outward(message, 1)
    far = from_outward(message, 2)
    behind = swapped(near[:rows])
    query, kv = project(pair, near, attn_gain, w_qkv[0])
    ring_own = attend_own(base, own, query, kv, behind, attn_gain, w_qkv[0], w_out[0])
    ring_near = attend_near(sums, near, query, kv, far, attn_gain, w_qkv[0], w_out[0], ring_own)
    back_own = swapped(ring_own)
    back_near = swapped(ring_near[:rows])
    mesh_part = mesh_hidden(ring_own, ring_near, dec_w1)
    return decode(
        m2g_owner, m2g_weight.reshape(nblocks, rows), ring_own, ring_near, back_own, back_near,
        grid_part, mesh_part, encoded, dec_w1, dec_w2,
    )


def solution(mesh):
    split = P(AXES, None)
    flat = P(AXES)
    in_specs = (split, flat, flat, flat, flat, split, split) + (P(),) * 7
    return jax.shard_map(
        on_device, mesh=mesh, in_specs=in_specs, out_specs=(split, split), check_vma=False
    )
```

```python
import functools

import jax
import jax.numpy as jnp
from jax import lax
from jax.experimental import pallas as pl
from jax.experimental.pallas import tpu as pltpu
from jax.sharding import PartitionSpec as P

HD = 128
REACH = 2
EXTRA = 16
AXES = ("tile", "sub")
BF16 = jnp.bfloat16
F32 = jnp.float32
VMEM = pl.BlockSpec(memory_space=pltpu.VMEM)
SMEM = pl.BlockSpec(memory_space=pltpu.SMEM)
ANY = pl.BlockSpec(memory_space=pl.ANY)


def swapped(block):
    count = lax.axis_size(AXES)
    return lax.ppermute(block, AXES, [(i, i ^ 1) for i in range(count)])


def from_outward(block, chips):
    count = lax.axis_size(AXES)
    route = []
    for i in range(count):
        step = 2 * chips - 1
        route.append((i, (i + step if i % 2 else i - step) % count))
    return lax.ppermute(block, AXES, route)


def tiles_of(rows, columns):
    return min(rows, 512), min(columns, 1024)


def outward_of():
    return 2 * lax.axis_index("sub") - 1


def offset_of(owner, mine, count):
    return lax.rem(owner - mine + REACH + count, count) - REACH


def kept(shape, dtype=BF16):
    return pltpu.VMEM(shape, dtype)


def in_hbm(*arrays):
    return [pltpu.with_memory_space_constraint(a, pltpu.HBM) for a in arrays]


def hidden_layer(x_ref, first, act, tile, part, arrive, before):
    for j in range(first.shape[1] // part):
        before(j)
        cols = slice(j * part, (j + 1) * part)
        for r in range(x_ref.shape[0] // tile):
            if j == 0:
                arrive(r)
            cut = slice(r * tile, (r + 1) * tile)
            half = jnp.dot(x_ref[cut, :] * BF16(0.5), first[:, cols], preferred_element_type=F32)
            act[cut, cols] = (half * jnp.tanh(half) + half).astype(BF16)


def encode_kernel(
    owner_hbm, listed_hbm, weight_hbm, feat_hbm, x_hbm, first_hbm, second_hbm,
    enc_ref, msg_ref, base_ref, loc_ref,
    owner, listed, weight_ref, feat_ref, first, second, act, total, sems, io_sems,
):
    rows, depth = feat_ref.shape
    tile, part = tiles_of(enc_ref.shape[0], first.shape[1])
    tiles, parts = enc_ref.shape[0] // tile, first.shape[1] // part
    loads = [
        pltpu.make_async_copy(x_hbm.at[pl.ds(r * tile, tile)], enc_ref.at[pl.ds(r * tile, tile)], io_sems.at[r])
        for r in range(tiles)
    ]
    ones, twos = [], []
    for j in range(parts):
        cut = pl.ds(j * part, part)
        ones.append(pltpu.make_async_copy(first_hbm.at[:, cut], first.at[:, cut], sems.at[0, j]))
        twos.append(pltpu.make_async_copy(second_hbm.at[cut], second.at[cut], sems.at[1, j]))
    small = [
        pltpu.make_async_copy(weight_hbm, weight_ref, io_sems.at[tiles]),
        pltpu.make_async_copy(feat_hbm, feat_ref, io_sems.at[tiles + 1]),
        pltpu.make_async_copy(owner_hbm, owner, io_sems.at[tiles + 2]),
        pltpu.make_async_copy(listed_hbm, listed, io_sems.at[tiles + 3]),
    ]
    for copy in loads + ones:
        copy.start()

    def arrive(r):
        if r == 0:
            for copy in loads:
                copy.wait()
            for copy in twos + small:
                copy.start()

    mine, count = lax.axis_index(AXES), lax.axis_size(AXES)
    outward = outward_of()
    total[...] = jnp.zeros_like(total)
    hidden_layer(enc_ref, first, act, tile, part, arrive, lambda j: ones[j].wait())
    for copy in twos + small:
        copy.wait()
    columns = jnp.transpose(weight_ref[...])
    tile = min(tile, 256)
    for r in range(enc_ref.shape[0] // tile):
        cut = slice(r * tile, (r + 1) * tile)
        out = jnp.dot(act[cut, :], second[...], preferred_element_type=F32)
        enc_ref[cut, :] = (enc_ref[cut, :].astype(F32) + out).astype(BF16)
        for b in range(r * tile // rows, (r + 1) * tile // rows):
            slot = outward * offset_of(owner[b], mine, count) + REACH
            block = enc_ref[b * rows:(b + 1) * rows, :].astype(F32)
            total[slot] += columns[:, b:b + 1] * block
    absent = sum(-offset_of(listed[0, n], mine, count) for n in range(listed.shape[1])).astype(F32)
    spot = lax.broadcasted_iota(jnp.int32, (EXTRA, depth), 1)
    msg_ref[:rows, :] = total[0].astype(BF16)
    msg_ref[rows:, :] = jnp.where(spot == 1, absent, 0.0).astype(BF16)
    base_ref[:rows, :] = total[4].astype(BF16)
    base_ref[rows:2 * rows, :] = total[3].astype(BF16)
    base_ref[2 * rows:, :] = jnp.where(spot == 0, absent, 0.0).astype(BF16)
    loc_ref[:rows, :] = total[1]
    loc_ref[rows:, :] = total[2] + feat_ref[...].astype(F32)


def encode(owner, listed, weights, feat, grid, first, second):
    cells, depth = grid.shape
    hidden = first.shape[1]
    rows = feat.shape[0]
    tile, part = tiles_of(cells, hidden)
    return pl.pallas_call(
        encode_kernel,
        out_shape=(
            kept((cells, depth)),
            kept((rows + EXTRA, depth)),
            kept((2 * rows + EXTRA, depth)),
            kept((2 * rows, depth), F32),
        ),
        in_specs=[ANY] * 7,
        out_specs=(VMEM,) * 4,
        scratch_shapes=[
            pltpu.SMEM(owner.shape, jnp.int32),
            pltpu.SMEM(listed.shape, jnp.int32),
            pltpu.VMEM(weights.shape, F32),
            pltpu.VMEM(feat.shape, BF16),
            pltpu.VMEM((depth, hidden), BF16),
            pltpu.VMEM((hidden, depth), BF16),
            pltpu.VMEM((cells, hidden), BF16),
            pltpu.VMEM((2 * REACH + 1, rows, depth), F32),
            pltpu.SemaphoreType.DMA((2, hidden // part)),
            pltpu.SemaphoreType.DMA((cells // tile + 4,)),
        ],
        compiler_params=pltpu.CompilerParams(vmem_limit_bytes=24 << 20),
        cost_estimate=pl.CostEstimate(
            flops=4 * cells * depth * hidden, bytes_accessed=4 * (cells + hidden) * depth, transcendentals=cells * hidden
        ),
        name="encode",
    )(*in_hbm(owner, listed, weights, feat, grid, first, second))


def outgoing_kernel(base_ref, arrived_ref, out_ref):
    rows = arrived_ref.shape[0] - EXTRA
    out_ref[:rows, :] = base_ref[:rows, :]
    out_ref[rows:, :] = (base_ref[rows:, :].astype(F32) + arrived_ref[...].astype(F32)).astype(BF16)


def outgoing_sums(base, arrived):
    return pl.pallas_call(
        outgoing_kernel, out_shape=kept(base.shape), in_specs=[VMEM] * 2, out_specs=VMEM,
        compiler_params=pltpu.CompilerParams(vmem_limit_bytes=4 << 20), name="outgoing_sums"
    )(base, arrived)


def share_kernel(loc_ref, arrived_ref, after, share_ref, msg_ref):
    del after
    rows = loc_ref.shape[0] // 2
    share_ref[...] = loc_ref[...] + arrived_ref[:2 * rows, :].astype(F32)
    msg_ref[:rows, :] = share_ref[rows:, :].astype(BF16)
    msg_ref[rows:, :] = share_ref[:rows, :].astype(BF16)


def chip_share(local, arrived, after):
    return pl.pallas_call(
        share_kernel,
        out_shape=(kept(local.shape, F32), kept(local.shape)),
        in_specs=[VMEM] * 2 + [ANY],
        out_specs=(VMEM,) * 2,
        compiler_params=pltpu.CompilerParams(vmem_limit_bytes=4 << 20),
        name="chip_share",
    )(local, arrived, after)


def state_kernel(share_ref, other_ref, own_ref, pair_ref, msg_ref):
    rows = own_ref.shape[0]
    own_ref[...] = share_ref[rows:, :] + other_ref[rows:, :].astype(F32)
    pair_ref[:rows, :] = (share_ref[:rows, :] + other_ref[:rows, :].astype(F32)).astype(BF16)
    pair_ref[rows:, :] = own_ref[...].astype(BF16)
    msg_ref[:rows, :] = pair_ref[rows:, :]
    msg_ref[rows:, :] = pair_ref[:rows, :]


def chip_states(share, other):
    rows, depth = share.shape[0] // 2, share.shape[1]
    return pl.pallas_call(
        state_kernel,
        out_shape=(kept((rows, depth), F32), kept(share.shape), kept(share.shape)),
        in_specs=[VMEM] * 2,
        out_specs=(VMEM,) * 3,
        compiler_params=pltpu.CompilerParams(vmem_limit_bytes=4 << 20),
        name="chip_states",
    )(share, other)


def normal(block, gain):
    state = block.astype(F32)
    scale = lax.rsqrt(jnp.mean(state * state, axis=-1, keepdims=True) + 1e-6)
    return (state * scale * gain).astype(BF16)


def project_kernel(pair_ref, near_ref, gain_ref, w_qkv, query_ref, kv_ref, normed):
    rows, depth = pair_ref.shape[0] // 2, pair_ref.shape[1]
    gain = gain_ref[...]
    normed[:2 * rows, :] = normal(pair_ref[...], gain)
    normed[2 * rows:, :] = normal(near_ref[...], gain)
    kv_ref[...] = jnp.dot(normed[...], w_qkv[:, depth:], preferred_element_type=F32).astype(BF16)
    query_ref[...] = jnp.dot(normed[rows:, :], w_qkv[:, :depth], preferred_element_type=F32).astype(BF16)


def project(pair, near, gain, w_qkv):
    rows, depth = pair.shape[0] // 2, pair.shape[1]
    return pl.pallas_call(
        project_kernel,
        out_shape=(kept((3 * rows, depth)), kept((4 * rows, 2 * depth))),
        in_specs=[VMEM] * 4,
        out_specs=(VMEM,) * 2,
        scratch_shapes=[pltpu.VMEM((4 * rows, depth), BF16)],
        compiler_params=pltpu.CompilerParams(vmem_limit_bytes=8 << 20),
        cost_estimate=pl.CostEstimate(
            flops=22 * rows * depth * depth, bytes_accessed=2 * rows * depth, transcendentals=0
        ),
        name="project",
    )(pair, near, gain, w_qkv)


def attention(query, window, keep):
    depth = query.shape[1]
    every = [slice(h * HD, (h + 1) * HD) for h in range(depth // HD)]
    scores = [
        jnp.concatenate([
            lax.dot_general(
                query[:, cols], ref[first:first + size, cols], (((1,), (1,)), ((), ())), preferred_element_type=F32
            )
            for ref, first, size in window
        ], axis=1)
        for cols in every
    ]
    scores = [jnp.where(keep, score, -jnp.inf) for score in scores]
    below = [(score - jnp.max(score, axis=-1, keepdims=True)) * (HD ** -0.5) for score in scores]
    grown = [jnp.exp(score.astype(BF16)) for score in below]
    heads = []
    for h, cols in enumerate(every):
        start, taken = 0, None
        for ref, first, size in window:
            value = ref[first:first + size, depth + cols.start:depth + cols.stop]
            value = jnp.concatenate([value, jnp.ones((size, HD), BF16)], axis=1)
            term = jnp.dot(grown[h][:, start:start + size], value, preferred_element_type=F32)
            taken = term if taken is None else taken + term
            start += size
        heads.append((taken[:, :HD] / taken[:, HD:]).astype(BF16))
    return jnp.concatenate(heads, axis=1)


def kept_lanes(rows, absent):
    block = (lax.broadcasted_iota(jnp.int32, (rows, (2 * REACH + 1) * rows), 1) // rows).astype(F32)
    return block != outward_of().astype(F32) * absent.astype(F32) + REACH


def attend_own_kernel(base_ref, own_ref, query_ref, kv_ref, behind_ref, gain_ref, w_qkv, w_out, ring_ref, kv_behind):
    rows, depth = own_ref.shape
    kv_behind[...] = jnp.dot(
        normal(behind_ref[...], gain_ref[...]), w_qkv[:, depth:], preferred_element_type=F32
    ).astype(BF16)
    keep = kept_lanes(rows, base_ref[2 * rows:2 * rows + 1, 0:1])
    mixed = attention(query_ref[:rows, :], [(kv_behind, 0, rows), (kv_ref, 0, 4 * rows)], keep)
    ring_ref[...] = (own_ref[...] + jnp.dot(mixed, w_out[...], preferred_element_type=F32)).astype(BF16)


def attend_near_kernel(
    sums_ref, near_ref, query_ref, kv_ref, far_ref, gain_ref, w_qkv, w_out, after, ring_ref, kv_far, mixed
):
    del after
    rows, depth = near_ref.shape[0] // 2, near_ref.shape[1]
    kv_far[...] = jnp.dot(
        normal(far_ref[...], gain_ref[...]), w_qkv[:, depth:], preferred_element_type=F32
    ).astype(BF16)
    windows = [
        [(kv_ref, 0, 4 * rows), (kv_far, 0, rows)],
        [(kv_ref, rows, 3 * rows), (kv_far, 0, 2 * rows)],
    ]
    for n, window in enumerate(windows):
        keep = kept_lanes(rows, sums_ref[2 * rows:2 * rows + 1, n:n + 1])
        mixed[n * rows:(n + 1) * rows, :] = attention(query_ref[(n + 1) * rows:(n + 2) * rows, :], window, keep)
    added = jnp.dot(mixed[...], w_out[...], preferred_element_type=F32)
    ring_ref[...] = (near_ref[...].astype(F32) + added).astype(BF16)


def attend_own(base, own, query, kv, behind, gain, w_qkv, w_out):
    rows, depth = own.shape
    return pl.pallas_call(
        attend_own_kernel,
        out_shape=kept((rows, depth)),
        in_specs=[VMEM] * 8,
        out_specs=VMEM,
        scratch_shapes=[pltpu.VMEM((rows, 2 * depth), BF16)],
        compiler_params=pltpu.CompilerParams(vmem_limit_bytes=12 << 20),
        cost_estimate=pl.CostEstimate(
            flops=20 * rows * depth * depth, bytes_accessed=2 * rows * depth, transcendentals=0
        ),
        name="attend_own",
    )(base, own, query, kv, behind, gain, w_qkv, w_out)


def attend_near(sums, near, query, kv, far, gain, w_qkv, w_out, after):
    rows, depth = near.shape[0] // 2, near.shape[1]
    return pl.pallas_call(
        attend_near_kernel,
        out_shape=kept((2 * rows, depth)),
        in_specs=[VMEM] * 8 + [ANY],
        out_specs=VMEM,
        scratch_shapes=[pltpu.VMEM((2 * rows, 2 * depth), BF16), pltpu.VMEM((2 * rows, depth), BF16)],
        compiler_params=pltpu.CompilerParams(vmem_limit_bytes=12 << 20),
        cost_estimate=pl.CostEstimate(
            flops=40 * rows * depth * depth, bytes_accessed=2 * rows * depth, transcendentals=0
        ),
        name="attend_near",
    )(sums, near, query, kv, far, gain, w_qkv, w_out, after)


def halved(rows, first):
    return jnp.dot(rows * BF16(0.5), first, preferred_element_type=F32)


def grid_hidden_kernel(enc_ref, first, after, out_ref):
    del after
    tile, part = tiles_of(*out_ref.shape)
    for j in range(out_ref.shape[1] // part):
        cols = slice(j * part, (j + 1) * part)
        for r in range(out_ref.shape[0] // tile):
            cut = slice(r * tile, (r + 1) * tile)
            out_ref[cut, cols] = halved(enc_ref[cut, :], first[:, cols]).astype(BF16)


def grid_hidden(encoded, first, after):
    cells, depth = encoded.shape
    hidden = first.shape[1]
    return pl.pallas_call(
        grid_hidden_kernel,
        out_shape=kept((cells, hidden)),
        in_specs=[VMEM] * 2 + [ANY],
        out_specs=VMEM,
        compiler_params=pltpu.CompilerParams(vmem_limit_bytes=12 << 20),
        cost_estimate=pl.CostEstimate(
            flops=2 * cells * depth * hidden, bytes_accessed=2 * (cells + hidden) * depth, transcendentals=0
        ),
        name="grid_hidden",
    )(encoded, first, after)


def mesh_hidden_kernel(back_own, ring_own, ring_near, first, out_ref):
    rows = ring_own.shape[0]
    out_ref[rows:REACH * rows, :] = halved(back_own[...], first[...]).astype(BF16)
    out_ref[REACH * rows:(REACH + 1) * rows, :] = halved(ring_own[...], first[...]).astype(BF16)
    out_ref[(REACH + 1) * rows:, :] = halved(ring_near[...], first[...]).astype(BF16)


def mesh_hidden(back_own, ring_own, ring_near, first):
    rows, depth = ring_own.shape
    return pl.pallas_call(
        mesh_hidden_kernel,
        out_shape=kept(((2 * REACH + 1) * rows, first.shape[1])),
        in_specs=[VMEM] * 4,
        out_specs=VMEM,
        compiler_params=pltpu.CompilerParams(vmem_limit_bytes=12 << 20),
        cost_estimate=pl.CostEstimate(
            flops=8 * rows * depth * first.shape[1], bytes_accessed=2 * rows * depth, transcendentals=0
        ),
        name="mesh_hidden",
    )(back_own, ring_own, ring_near, first)


def decode_kernel(
    owner_hbm, weight_ref, ring_own, ring_near, back_own, back_near, grid_ref, mesh_in, enc_ref, first, second,
    out_hbm, mesh_hbm, mesh_ref,
    owner, x_ref, act, ring, io_sems,
):
    del mesh_in
    rows = ring_own.shape[0]
    tile, part = tiles_of(x_ref.shape[0], first.shape[1])
    tile = min(tile, 256)
    tiles, parts = x_ref.shape[0] // tile, first.shape[1] // part
    stores = [pltpu.make_async_copy(ring_own, mesh_hbm, io_sems.at[tiles])]
    index = pltpu.make_async_copy(owner_hbm, owner, io_sems.at[tiles + 1])
    index.start()
    stores[0].start()
    mine, count = lax.axis_index(AXES), lax.axis_size(AXES)
    outward = outward_of()
    mesh_ref[:rows, :] = halved(back_near[...], first[...]).astype(BF16)
    ring[:rows, :] = back_near[...]
    ring[rows:2 * rows, :] = back_own[...]
    ring[2 * rows:3 * rows, :] = ring_own[...]
    ring[3 * rows:, :] = ring_near[...]
    columns = jnp.transpose(weight_ref[...])
    index.wait()
    for r in range(tiles):
        cut = slice(r * tile, (r + 1) * tile)
        for b in range(r * tile // rows, (r + 1) * tile // rows):
            slot = outward * offset_of(owner[b], mine, count) + REACH
            lines = pl.ds(pl.multiple_of(slot * rows, rows), rows)
            block = slice(b * rows, (b + 1) * rows)
            weight = columns[:, b:b + 1]
            narrow = weight.astype(BF16)
            for j in range(parts):
                cols = slice(j * part, (j + 1) * part)
                half = grid_ref[block, cols] + narrow * mesh_ref[lines, cols]
                act[block, cols] = half * jnp.tanh(half) + half
            x_ref[block, :] = (enc_ref[block, :].astype(F32) + weight * ring[lines, :].astype(F32)).astype(BF16)
        out = jnp.dot(act[cut, :], second[...], preferred_element_type=F32)
        x_ref[cut, :] = (x_ref[cut, :].astype(F32) + out).astype(BF16)
        copy = pltpu.make_async_copy(x_ref.at[pl.ds(r * tile, tile)], out_hbm.at[pl.ds(r * tile, tile)], io_sems.at[r])
        copy.start()
        stores.append(copy)
    for copy in stores:
        copy.wait()


def decode(owner, weights, ring_own, ring_near, back_own, back_near, grid_part, mesh_part, encoded, first, second):
    cells, depth = encoded.shape
    hidden = first.shape[1]
    rows = ring_own.shape[0]
    return pl.pallas_call(
        decode_kernel,
        out_shape=(
            jax.ShapeDtypeStruct((cells, depth), BF16),
            jax.ShapeDtypeStruct((rows, depth), BF16),
            kept(mesh_part.shape),
        ),
        in_specs=[ANY] + [VMEM] * 10,
        out_specs=(ANY, ANY, VMEM),
        input_output_aliases={7: 2},
        scratch_shapes=[
            pltpu.SMEM(owner.shape, jnp.int32),
            pltpu.VMEM((cells, depth), BF16),
            pltpu.VMEM((cells, hidden), BF16),
            pltpu.VMEM(((2 * REACH + 1) * rows, depth), BF16),
            pltpu.SemaphoreType.DMA((cells // min(cells, 256) + 2,)),
        ],
        compiler_params=pltpu.CompilerParams(vmem_limit_bytes=16 << 20),
        cost_estimate=pl.CostEstimate(
            flops=2 * cells * depth * hidden, bytes_accessed=4 * (cells + hidden) * depth, transcendentals=cells * hidden
        ),
        name="decode",
    )(*in_hbm(owner), weights, ring_own, ring_near, back_own, back_near, grid_part, mesh_part, encoded, first, second)[:2]


def on_device(
    grid, g2m_owner, g2m_weight, m2g_owner, m2g_weight, mesh_feat, neighbours,
    enc_w1, enc_w2, attn_gain, w_qkv, w_out, dec_w1, dec_w2,
):
    rows = mesh_feat.shape[0]
    nblocks = g2m_owner.shape[0]
    encoded, message, base, local = encode(
        g2m_owner, neighbours, g2m_weight.reshape(nblocks, rows), mesh_feat, grid, enc_w1, enc_w2
    )
    outgoing = outgoing_sums(base, swapped(message))
    sums = from_outward(outgoing, 1)
    grid_part = grid_hidden(encoded, dec_w1, outgoing)
    share, message = chip_share(local, sums, grid_part)
    own, pair, message = chip_states(share, swapped(message))
    near = from_outward(message, 1)
    far = from_outward(message, 2)
    behind = swapped(near[:rows])
    query, kv = project(pair, near, attn_gain, w_qkv[0])
    ring_own = attend_own(base, own, query, kv, behind, attn_gain, w_qkv[0], w_out[0])
    ring_near = attend_near(sums, near, query, kv, far, attn_gain, w_qkv[0], w_out[0], ring_own)
    back_own = swapped(ring_own)
    back_near = swapped(ring_near[:rows])
    mesh_part = mesh_hidden(back_own, ring_own, ring_near, dec_w1)
    return decode(
        m2g_owner, m2g_weight.reshape(nblocks, rows), ring_own, ring_near, back_own, back_near,
        grid_part, mesh_part, encoded, dec_w1, dec_w2,
    )


def solution(mesh):
    split = P(AXES, None)
    flat = P(AXES)
    in_specs = (split, flat, flat, flat, flat, split, split) + (P(),) * 7
    return jax.shard_map(
        on_device, mesh=mesh, in_specs=in_specs, out_specs=(split, split), check_vma=False
    )
```

```python
import functools

import jax
import jax.numpy as jnp
from jax import lax
from jax.experimental import pallas as pl
from jax.experimental.pallas import tpu as pltpu
from jax.sharding import PartitionSpec as P

HD = 128
REACH = 2
EXTRA = 16
AXES = ("tile", "sub")
BF16 = jnp.bfloat16
F32 = jnp.float32
VMEM = pl.BlockSpec(memory_space=pltpu.VMEM)
SMEM = pl.BlockSpec(memory_space=pltpu.SMEM)
ANY = pl.BlockSpec(memory_space=pl.ANY)


def swapped(block):
    count = lax.axis_size(AXES)
    return lax.ppermute(block, AXES, [(i, i ^ 1) for i in range(count)])


def from_outward(block, chips):
    count = lax.axis_size(AXES)
    route = []
    for i in range(count):
        step = 2 * chips - 1
        route.append((i, (i + step if i % 2 else i - step) % count))
    return lax.ppermute(block, AXES, route)


def tiles_of(rows, columns):
    return min(rows, 1024), min(columns, 1024)


def outward_of():
    return 2 * lax.axis_index("sub") - 1


def offset_of(owner, mine, count):
    return lax.rem(owner - mine + REACH + count, count) - REACH


def kept(shape, dtype=BF16):
    return pltpu.VMEM(shape, dtype)


def in_hbm(*arrays):
    return [pltpu.with_memory_space_constraint(a, pltpu.HBM) for a in arrays]


def hidden_layer(x_ref, first, act, tile, part, arrive, before):
    for j in range(first.shape[1] // part):
        before(j)
        cols = slice(j * part, (j + 1) * part)
        for r in range(x_ref.shape[0] // tile):
            if j == 0:
                arrive(r)
            cut = slice(r * tile, (r + 1) * tile)
            half = jnp.dot(x_ref[cut, :] * BF16(0.5), first[:, cols], preferred_element_type=F32)
            act[cut, cols] = (half * jnp.tanh(half) + half).astype(BF16)


def encode_kernel(
    owner_hbm, listed_hbm, weight_hbm, feat_hbm, x_hbm, first_hbm, second_hbm, next_hbm,
    enc_ref, msg_ref, base_ref, loc_ref, next_ref,
    owner, listed, weight_ref, feat_ref, first, second, act, total, sems, io_sems,
):
    rows, depth = feat_ref.shape
    tile, part = tiles_of(enc_ref.shape[0], first.shape[1])
    tiles, parts = enc_ref.shape[0] // tile, first.shape[1] // part
    loads = [
        pltpu.make_async_copy(x_hbm.at[pl.ds(r * tile, tile)], enc_ref.at[pl.ds(r * tile, tile)], io_sems.at[r])
        for r in range(tiles)
    ]
    ones, twos = [], []
    for j in range(parts):
        cut = pl.ds(j * part, part)
        ones.append(pltpu.make_async_copy(first_hbm.at[:, cut], first.at[:, cut], sems.at[0, j]))
        twos.append(pltpu.make_async_copy(second_hbm.at[cut], second.at[cut], sems.at[1, j]))
    small = [
        pltpu.make_async_copy(weight_hbm, weight_ref, io_sems.at[tiles]),
        pltpu.make_async_copy(feat_hbm, feat_ref, io_sems.at[tiles + 1]),
        pltpu.make_async_copy(owner_hbm, owner, io_sems.at[tiles + 2]),
        pltpu.make_async_copy(listed_hbm, listed, io_sems.at[tiles + 3]),
    ]
    later = pltpu.make_async_copy(next_hbm, next_ref, io_sems.at[tiles + 4])
    for copy in loads + ones + twos + small + [later]:
        copy.start()

    def arrive(r):
        if r == 0:
            for copy in loads:
                copy.wait()

    mine, count = lax.axis_index(AXES), lax.axis_size(AXES)
    outward = outward_of()
    total[...] = jnp.zeros_like(total)

    def before(j):
        due = ones[:1] if j == 0 else []
        if j == min(1, parts - 1):
            due = due + ones[1:] + twos + small
        for copy in due:
            copy.wait()

    hidden_layer(enc_ref, first, act, tile, part, arrive, before)
    columns = jnp.transpose(weight_ref[...])
    tile = min(tile, 256)
    for r in range(enc_ref.shape[0] // tile):
        cut = slice(r * tile, (r + 1) * tile)
        out = enc_ref[cut, :].astype(F32) + jnp.dot(act[cut, :], second[...], preferred_element_type=F32)
        enc_ref[cut, :] = out.astype(BF16)
        for b in range(r * tile // rows, (r + 1) * tile // rows):
            slot = outward * offset_of(owner[b], mine, count) + REACH
            total[slot] += columns[:, b:b + 1] * out[b * rows - r * tile:(b + 1) * rows - r * tile, :]
    absent = sum(-offset_of(listed[0, n], mine, count) for n in range(listed.shape[1])).astype(F32)
    spot = lax.broadcasted_iota(jnp.int32, (EXTRA, depth), 1)
    msg_ref[:rows, :] = total[0].astype(BF16)
    msg_ref[rows:, :] = jnp.where(spot == 1, absent, 0.0).astype(BF16)
    base_ref[:rows, :] = total[4].astype(BF16)
    base_ref[rows:2 * rows, :] = total[3].astype(BF16)
    base_ref[2 * rows:, :] = jnp.where(spot == 0, absent, 0.0).astype(BF16)
    loc_ref[:rows, :] = total[1]
    loc_ref[rows:, :] = total[2] + feat_ref[...].astype(F32)
    later.wait()


def encode(owner, listed, weights, feat, grid, first, second, following):
    cells, depth = grid.shape
    hidden = first.shape[1]
    rows = feat.shape[0]
    tile, part = tiles_of(cells, hidden)
    return pl.pallas_call(
        encode_kernel,
        out_shape=(
            kept((cells, depth)),
            kept((rows + EXTRA, depth)),
            kept((2 * rows + EXTRA, depth)),
            kept((2 * rows, depth), F32),
            kept(following.shape),
        ),
        in_specs=[ANY] * 8,
        out_specs=(VMEM,) * 5,
        scratch_shapes=[
            pltpu.SMEM(owner.shape, jnp.int32),
            pltpu.SMEM(listed.shape, jnp.int32),
            pltpu.VMEM(weights.shape, F32),
            pltpu.VMEM(feat.shape, BF16),
            pltpu.VMEM((depth, hidden), BF16),
            pltpu.VMEM((hidden, depth), BF16),
            pltpu.VMEM((cells, hidden), BF16),
            pltpu.VMEM((2 * REACH + 1, rows, depth), F32),
            pltpu.SemaphoreType.DMA((2, hidden // part)),
            pltpu.SemaphoreType.DMA((cells // tile + 5,)),
        ],
        compiler_params=pltpu.CompilerParams(vmem_limit_bytes=24 << 20),
        cost_estimate=pl.CostEstimate(
            flops=4 * cells * depth * hidden, bytes_accessed=4 * (cells + hidden) * depth, transcendentals=cells * hidden
        ),
        name="encode",
    )(*in_hbm(owner, listed, weights, feat, grid, first, second, following))


def outgoing_kernel(base_ref, arrived_ref, out_ref):
    rows = arrived_ref.shape[0] - EXTRA
    out_ref[:rows, :] = base_ref[:rows, :]
    out_ref[rows:, :] = (base_ref[rows:, :].astype(F32) + arrived_ref[...].astype(F32)).astype(BF16)


def outgoing_sums(base, arrived):
    return pl.pallas_call(
        outgoing_kernel, out_shape=kept(base.shape), in_specs=[VMEM] * 2, out_specs=VMEM,
        compiler_params=pltpu.CompilerParams(vmem_limit_bytes=4 << 20), name="outgoing_sums"
    )(base, arrived)


def share_kernel(loc_ref, arrived_ref, after, share_ref, msg_ref):
    del after
    rows = loc_ref.shape[0] // 2
    share_ref[...] = loc_ref[...] + arrived_ref[:2 * rows, :].astype(F32)
    msg_ref[:rows, :] = share_ref[rows:, :].astype(BF16)
    msg_ref[rows:, :] = share_ref[:rows, :].astype(BF16)


def chip_share(local, arrived, after):
    return pl.pallas_call(
        share_kernel,
        out_shape=(kept(local.shape, F32), kept(local.shape)),
        in_specs=[VMEM] * 2 + [ANY],
        out_specs=(VMEM,) * 2,
        compiler_params=pltpu.CompilerParams(vmem_limit_bytes=4 << 20),
        name="chip_share",
    )(local, arrived, after)


def state_kernel(share_ref, other_ref, own_ref, pair_ref, msg_ref):
    rows = own_ref.shape[0]
    own_ref[...] = share_ref[rows:, :] + other_ref[rows:, :].astype(F32)
    pair_ref[:rows, :] = (share_ref[:rows, :] + other_ref[:rows, :].astype(F32)).astype(BF16)
    pair_ref[rows:, :] = own_ref[...].astype(BF16)
    msg_ref[:rows, :] = pair_ref[rows:, :]
    msg_ref[rows:, :] = pair_ref[:rows, :]


def chip_states(share, other):
    rows, depth = share.shape[0] // 2, share.shape[1]
    return pl.pallas_call(
        state_kernel,
        out_shape=(kept((rows, depth), F32), kept(share.shape), kept(share.shape)),
        in_specs=[VMEM] * 2,
        out_specs=(VMEM,) * 3,
        compiler_params=pltpu.CompilerParams(vmem_limit_bytes=4 << 20),
        name="chip_states",
    )(share, other)


def normal(block, gain):
    state = block.astype(F32)
    scale = lax.rsqrt(jnp.mean(state * state, axis=-1, keepdims=True) + 1e-6)
    return (state * scale * gain).astype(BF16)


def project_kernel(pair_ref, near_ref, gain_ref, w_qkv, query_ref, kv_ref, normed):
    rows, depth = pair_ref.shape[0] // 2, pair_ref.shape[1]
    gain = gain_ref[...]
    normed[:2 * rows, :] = normal(pair_ref[...], gain)
    normed[2 * rows:, :] = normal(near_ref[...], gain)
    kv_ref[...] = jnp.dot(normed[...], w_qkv[:, depth:], preferred_element_type=F32).astype(BF16)
    query_ref[...] = jnp.dot(normed[rows:, :], w_qkv[:, :depth], preferred_element_type=F32).astype(BF16)


def project(pair, near, gain, w_qkv):
    rows, depth = pair.shape[0] // 2, pair.shape[1]
    return pl.pallas_call(
        project_kernel,
        out_shape=(kept((3 * rows, depth)), kept((4 * rows, 2 * depth))),
        in_specs=[VMEM] * 4,
        out_specs=(VMEM,) * 2,
        scratch_shapes=[pltpu.VMEM((4 * rows, depth), BF16)],
        compiler_params=pltpu.CompilerParams(vmem_limit_bytes=8 << 20),
        cost_estimate=pl.CostEstimate(
            flops=22 * rows * depth * depth, bytes_accessed=2 * rows * depth, transcendentals=0
        ),
        name="project",
    )(pair, near, gain, w_qkv)


def attention(query, window, keep):
    depth = query.shape[1]
    every = [slice(h * HD, (h + 1) * HD) for h in range(depth // HD)]
    scores = [
        jnp.concatenate([
            lax.dot_general(
                query[:, cols], ref[first:first + size, cols], (((1,), (1,)), ((), ())), preferred_element_type=F32
            )
            for ref, first, size in window
        ], axis=1)
        for cols in every
    ]
    scores = [jnp.where(keep, score, -jnp.inf) for score in scores]
    below = [(score - jnp.max(score, axis=-1, keepdims=True)) * (HD ** -0.5) for score in scores]
    grown = [jnp.exp(score.astype(BF16)) for score in below]
    heads = []
    for h, cols in enumerate(every):
        start, taken = 0, None
        for ref, first, size in window:
            value = ref[first:first + size, depth + cols.start:depth + cols.stop]
            value = jnp.concatenate([value, jnp.ones((size, HD), BF16)], axis=1)
            term = jnp.dot(grown[h][:, start:start + size], value, preferred_element_type=F32)
            taken = term if taken is None else taken + term
            start += size
        heads.append((taken[:, :HD] / taken[:, HD:]).astype(BF16))
    return jnp.concatenate(heads, axis=1)


def kept_lanes(rows, absent):
    block = (lax.broadcasted_iota(jnp.int32, (rows, (2 * REACH + 1) * rows), 1) // rows).astype(F32)
    return block != outward_of().astype(F32) * absent + REACH


def attend_own_kernel(base_ref, own_ref, query_ref, kv_ref, behind_ref, gain_ref, w_qkv, w_out, ring_ref, kv_behind):
    rows, depth = own_ref.shape
    kv_behind[...] = jnp.dot(
        normal(behind_ref[...], gain_ref[...]), w_qkv[:, depth:], preferred_element_type=F32
    ).astype(BF16)
    keep = kept_lanes(rows, base_ref[2 * rows:, 0:HD].astype(F32)[0:1, 0:1])
    mixed = attention(query_ref[:rows, :], [(kv_behind, 0, rows), (kv_ref, 0, 4 * rows)], keep)
    ring_ref[...] = (own_ref[...] + jnp.dot(mixed, w_out[...], preferred_element_type=F32)).astype(BF16)


def attend_near_kernel(
    sums_ref, near_ref, query_ref, kv_ref, far_ref, gain_ref, w_qkv, w_out, after, ring_ref, kv_far, mixed
):
    del after
    rows, depth = near_ref.shape[0] // 2, near_ref.shape[1]
    kv_far[...] = jnp.dot(
        normal(far_ref[...], gain_ref[...]), w_qkv[:, depth:], preferred_element_type=F32
    ).astype(BF16)
    windows = [
        [(kv_ref, 0, 4 * rows), (kv_far, 0, rows)],
        [(kv_ref, rows, 3 * rows), (kv_far, 0, 2 * rows)],
    ]
    for n, window in enumerate(windows):
        keep = kept_lanes(rows, sums_ref[2 * rows:, 0:HD].astype(F32)[0:1, n:n + 1])
        mixed[n * rows:(n + 1) * rows, :] = attention(query_ref[(n + 1) * rows:(n + 2) * rows, :], window, keep)
    added = jnp.dot(mixed[...], w_out[...], preferred_element_type=F32)
    ring_ref[...] = (near_ref[...].astype(F32) + added).astype(BF16)


def attend_own(base, own, query, kv, behind, gain, w_qkv, w_out):
    rows, depth = own.shape
    return pl.pallas_call(
        attend_own_kernel,
        out_shape=kept((rows, depth)),
        in_specs=[VMEM] * 8,
        out_specs=VMEM,
        scratch_shapes=[pltpu.VMEM((rows, 2 * depth), BF16)],
        compiler_params=pltpu.CompilerParams(vmem_limit_bytes=12 << 20),
        cost_estimate=pl.CostEstimate(
            flops=20 * rows * depth * depth, bytes_accessed=2 * rows * depth, transcendentals=0
        ),
        name="attend_own",
    )(base, own, query, kv, behind, gain, w_qkv, w_out)


def attend_near(sums, near, query, kv, far, gain, w_qkv, w_out, after):
    rows, depth = near.shape[0] // 2, near.shape[1]
    return pl.pallas_call(
        attend_near_kernel,
        out_shape=kept((2 * rows, depth)),
        in_specs=[VMEM] * 8 + [ANY],
        out_specs=VMEM,
        scratch_shapes=[pltpu.VMEM((2 * rows, 2 * depth), BF16), pltpu.VMEM((2 * rows, depth), BF16)],
        compiler_params=pltpu.CompilerParams(vmem_limit_bytes=12 << 20),
        cost_estimate=pl.CostEstimate(
            flops=40 * rows * depth * depth, bytes_accessed=2 * rows * depth, transcendentals=0
        ),
        name="attend_near",
    )(sums, near, query, kv, far, gain, w_qkv, w_out, after)


def halved(rows, first):
    return jnp.dot(rows * BF16(0.5), first, preferred_element_type=F32)


def grid_hidden_kernel(enc_ref, first, second_hbm, after, out_ref, second, sem):
    del after
    copy = pltpu.make_async_copy(second_hbm, second, sem)
    copy.start()
    tile, part = tiles_of(*out_ref.shape)
    for j in range(out_ref.shape[1] // part):
        cols = slice(j * part, (j + 1) * part)
        for r in range(out_ref.shape[0] // tile):
            cut = slice(r * tile, (r + 1) * tile)
            out_ref[cut, cols] = halved(enc_ref[cut, :], first[:, cols]).astype(BF16)
    copy.wait()


def grid_hidden(encoded, first, second, after):
    cells, depth = encoded.shape
    hidden = first.shape[1]
    return pl.pallas_call(
        grid_hidden_kernel,
        out_shape=(kept((cells, hidden)), kept(second.shape)),
        in_specs=[VMEM] * 2 + [ANY] * 2,
        out_specs=(VMEM, VMEM),
        scratch_shapes=[pltpu.SemaphoreType.DMA],
        compiler_params=pltpu.CompilerParams(vmem_limit_bytes=12 << 20),
        cost_estimate=pl.CostEstimate(
            flops=2 * cells * depth * hidden, bytes_accessed=2 * (cells + hidden) * depth, transcendentals=0
        ),
        name="grid_hidden",
    )(encoded, first, *in_hbm(second), after)


def mesh_hidden_kernel(back_own, ring_own, ring_near, first, out_ref):
    rows = ring_own.shape[0]
    out_ref[rows:REACH * rows, :] = halved(back_own[...], first[...]).astype(BF16)
    out_ref[REACH * rows:(REACH + 1) * rows, :] = halved(ring_own[...], first[...]).astype(BF16)
    out_ref[(REACH + 1) * rows:, :] = halved(ring_near[...], first[...]).astype(BF16)


def mesh_hidden(back_own, ring_own, ring_near, first):
    rows, depth = ring_own.shape
    return pl.pallas_call(
        mesh_hidden_kernel,
        out_shape=kept(((2 * REACH + 1) * rows, first.shape[1])),
        in_specs=[VMEM] * 4,
        out_specs=VMEM,
        compiler_params=pltpu.CompilerParams(vmem_limit_bytes=12 << 20),
        cost_estimate=pl.CostEstimate(
            flops=8 * rows * depth * first.shape[1], bytes_accessed=2 * rows * depth, transcendentals=0
        ),
        name="mesh_hidden",
    )(back_own, ring_own, ring_near, first)


def decode_kernel(
    owner_hbm, weight_ref, ring_own, ring_near, back_own, back_near, grid_ref, mesh_in, enc_ref, first, second,
    out_hbm, mesh_hbm, mesh_ref,
    owner, x_ref, act, ring, io_sems,
):
    del mesh_in
    rows = ring_own.shape[0]
    tile, part = tiles_of(x_ref.shape[0], first.shape[1])
    tile = min(tile, 256)
    tiles, parts = x_ref.shape[0] // tile, first.shape[1] // part
    stores = [pltpu.make_async_copy(ring_own, mesh_hbm, io_sems.at[tiles])]
    index = pltpu.make_async_copy(owner_hbm, owner, io_sems.at[tiles + 1])
    index.start()
    stores[0].start()
    mine, count = lax.axis_index(AXES), lax.axis_size(AXES)
    outward = outward_of()
    mesh_ref[:rows, :] = halved(back_near[...], first[...]).astype(BF16)
    ring[:rows, :] = back_near[...]
    ring[rows:2 * rows, :] = back_own[...]
    ring[2 * rows:3 * rows, :] = ring_own[...]
    ring[3 * rows:, :] = ring_near[...]
    columns = jnp.transpose(weight_ref[...])
    index.wait()
    for r in range(tiles):
        cut = slice(r * tile, (r + 1) * tile)
        for b in range(r * tile // rows, (r + 1) * tile // rows):
            slot = outward * offset_of(owner[b], mine, count) + REACH
            lines = pl.ds(pl.multiple_of(slot * rows, rows), rows)
            block = slice(b * rows, (b + 1) * rows)
            weight = columns[:, b:b + 1]
            narrow = weight.astype(BF16)
            for j in range(parts):
                cols = slice(j * part, (j + 1) * part)
                half = grid_ref[block, cols] + narrow * mesh_ref[lines, cols]
                act[block, cols] = half * jnp.tanh(half) + half
            x_ref[block, :] = (enc_ref[block, :].astype(F32) + weight * ring[lines, :].astype(F32)).astype(BF16)
        out = jnp.dot(act[cut, :], second[...], preferred_element_type=F32)
        x_ref[cut, :] = (x_ref[cut, :].astype(F32) + out).astype(BF16)
        copy = pltpu.make_async_copy(x_ref.at[pl.ds(r * tile, tile)], out_hbm.at[pl.ds(r * tile, tile)], io_sems.at[r])
        copy.start()
        stores.append(copy)
    for copy in stores:
        copy.wait()


def decode(owner, weights, ring_own, ring_near, back_own, back_near, grid_part, mesh_part, encoded, first, second):
    cells, depth = encoded.shape
    hidden = first.shape[1]
    rows = ring_own.shape[0]
    return pl.pallas_call(
        decode_kernel,
        out_shape=(
            jax.ShapeDtypeStruct((cells, depth), BF16),
            jax.ShapeDtypeStruct((rows, depth), BF16),
            kept(mesh_part.shape),
        ),
        in_specs=[ANY] + [VMEM] * 10,
        out_specs=(ANY, ANY, VMEM),
        input_output_aliases={7: 2},
        scratch_shapes=[
            pltpu.SMEM(owner.shape, jnp.int32),
            pltpu.VMEM((cells, depth), BF16),
            pltpu.VMEM((cells, hidden), BF16),
            pltpu.VMEM(((2 * REACH + 1) * rows, depth), BF16),
            pltpu.SemaphoreType.DMA((cells // min(cells, 256) + 2,)),
        ],
        compiler_params=pltpu.CompilerParams(vmem_limit_bytes=16 << 20),
        cost_estimate=pl.CostEstimate(
            flops=2 * cells * depth * hidden, bytes_accessed=4 * (cells + hidden) * depth, transcendentals=cells * hidden
        ),
        name="decode",
    )(*in_hbm(owner), weights, ring_own, ring_near, back_own, back_near, grid_part, mesh_part, encoded, first, second)[:2]


def on_device(
    grid, g2m_owner, g2m_weight, m2g_owner, m2g_weight, mesh_feat, neighbours,
    enc_w1, enc_w2, attn_gain, w_qkv, w_out, dec_w1, dec_w2,
):
    rows = mesh_feat.shape[0]
    nblocks = g2m_owner.shape[0]
    encoded, message, base, local, first = encode(
        g2m_owner, neighbours, g2m_weight.reshape(nblocks, rows), mesh_feat, grid, enc_w1, enc_w2, dec_w1
    )
    outgoing = outgoing_sums(base, swapped(message))
    sums = from_outward(outgoing, 1)
    grid_part, second = grid_hidden(encoded, first, dec_w2, outgoing)
    share, message = chip_share(local, sums, grid_part)
    own, pair, message = chip_states(share, swapped(message))
    near = from_outward(message, 1)
    far = from_outward(message, 2)
    behind = swapped(near[:rows])
    query, kv = project(pair, near, attn_gain, w_qkv[0])
    ring_own = attend_own(base, own, query, kv, behind, attn_gain, w_qkv[0], w_out[0])
    ring_near = attend_near(sums, near, query, kv, far, attn_gain, w_qkv[0], w_out[0], ring_own)
    back_own = swapped(ring_own)
    back_near = swapped(ring_near[:rows])
    mesh_part = mesh_hidden(back_own, ring_own, ring_near, first)
    return decode(
        m2g_owner, m2g_weight.reshape(nblocks, rows), ring_own, ring_near, back_own, back_near,
        grid_part, mesh_part, encoded, first, second,
    )


def solution(mesh):
    split = P(AXES, None)
    flat = P(AXES)
    in_specs = (split, flat, flat, flat, flat, split, split) + (P(),) * 7
    return jax.shard_map(
        on_device, mesh=mesh, in_specs=in_specs, out_specs=(split, split), check_vma=False
    )
```

```python
import functools

import jax
import jax.numpy as jnp
from jax import lax
from jax.experimental import pallas as pl
from jax.experimental.pallas import tpu as pltpu
from jax.sharding import PartitionSpec as P

HD = 128
REACH = 2
LOG2E = 1.4426950408889634
EXTRA = 16
AXES = ("tile", "sub")
BF16 = jnp.bfloat16
F32 = jnp.float32
VMEM = pl.BlockSpec(memory_space=pltpu.VMEM)
SMEM = pl.BlockSpec(memory_space=pltpu.SMEM)
ANY = pl.BlockSpec(memory_space=pl.ANY)


def swapped(block):
    count = lax.axis_size(AXES)
    return lax.ppermute(block, AXES, [(i, i ^ 1) for i in range(count)])


def from_outward(block, chips):
    count = lax.axis_size(AXES)
    route = []
    for i in range(count):
        step = 2 * chips - 1
        route.append((i, (i + step if i % 2 else i - step) % count))
    return lax.ppermute(block, AXES, route)


def tiles_of(rows, columns):
    return min(rows, 1024), min(columns, 1024)


def outward_of():
    return 2 * lax.axis_index("sub") - 1


def offset_of(owner, mine, count):
    return lax.rem(owner - mine + REACH + count, count) - REACH


def kept(shape, dtype=BF16):
    return pltpu.VMEM(shape, dtype)


def in_hbm(*arrays):
    return [pltpu.with_memory_space_constraint(a, pltpu.HBM) for a in arrays]


def hidden_layer(x_ref, first, act, tile, part, arrive, before):
    for j in range(first.shape[1] // part):
        before(j)
        cols = slice(j * part, (j + 1) * part)
        for r in range(x_ref.shape[0] // tile):
            if j == 0:
                arrive(r)
            cut = slice(r * tile, (r + 1) * tile)
            half = jnp.dot(x_ref[cut, :] * BF16(0.5), first[:, cols], preferred_element_type=F32)
            act[cut, cols] = (half * jnp.tanh(half) + half).astype(BF16)


def encode_kernel(
    owner_hbm, listed_hbm, weight_hbm, feat_hbm, x_hbm, first_hbm, second_hbm, next_hbm,
    enc_ref, msg_ref, base_ref, loc_ref, next_ref,
    owner, listed, weight_ref, feat_ref, first, second, act, total, sems, io_sems,
):
    rows, depth = feat_ref.shape
    tile, part = tiles_of(enc_ref.shape[0], first.shape[1])
    tiles, parts = enc_ref.shape[0] // tile, first.shape[1] // part
    loads = [
        pltpu.make_async_copy(x_hbm.at[pl.ds(r * tile, tile)], enc_ref.at[pl.ds(r * tile, tile)], io_sems.at[r])
        for r in range(tiles)
    ]
    ones, twos = [], []
    for j in range(parts):
        cut = pl.ds(j * part, part)
        ones.append(pltpu.make_async_copy(first_hbm.at[:, cut], first.at[:, cut], sems.at[0, j]))
        twos.append(pltpu.make_async_copy(second_hbm.at[cut], second.at[cut], sems.at[1, j]))
    small = [
        pltpu.make_async_copy(weight_hbm, weight_ref, io_sems.at[tiles]),
        pltpu.make_async_copy(feat_hbm, feat_ref, io_sems.at[tiles + 1]),
        pltpu.make_async_copy(owner_hbm, owner, io_sems.at[tiles + 2]),
        pltpu.make_async_copy(listed_hbm, listed, io_sems.at[tiles + 3]),
    ]
    later = pltpu.make_async_copy(next_hbm, next_ref, io_sems.at[tiles + 4])
    for copy in loads + ones + twos + small + [later]:
        copy.start()

    def arrive(r):
        if r == 0:
            for copy in loads:
                copy.wait()

    mine, count = lax.axis_index(AXES), lax.axis_size(AXES)
    outward = outward_of()
    total[...] = jnp.zeros_like(total)

    def before(j):
        due = ones[:1] if j == 0 else []
        if j == min(1, parts - 1):
            due = due + ones[1:] + twos + small
        for copy in due:
            copy.wait()

    hidden_layer(enc_ref, first, act, tile, part, arrive, before)
    columns = jnp.transpose(weight_ref[...])
    tile = min(tile, 256)
    for r in range(enc_ref.shape[0] // tile):
        cut = slice(r * tile, (r + 1) * tile)
        out = enc_ref[cut, :].astype(F32) + jnp.dot(act[cut, :], second[...], preferred_element_type=F32)
        enc_ref[cut, :] = out.astype(BF16)
        for b in range(r * tile // rows, (r + 1) * tile // rows):
            slot = outward * offset_of(owner[b], mine, count) + REACH
            total[slot] += columns[:, b:b + 1] * out[b * rows - r * tile:(b + 1) * rows - r * tile, :]
    absent = sum(-offset_of(listed[0, n], mine, count) for n in range(listed.shape[1])).astype(F32)
    spot = lax.broadcasted_iota(jnp.int32, (EXTRA, depth), 1)
    msg_ref[:rows, :] = total[0].astype(BF16)
    msg_ref[rows:, :] = jnp.where(spot == 1, absent, 0.0).astype(BF16)
    base_ref[:rows, :] = total[4].astype(BF16)
    base_ref[rows:2 * rows, :] = total[3].astype(BF16)
    base_ref[2 * rows:, :] = jnp.where(spot == 0, absent, 0.0).astype(BF16)
    loc_ref[:rows, :] = total[1]
    loc_ref[rows:, :] = total[2] + feat_ref[...].astype(F32)
    later.wait()


def encode(owner, listed, weights, feat, grid, first, second, following):
    cells, depth = grid.shape
    hidden = first.shape[1]
    rows = feat.shape[0]
    tile, part = tiles_of(cells, hidden)
    return pl.pallas_call(
        encode_kernel,
        out_shape=(
            kept((cells, depth)),
            kept((rows + EXTRA, depth)),
            kept((2 * rows + EXTRA, depth)),
            kept((2 * rows, depth), F32),
            kept(following.shape),
        ),
        in_specs=[ANY] * 8,
        out_specs=(VMEM,) * 5,
        scratch_shapes=[
            pltpu.SMEM(owner.shape, jnp.int32),
            pltpu.SMEM(listed.shape, jnp.int32),
            pltpu.VMEM(weights.shape, F32),
            pltpu.VMEM(feat.shape, BF16),
            pltpu.VMEM((depth, hidden), BF16),
            pltpu.VMEM((hidden, depth), BF16),
            pltpu.VMEM((cells, hidden), BF16),
            pltpu.VMEM((2 * REACH + 1, rows, depth), F32),
            pltpu.SemaphoreType.DMA((2, hidden // part)),
            pltpu.SemaphoreType.DMA((cells // tile + 5,)),
        ],
        compiler_params=pltpu.CompilerParams(vmem_limit_bytes=24 << 20),
        cost_estimate=pl.CostEstimate(
            flops=4 * cells * depth * hidden, bytes_accessed=4 * (cells + hidden) * depth, transcendentals=cells * hidden
        ),
        name="encode",
    )(*in_hbm(owner, listed, weights, feat, grid, first, second, following))


def outgoing_kernel(base_ref, arrived_ref, out_ref):
    rows = arrived_ref.shape[0] - EXTRA
    out_ref[:rows, :] = base_ref[:rows, :]
    out_ref[rows:, :] = (base_ref[rows:, :].astype(F32) + arrived_ref[...].astype(F32)).astype(BF16)


def outgoing_sums(base, arrived):
    return pl.pallas_call(
        outgoing_kernel, out_shape=kept(base.shape), in_specs=[VMEM] * 2, out_specs=VMEM,
        compiler_params=pltpu.CompilerParams(vmem_limit_bytes=4 << 20), name="outgoing_sums"
    )(base, arrived)


def share_kernel(loc_ref, arrived_ref, after, share_ref, msg_ref):
    del after
    rows = loc_ref.shape[0] // 2
    share_ref[...] = loc_ref[...] + arrived_ref[:2 * rows, :].astype(F32)
    msg_ref[:rows, :] = share_ref[rows:, :].astype(BF16)
    msg_ref[rows:, :] = share_ref[:rows, :].astype(BF16)


def chip_share(local, arrived, after):
    return pl.pallas_call(
        share_kernel,
        out_shape=(kept(local.shape, F32), kept(local.shape)),
        in_specs=[VMEM] * 2 + [ANY],
        out_specs=(VMEM,) * 2,
        compiler_params=pltpu.CompilerParams(vmem_limit_bytes=4 << 20),
        name="chip_share",
    )(local, arrived, after)


def state_kernel(share_ref, other_ref, own_ref, pair_ref, msg_ref):
    rows = own_ref.shape[0]
    own_ref[...] = share_ref[rows:, :] + other_ref[rows:, :].astype(F32)
    pair_ref[:rows, :] = (share_ref[:rows, :] + other_ref[:rows, :].astype(F32)).astype(BF16)
    pair_ref[rows:, :] = own_ref[...].astype(BF16)
    msg_ref[:rows, :] = pair_ref[rows:, :]
    msg_ref[rows:, :] = pair_ref[:rows, :]


def chip_states(share, other):
    rows, depth = share.shape[0] // 2, share.shape[1]
    return pl.pallas_call(
        state_kernel,
        out_shape=(kept((rows, depth), F32), kept(share.shape), kept(share.shape)),
        in_specs=[VMEM] * 2,
        out_specs=(VMEM,) * 3,
        compiler_params=pltpu.CompilerParams(vmem_limit_bytes=4 << 20),
        name="chip_states",
    )(share, other)


def normal(block, gain):
    state = block.astype(F32)
    scale = lax.rsqrt(jnp.mean(state * state, axis=-1, keepdims=True) + 1e-6)
    return (state * scale * gain).astype(BF16)


def project_kernel(pair_ref, near_ref, gain_ref, w_qkv, query_ref, kv_ref, normed):
    rows, depth = pair_ref.shape[0] // 2, pair_ref.shape[1]
    gain = gain_ref[...]
    normed[:2 * rows, :] = normal(pair_ref[...], gain)
    normed[2 * rows:, :] = normal(near_ref[...], gain)
    kv_ref[...] = jnp.dot(normed[...], w_qkv[:, depth:], preferred_element_type=F32).astype(BF16)
    query_ref[...] = jnp.dot(normed[rows:, :], w_qkv[:, :depth], preferred_element_type=F32).astype(BF16)


def project(pair, near, gain, w_qkv):
    rows, depth = pair.shape[0] // 2, pair.shape[1]
    return pl.pallas_call(
        project_kernel,
        out_shape=(kept((3 * rows, depth)), kept((4 * rows, 2 * depth))),
        in_specs=[VMEM] * 4,
        out_specs=(VMEM,) * 2,
        scratch_shapes=[pltpu.VMEM((4 * rows, depth), BF16)],
        compiler_params=pltpu.CompilerParams(vmem_limit_bytes=8 << 20),
        cost_estimate=pl.CostEstimate(
            flops=22 * rows * depth * depth, bytes_accessed=2 * rows * depth, transcendentals=0
        ),
        name="project",
    )(pair, near, gain, w_qkv)


def attention(query, window, keep):
    depth = query.shape[1]
    every = [slice(h * HD, (h + 1) * HD) for h in range(depth // HD)]
    scores = [
        jnp.concatenate([
            lax.dot_general(
                query[:, cols], ref[first:first + size, cols], (((1,), (1,)), ((), ())), preferred_element_type=F32
            )
            for ref, first, size in window
        ], axis=1)
        for cols in every
    ]
    scores = [jnp.where(keep, score, -jnp.inf) for score in scores]
    below = [(score - jnp.max(score, axis=-1, keepdims=True)) * (HD ** -0.5 * LOG2E) for score in scores]
    grown = [jnp.exp2(score.astype(BF16)) for score in below]
    heads = []
    for h, cols in enumerate(every):
        start, taken = 0, None
        for ref, first, size in window:
            value = ref[first:first + size, depth + cols.start:depth + cols.stop]
            value = jnp.concatenate([value, jnp.ones((size, HD), BF16)], axis=1)
            term = jnp.dot(grown[h][:, start:start + size], value, preferred_element_type=F32)
            taken = term if taken is None else taken + term
            start += size
        heads.append((taken[:, :HD] / taken[:, HD:]).astype(BF16))
    return jnp.concatenate(heads, axis=1)


def kept_lanes(rows, absent):
    block = (lax.broadcasted_iota(jnp.int32, (rows, (2 * REACH + 1) * rows), 1) // rows).astype(F32)
    return block != outward_of().astype(F32) * absent + REACH


def attend_own_kernel(base_ref, own_ref, query_ref, kv_ref, behind_ref, gain_ref, w_qkv, w_out, ring_ref, kv_behind):
    rows, depth = own_ref.shape
    kv_behind[...] = jnp.dot(
        normal(behind_ref[...], gain_ref[...]), w_qkv[:, depth:], preferred_element_type=F32
    ).astype(BF16)
    keep = kept_lanes(rows, base_ref[2 * rows:, 0:HD].astype(F32)[0:1, 0:1])
    mixed = attention(query_ref[:rows, :], [(kv_behind, 0, rows), (kv_ref, 0, 4 * rows)], keep)
    ring_ref[...] = (own_ref[...] + jnp.dot(mixed, w_out[...], preferred_element_type=F32)).astype(BF16)


def attend_near_kernel(
    sums_ref, near_ref, query_ref, kv_ref, far_ref, gain_ref, w_qkv, w_out, after, ring_ref, kv_far, mixed
):
    del after
    rows, depth = near_ref.shape[0] // 2, near_ref.shape[1]
    kv_far[...] = jnp.dot(
        normal(far_ref[...], gain_ref[...]), w_qkv[:, depth:], preferred_element_type=F32
    ).astype(BF16)
    windows = [
        [(kv_ref, 0, 4 * rows), (kv_far, 0, rows)],
        [(kv_ref, rows, 3 * rows), (kv_far, 0, 2 * rows)],
    ]
    for n, window in enumerate(windows):
        keep = kept_lanes(rows, sums_ref[2 * rows:, 0:HD].astype(F32)[0:1, n:n + 1])
        mixed[n * rows:(n + 1) * rows, :] = attention(query_ref[(n + 1) * rows:(n + 2) * rows, :], window, keep)
    added = jnp.dot(mixed[...], w_out[...], preferred_element_type=F32)
    ring_ref[...] = (near_ref[...].astype(F32) + added).astype(BF16)


def attend_own(base, own, query, kv, behind, gain, w_qkv, w_out):
    rows, depth = own.shape
    return pl.pallas_call(
        attend_own_kernel,
        out_shape=kept((rows, depth)),
        in_specs=[VMEM] * 8,
        out_specs=VMEM,
        scratch_shapes=[pltpu.VMEM((rows, 2 * depth), BF16)],
        compiler_params=pltpu.CompilerParams(vmem_limit_bytes=12 << 20),
        cost_estimate=pl.CostEstimate(
            flops=20 * rows * depth * depth, bytes_accessed=2 * rows * depth, transcendentals=0
        ),
        name="attend_own",
    )(base, own, query, kv, behind, gain, w_qkv, w_out)


def attend_near(sums, near, query, kv, far, gain, w_qkv, w_out, after):
    rows, depth = near.shape[0] // 2, near.shape[1]
    return pl.pallas_call(
        attend_near_kernel,
        out_shape=kept((2 * rows, depth)),
        in_specs=[VMEM] * 8 + [ANY],
        out_specs=VMEM,
        scratch_shapes=[pltpu.VMEM((2 * rows, 2 * depth), BF16), pltpu.VMEM((2 * rows, depth), BF16)],
        compiler_params=pltpu.CompilerParams(vmem_limit_bytes=12 << 20),
        cost_estimate=pl.CostEstimate(
            flops=40 * rows * depth * depth, bytes_accessed=2 * rows * depth, transcendentals=0
        ),
        name="attend_near",
    )(sums, near, query, kv, far, gain, w_qkv, w_out, after)


def halved(rows, first):
    return jnp.dot(rows * BF16(0.5), first, preferred_element_type=F32)


def grid_hidden_kernel(enc_ref, first, second_hbm, after, out_ref, second, sem):
    del after
    copy = pltpu.make_async_copy(second_hbm, second, sem)
    copy.start()
    tile, part = tiles_of(*out_ref.shape)
    for j in range(out_ref.shape[1] // part):
        cols = slice(j * part, (j + 1) * part)
        for r in range(out_ref.shape[0] // tile):
            cut = slice(r * tile, (r + 1) * tile)
            out_ref[cut, cols] = halved(enc_ref[cut, :], first[:, cols]).astype(BF16)
    copy.wait()


def grid_hidden(encoded, first, second, after):
    cells, depth = encoded.shape
    hidden = first.shape[1]
    return pl.pallas_call(
        grid_hidden_kernel,
        out_shape=(kept((cells, hidden)), kept(second.shape)),
        in_specs=[VMEM] * 2 + [ANY] * 2,
        out_specs=(VMEM, VMEM),
        scratch_shapes=[pltpu.SemaphoreType.DMA],
        compiler_params=pltpu.CompilerParams(vmem_limit_bytes=12 << 20),
        cost_estimate=pl.CostEstimate(
            flops=2 * cells * depth * hidden, bytes_accessed=2 * (cells + hidden) * depth, transcendentals=0
        ),
        name="grid_hidden",
    )(encoded, first, *in_hbm(second), after)


def mesh_hidden_kernel(back_own, ring_own, ring_near, first, out_ref):
    rows = ring_own.shape[0]
    out_ref[rows:REACH * rows, :] = halved(back_own[...], first[...]).astype(BF16)
    out_ref[REACH * rows:(REACH + 1) * rows, :] = halved(ring_own[...], first[...]).astype(BF16)
    out_ref[(REACH + 1) * rows:, :] = halved(ring_near[...], first[...]).astype(BF16)


def mesh_hidden(back_own, ring_own, ring_near, first):
    rows, depth = ring_own.shape
    return pl.pallas_call(
        mesh_hidden_kernel,
        out_shape=kept(((2 * REACH + 1) * rows, first.shape[1])),
        in_specs=[VMEM] * 4,
        out_specs=VMEM,
        compiler_params=pltpu.CompilerParams(vmem_limit_bytes=12 << 20),
        cost_estimate=pl.CostEstimate(
            flops=8 * rows * depth * first.shape[1], bytes_accessed=2 * rows * depth, transcendentals=0
        ),
        name="mesh_hidden",
    )(back_own, ring_own, ring_near, first)


def decode_kernel(
    owner_hbm, weight_ref, ring_own, ring_near, back_own, back_near, grid_ref, mesh_in, enc_ref, first, second,
    out_hbm, mesh_hbm, mesh_ref,
    owner, x_ref, act, ring, io_sems,
):
    del mesh_in
    rows = ring_own.shape[0]
    tile, part = tiles_of(x_ref.shape[0], first.shape[1])
    tile = min(tile, 256)
    tiles, parts = x_ref.shape[0] // tile, first.shape[1] // part
    stores = [pltpu.make_async_copy(ring_own, mesh_hbm, io_sems.at[x_ref.shape[0] // rows])]
    index = pltpu.make_async_copy(owner_hbm, owner, io_sems.at[x_ref.shape[0] // rows + 1])
    index.start()
    stores[0].start()
    mine, count = lax.axis_index(AXES), lax.axis_size(AXES)
    outward = outward_of()
    mesh_ref[:rows, :] = halved(back_near[...], first[...]).astype(BF16)
    ring[:rows, :] = back_near[...]
    ring[rows:2 * rows, :] = back_own[...]
    ring[2 * rows:3 * rows, :] = ring_own[...]
    ring[3 * rows:, :] = ring_near[...]
    columns = jnp.transpose(weight_ref[...])
    index.wait()
    for r in range(tiles):
        cut = slice(r * tile, (r + 1) * tile)
        reads = []
        for b in range(r * tile // rows, (r + 1) * tile // rows):
            slot = outward * offset_of(owner[b], mine, count) + REACH
            lines = pl.ds(pl.multiple_of(slot * rows, rows), rows)
            block = slice(b * rows, (b + 1) * rows)
            weight = columns[:, b:b + 1]
            narrow = weight.astype(BF16)
            for j in range(parts):
                cols = slice(j * part, (j + 1) * part)
                half = grid_ref[block, cols] + narrow * mesh_ref[lines, cols]
                act[block, cols] = half * jnp.tanh(half) + half
            reads.append((block, weight, lines))
        out = jnp.dot(act[cut, :], second[...], preferred_element_type=F32)
        for n, (block, weight, lines) in enumerate(reads):
            rest = enc_ref[block, :].astype(F32) + weight * ring[lines, :].astype(F32)
            x_ref[block, :] = (rest + out[n * rows:(n + 1) * rows, :]).astype(BF16)
            copy = pltpu.make_async_copy(x_ref.at[block], out_hbm.at[block], io_sems.at[r * tile // rows + n])
            copy.start()
            stores.append(copy)
    for copy in stores:
        copy.wait()


def decode(owner, weights, ring_own, ring_near, back_own, back_near, grid_part, mesh_part, encoded, first, second):
    cells, depth = encoded.shape
    hidden = first.shape[1]
    rows = ring_own.shape[0]
    return pl.pallas_call(
        decode_kernel,
        out_shape=(
            jax.ShapeDtypeStruct((cells, depth), BF16),
            jax.ShapeDtypeStruct((rows, depth), BF16),
            kept(mesh_part.shape),
        ),
        in_specs=[ANY] + [VMEM] * 10,
        out_specs=(ANY, ANY, VMEM),
        input_output_aliases={7: 2},
        scratch_shapes=[
            pltpu.SMEM(owner.shape, jnp.int32),
            pltpu.VMEM((cells, depth), BF16),
            pltpu.VMEM((cells, hidden), BF16),
            pltpu.VMEM(((2 * REACH + 1) * rows, depth), BF16),
            pltpu.SemaphoreType.DMA((cells // rows + 2,)),
        ],
        compiler_params=pltpu.CompilerParams(vmem_limit_bytes=16 << 20),
        cost_estimate=pl.CostEstimate(
            flops=2 * cells * depth * hidden, bytes_accessed=4 * (cells + hidden) * depth, transcendentals=cells * hidden
        ),
        name="decode",
    )(*in_hbm(owner), weights, ring_own, ring_near, back_own, back_near, grid_part, mesh_part, encoded, first, second)[:2]


def on_device(
    grid, g2m_owner, g2m_weight, m2g_owner, m2g_weight, mesh_feat, neighbours,
    enc_w1, enc_w2, attn_gain, w_qkv, w_out, dec_w1, dec_w2,
):
    rows = mesh_feat.shape[0]
    nblocks = g2m_owner.shape[0]
    encoded, message, base, local, first = encode(
        g2m_owner, neighbours, g2m_weight.reshape(nblocks, rows), mesh_feat, grid, enc_w1, enc_w2, dec_w1
    )
    outgoing = outgoing_sums(base, swapped(message))
    sums = from_outward(outgoing, 1)
    grid_part, second = grid_hidden(encoded, first, dec_w2, outgoing)
    share, message = chip_share(local, sums, grid_part)
    own, pair, message = chip_states(share, swapped(message))
    near = from_outward(message, 1)
    far = from_outward(message, 2)
    behind = swapped(near[:rows])
    query, kv = project(pair, near, attn_gain, w_qkv[0])
    ring_own = attend_own(base, own, query, kv, behind, attn_gain, w_qkv[0], w_out[0])
    ring_near = attend_near(sums, near, query, kv, far, attn_gain, w_qkv[0], w_out[0], ring_own)
    back_own = swapped(ring_own)
    back_near = swapped(ring_near[:rows])
    mesh_part = mesh_hidden(back_own, ring_own, ring_near, first)
    return decode(
        m2g_owner, m2g_weight.reshape(nblocks, rows), ring_own, ring_near, back_own, back_near,
        grid_part, mesh_part, encoded, first, second,
    )


def solution(mesh):
    split = P(AXES, None)
    flat = P(AXES)
    in_specs = (split, flat, flat, flat, flat, split, split) + (P(),) * 7
    return jax.shard_map(
        on_device, mesh=mesh, in_specs=in_specs, out_specs=(split, split), check_vma=False
    )
```

```python
import functools

import jax
import jax.numpy as jnp
from jax import lax
from jax.experimental import pallas as pl
from jax.experimental.pallas import tpu as pltpu
from jax.sharding import PartitionSpec as P

HD = 128
REACH = 2
LOG2E = 1.4426950408889634
EXTRA = 16
LANES = 128
AXES = ("tile", "sub")
BF16 = jnp.bfloat16
F32 = jnp.float32
VMEM = pl.BlockSpec(memory_space=pltpu.VMEM)
SMEM = pl.BlockSpec(memory_space=pltpu.SMEM)
ANY = pl.BlockSpec(memory_space=pl.ANY)


def swapped(block):
    count = lax.axis_size(AXES)
    return lax.ppermute(block, AXES, [(i, i ^ 1) for i in range(count)])


def from_outward(block, chips):
    count = lax.axis_size(AXES)
    route = []
    for i in range(count):
        step = 2 * chips - 1
        route.append((i, (i + step if i % 2 else i - step) % count))
    return lax.ppermute(block, AXES, route)


def tiles_of(rows, columns):
    return min(rows, 1024), min(columns, 1024)


def outward_of():
    return 2 * lax.axis_index("sub") - 1


def offset_of(owner, mine, count):
    return lax.rem(owner - mine + REACH + count, count) - REACH


def kept(shape, dtype=BF16):
    return pltpu.VMEM(shape, dtype)


def in_hbm(*arrays):
    return [pltpu.with_memory_space_constraint(a, pltpu.HBM) for a in arrays]


def strips(depth):
    return [slice(k, k + LANES) for k in range(0, depth, LANES)]


def spread(ref, first, block):
    rows = block.shape[0]
    for k, cols in enumerate(strips(block.shape[1])):
        ref[first + k * rows:first + (k + 1) * rows, :] = block[:, cols].astype(BF16)


def hidden_layer(x_ref, first, act, tile, part, arrive, before):
    for j in range(first.shape[1] // part):
        before(j)
        cols = slice(j * part, (j + 1) * part)
        for r in range(x_ref.shape[0] // tile):
            if j == 0:
                arrive(r)
            cut = slice(r * tile, (r + 1) * tile)
            half = jnp.dot(x_ref[cut, :] * BF16(0.5), first[:, cols], preferred_element_type=F32)
            act[cut, cols] = (half * jnp.tanh(half) + half).astype(BF16)


def encode_kernel(
    owner_hbm, listed_hbm, weight_hbm, feat_hbm, x_hbm, first_hbm, second_hbm, next_hbm,
    enc_ref, msg_ref, base_ref, loc_ref, next_ref,
    owner, listed, weight_ref, feat_ref, first, second, act, total, sems, io_sems,
):
    rows, depth = feat_ref.shape
    tile, part = tiles_of(enc_ref.shape[0], first.shape[1])
    tiles, parts = enc_ref.shape[0] // tile, first.shape[1] // part
    loads = [
        pltpu.make_async_copy(x_hbm.at[pl.ds(r * tile, tile)], enc_ref.at[pl.ds(r * tile, tile)], io_sems.at[r])
        for r in range(tiles)
    ]
    ones, twos = [], []
    for j in range(parts):
        cut = pl.ds(j * part, part)
        ones.append(pltpu.make_async_copy(first_hbm.at[:, cut], first.at[:, cut], sems.at[0, j]))
        twos.append(pltpu.make_async_copy(second_hbm.at[cut], second.at[cut], sems.at[1, j]))
    small = [
        pltpu.make_async_copy(weight_hbm, weight_ref, io_sems.at[tiles]),
        pltpu.make_async_copy(feat_hbm, feat_ref, io_sems.at[tiles + 1]),
        pltpu.make_async_copy(owner_hbm, owner, io_sems.at[tiles + 2]),
        pltpu.make_async_copy(listed_hbm, listed, io_sems.at[tiles + 3]),
    ]
    later = pltpu.make_async_copy(next_hbm, next_ref, io_sems.at[tiles + 4])
    for copy in loads + ones + twos + small + [later]:
        copy.start()

    def arrive(r):
        if r == 0:
            for copy in loads:
                copy.wait()

    mine, count = lax.axis_index(AXES), lax.axis_size(AXES)
    outward = outward_of()
    total[...] = jnp.zeros_like(total)

    def before(j):
        due = ones[:1] if j == 0 else []
        if j == min(1, parts - 1):
            due = due + ones[1:] + twos + small
        for copy in due:
            copy.wait()

    hidden_layer(enc_ref, first, act, tile, part, arrive, before)
    columns = jnp.transpose(weight_ref[...])
    tile = min(tile, 256)
    for r in range(enc_ref.shape[0] // tile):
        cut = slice(r * tile, (r + 1) * tile)
        out = enc_ref[cut, :].astype(F32) + jnp.dot(act[cut, :], second[...], preferred_element_type=F32)
        enc_ref[cut, :] = out.astype(BF16)
        for b in range(r * tile // rows, (r + 1) * tile // rows):
            slot = outward * offset_of(owner[b], mine, count) + REACH
            total[slot] += columns[:, b:b + 1] * out[b * rows - r * tile:(b + 1) * rows - r * tile, :]
    absent = sum(-offset_of(listed[0, n], mine, count) for n in range(listed.shape[1])).astype(F32)
    spot = lax.broadcasted_iota(jnp.int32, (EXTRA, LANES), 1)
    lines = rows * depth // LANES
    spread(msg_ref, 0, total[0])
    msg_ref[lines:, :] = jnp.where(spot == 1, absent, 0.0).astype(BF16)
    spread(base_ref, 0, total[4])
    spread(base_ref, lines, total[3])
    base_ref[2 * lines:, :] = jnp.where(spot == 0, absent, 0.0).astype(BF16)
    loc_ref[:rows, :] = total[1]
    loc_ref[rows:, :] = total[2] + feat_ref[...].astype(F32)
    later.wait()


def encode(owner, listed, weights, feat, grid, first, second, following):
    cells, depth = grid.shape
    hidden = first.shape[1]
    rows = feat.shape[0]
    tile, part = tiles_of(cells, hidden)
    return pl.pallas_call(
        encode_kernel,
        out_shape=(
            kept((cells, depth)),
            kept((rows * depth // LANES + EXTRA, LANES)),
            kept((2 * rows * depth // LANES + EXTRA, LANES)),
            kept((2 * rows, depth), F32),
            kept(following.shape),
        ),
        in_specs=[ANY] * 8,
        out_specs=(VMEM,) * 5,
        scratch_shapes=[
            pltpu.SMEM(owner.shape, jnp.int32),
            pltpu.SMEM(listed.shape, jnp.int32),
            pltpu.VMEM(weights.shape, F32),
            pltpu.VMEM(feat.shape, BF16),
            pltpu.VMEM((depth, hidden), BF16),
            pltpu.VMEM((hidden, depth), BF16),
            pltpu.VMEM((cells, hidden), BF16),
            pltpu.VMEM((2 * REACH + 1, rows, depth), F32),
            pltpu.SemaphoreType.DMA((2, hidden // part)),
            pltpu.SemaphoreType.DMA((cells // tile + 5,)),
        ],
        compiler_params=pltpu.CompilerParams(vmem_limit_bytes=24 << 20),
        cost_estimate=pl.CostEstimate(
            flops=4 * cells * depth * hidden, bytes_accessed=4 * (cells + hidden) * depth, transcendentals=cells * hidden
        ),
        name="encode",
    )(*in_hbm(owner, listed, weights, feat, grid, first, second, following))


def outgoing_kernel(base_ref, arrived_ref, out_ref):
    rows = arrived_ref.shape[0] - EXTRA
    out_ref[:rows, :] = base_ref[:rows, :]
    out_ref[rows:, :] = (base_ref[rows:, :].astype(F32) + arrived_ref[...].astype(F32)).astype(BF16)


def outgoing_sums(base, arrived):
    return pl.pallas_call(
        outgoing_kernel, out_shape=kept(base.shape), in_specs=[VMEM] * 2, out_specs=VMEM,
        compiler_params=pltpu.CompilerParams(vmem_limit_bytes=4 << 20), name="outgoing_sums"
    )(base, arrived)


def share_kernel(loc_ref, arrived_ref, after, share_ref, msg_ref):
    del after
    rows, depth = loc_ref.shape[0] // 2, loc_ref.shape[1]
    for half in range(2):
        cut = slice(half * rows, (half + 1) * rows)
        for k, cols in enumerate(strips(depth)):
            line = (half * depth // LANES + k) * rows
            share_ref[cut, cols] = loc_ref[cut, cols] + arrived_ref[line:line + rows, :].astype(F32)
    msg_ref[:rows, :] = share_ref[rows:, :].astype(BF16)
    msg_ref[rows:, :] = share_ref[:rows, :].astype(BF16)


def chip_share(local, arrived, after):
    return pl.pallas_call(
        share_kernel,
        out_shape=(kept(local.shape, F32), kept(local.shape)),
        in_specs=[VMEM] * 2 + [ANY],
        out_specs=(VMEM,) * 2,
        compiler_params=pltpu.CompilerParams(vmem_limit_bytes=4 << 20),
        name="chip_share",
    )(local, arrived, after)


def state_kernel(share_ref, other_ref, own_ref, pair_ref, msg_ref):
    rows = own_ref.shape[0]
    own_ref[...] = share_ref[rows:, :] + other_ref[rows:, :].astype(F32)
    pair_ref[:rows, :] = (share_ref[:rows, :] + other_ref[:rows, :].astype(F32)).astype(BF16)
    pair_ref[rows:, :] = own_ref[...].astype(BF16)
    msg_ref[:rows, :] = pair_ref[rows:, :]
    msg_ref[rows:, :] = pair_ref[:rows, :]


def chip_states(share, other):
    rows, depth = share.shape[0] // 2, share.shape[1]
    return pl.pallas_call(
        state_kernel,
        out_shape=(kept((rows, depth), F32), kept(share.shape), kept(share.shape)),
        in_specs=[VMEM] * 2,
        out_specs=(VMEM,) * 3,
        compiler_params=pltpu.CompilerParams(vmem_limit_bytes=4 << 20),
        name="chip_states",
    )(share, other)


def normal(block, gain):
    state = block.astype(F32)
    scale = lax.rsqrt(jnp.mean(state * state, axis=-1, keepdims=True) + 1e-6)
    return (state * scale * gain).astype(BF16)


def project_kernel(pair_ref, near_ref, gain_ref, w_qkv, query_ref, kv_ref, normed):
    rows, depth = pair_ref.shape[0] // 2, pair_ref.shape[1]
    gain = gain_ref[...]
    normed[:2 * rows, :] = normal(pair_ref[...], gain)
    normed[2 * rows:, :] = normal(near_ref[...], gain)
    kv_ref[...] = jnp.dot(normed[...], w_qkv[:, depth:], preferred_element_type=F32).astype(BF16)
    query_ref[...] = jnp.dot(normed[rows:, :], w_qkv[:, :depth], preferred_element_type=F32).astype(BF16)


def project(pair, near, gain, w_qkv):
    rows, depth = pair.shape[0] // 2, pair.shape[1]
    return pl.pallas_call(
        project_kernel,
        out_shape=(kept((3 * rows, depth)), kept((4 * rows, 2 * depth))),
        in_specs=[VMEM] * 4,
        out_specs=(VMEM,) * 2,
        scratch_shapes=[pltpu.VMEM((4 * rows, depth), BF16)],
        compiler_params=pltpu.CompilerParams(vmem_limit_bytes=8 << 20),
        cost_estimate=pl.CostEstimate(
            flops=22 * rows * depth * depth, bytes_accessed=2 * rows * depth, transcendentals=0
        ),
        name="project",
    )(pair, near, gain, w_qkv)


def attention(query, window, keep):
    depth = query.shape[1]
    every = [slice(h * HD, (h + 1) * HD) for h in range(depth // HD)]
    scores = [
        jnp.concatenate([
            lax.dot_general(
                query[:, cols], ref[first:first + size, cols], (((1,), (1,)), ((), ())), preferred_element_type=F32
            )
            for ref, first, size in window
        ], axis=1)
        for cols in every
    ]
    scores = [jnp.where(keep, score, -jnp.inf) for score in scores]
    below = [(score - jnp.max(score, axis=-1, keepdims=True)) * (HD ** -0.5 * LOG2E) for score in scores]
    grown = [jnp.exp2(score.astype(BF16)) for score in below]
    heads = []
    for h, cols in enumerate(every):
        start, taken = 0, None
        for ref, first, size in window:
            value = ref[first:first + size, depth + cols.start:depth + cols.stop]
            value = jnp.concatenate([value, jnp.ones((size, HD), BF16)], axis=1)
            term = jnp.dot(grown[h][:, start:start + size], value, preferred_element_type=F32)
            taken = term if taken is None else taken + term
            start += size
        heads.append((taken[:, :HD] / taken[:, HD:]).astype(BF16))
    return jnp.concatenate(heads, axis=1)


def kept_lanes(rows, absent):
    block = (lax.broadcasted_iota(jnp.int32, (rows, (2 * REACH + 1) * rows), 1) // rows).astype(F32)
    return block != outward_of().astype(F32) * absent + REACH


def attend_own_kernel(base_ref, own_ref, query_ref, kv_ref, behind_ref, gain_ref, w_qkv, w_out, ring_ref, kv_behind):
    rows, depth = own_ref.shape
    kv_behind[...] = jnp.dot(
        normal(behind_ref[...], gain_ref[...]), w_qkv[:, depth:], preferred_element_type=F32
    ).astype(BF16)
    keep = kept_lanes(rows, base_ref[2 * rows * depth // LANES:, :].astype(F32)[0:1, 0:1])
    mixed = attention(query_ref[:rows, :], [(kv_behind, 0, rows), (kv_ref, 0, 4 * rows)], keep)
    ring_ref[...] = (own_ref[...] + jnp.dot(mixed, w_out[...], preferred_element_type=F32)).astype(BF16)


def attend_near_kernel(
    sums_ref, near_ref, query_ref, kv_ref, far_ref, gain_ref, w_qkv, w_out, after, ring_ref, kv_far, mixed
):
    del after
    rows, depth = near_ref.shape[0] // 2, near_ref.shape[1]
    kv_far[...] = jnp.dot(
        normal(far_ref[...], gain_ref[...]), w_qkv[:, depth:], preferred_element_type=F32
    ).astype(BF16)
    windows = [
        [(kv_ref, 0, 4 * rows), (kv_far, 0, rows)],
        [(kv_ref, rows, 3 * rows), (kv_far, 0, 2 * rows)],
    ]
    for n, window in enumerate(windows):
        keep = kept_lanes(rows, sums_ref[2 * rows * depth // LANES:, :].astype(F32)[0:1, n:n + 1])
        mixed[n * rows:(n + 1) * rows, :] = attention(query_ref[(n + 1) * rows:(n + 2) * rows, :], window, keep)
    added = jnp.dot(mixed[...], w_out[...], preferred_element_type=F32)
    ring_ref[...] = (near_ref[...].astype(F32) + added).astype(BF16)


def attend_own(base, own, query, kv, behind, gain, w_qkv, w_out):
    rows, depth = own.shape
    return pl.pallas_call(
        attend_own_kernel,
        out_shape=kept((rows, depth)),
        in_specs=[VMEM] * 8,
        out_specs=VMEM,
        scratch_shapes=[pltpu.VMEM((rows, 2 * depth), BF16)],
        compiler_params=pltpu.CompilerParams(vmem_limit_bytes=12 << 20),
        cost_estimate=pl.CostEstimate(
            flops=20 * rows * depth * depth, bytes_accessed=2 * rows * depth, transcendentals=0
        ),
        name="attend_own",
    )(base, own, query, kv, behind, gain, w_qkv, w_out)


def attend_near(sums, near, query, kv, far, gain, w_qkv, w_out, after):
    rows, depth = near.shape[0] // 2, near.shape[1]
    return pl.pallas_call(
        attend_near_kernel,
        out_shape=kept((2 * rows, depth)),
        in_specs=[VMEM] * 8 + [ANY],
        out_specs=VMEM,
        scratch_shapes=[pltpu.VMEM((2 * rows, 2 * depth), BF16), pltpu.VMEM((2 * rows, depth), BF16)],
        compiler_params=pltpu.CompilerParams(vmem_limit_bytes=12 << 20),
        cost_estimate=pl.CostEstimate(
            flops=40 * rows * depth * depth, bytes_accessed=2 * rows * depth, transcendentals=0
        ),
        name="attend_near",
    )(sums, near, query, kv, far, gain, w_qkv, w_out, after)


def halved(rows, first):
    return jnp.dot(rows * BF16(0.5), first, preferred_element_type=F32)


def grid_hidden_kernel(enc_ref, first, second_hbm, after, out_ref, second, sem):
    del after
    copy = pltpu.make_async_copy(second_hbm, second, sem)
    copy.start()
    tile, part = tiles_of(*out_ref.shape)
    for j in range(out_ref.shape[1] // part):
        cols = slice(j * part, (j + 1) * part)
        for r in range(out_ref.shape[0] // tile):
            cut = slice(r * tile, (r + 1) * tile)
            out_ref[cut, cols] = halved(enc_ref[cut, :], first[:, cols]).astype(BF16)
    copy.wait()


def grid_hidden(encoded, first, second, after):
    cells, depth = encoded.shape
    hidden = first.shape[1]
    return pl.pallas_call(
        grid_hidden_kernel,
        out_shape=(kept((cells, hidden)), kept(second.shape)),
        in_specs=[VMEM] * 2 + [ANY] * 2,
        out_specs=(VMEM, VMEM),
        scratch_shapes=[pltpu.SemaphoreType.DMA],
        compiler_params=pltpu.CompilerParams(vmem_limit_bytes=12 << 20),
        cost_estimate=pl.CostEstimate(
            flops=2 * cells * depth * hidden, bytes_accessed=2 * (cells + hidden) * depth, transcendentals=0
        ),
        name="grid_hidden",
    )(encoded, first, *in_hbm(second), after)


def mesh_hidden_kernel(back_own, ring_own, ring_near, first, out_ref):
    rows = ring_own.shape[0]
    out_ref[rows:REACH * rows, :] = halved(back_own[...], first[...]).astype(BF16)
    out_ref[REACH * rows:(REACH + 1) * rows, :] = halved(ring_own[...], first[...]).astype(BF16)
    out_ref[(REACH + 1) * rows:, :] = halved(ring_near[...], first[...]).astype(BF16)


def mesh_hidden(back_own, ring_own, ring_near, first):
    rows, depth = ring_own.shape
    return pl.pallas_call(
        mesh_hidden_kernel,
        out_shape=kept(((2 * REACH + 1) * rows, first.shape[1])),
        in_specs=[VMEM] * 4,
        out_specs=VMEM,
        compiler_params=pltpu.CompilerParams(vmem_limit_bytes=12 << 20),
        cost_estimate=pl.CostEstimate(
            flops=8 * rows * depth * first.shape[1], bytes_accessed=2 * rows * depth, transcendentals=0
        ),
        name="mesh_hidden",
    )(back_own, ring_own, ring_near, first)


def decode_kernel(
    owner_hbm, weight_ref, ring_own, ring_near, back_own, back_near, grid_ref, mesh_in, enc_ref, first, second,
    out_hbm, mesh_hbm, mesh_ref,
    owner, x_ref, act, ring, io_sems,
):
    del mesh_in
    rows = ring_own.shape[0]
    tile, part = tiles_of(x_ref.shape[0], first.shape[1])
    tile = min(tile, 256)
    tiles, parts = x_ref.shape[0] // tile, first.shape[1] // part
    stores = [pltpu.make_async_copy(ring_own, mesh_hbm, io_sems.at[x_ref.shape[0] // rows])]
    index = pltpu.make_async_copy(owner_hbm, owner, io_sems.at[x_ref.shape[0] // rows + 1])
    index.start()
    stores[0].start()
    mine, count = lax.axis_index(AXES), lax.axis_size(AXES)
    outward = outward_of()
    mesh_ref[:rows, :] = halved(back_near[...], first[...]).astype(BF16)
    ring[:rows, :] = back_near[...]
    ring[rows:2 * rows, :] = back_own[...]
    ring[2 * rows:3 * rows, :] = ring_own[...]
    ring[3 * rows:, :] = ring_near[...]
    columns = jnp.transpose(weight_ref[...])
    index.wait()
    for r in range(tiles):
        cut = slice(r * tile, (r + 1) * tile)
        reads = []
        for b in range(r * tile // rows, (r + 1) * tile // rows):
            slot = outward * offset_of(owner[b], mine, count) + REACH
            lines = pl.ds(pl.multiple_of(slot * rows, rows), rows)
            block = slice(b * rows, (b + 1) * rows)
            weight = columns[:, b:b + 1]
            narrow = weight.astype(BF16)
            for j in range(parts):
                cols = slice(j * part, (j + 1) * part)
                half = grid_ref[block, cols] + narrow * mesh_ref[lines, cols]
                act[block, cols] = half * jnp.tanh(half) + half
            reads.append((block, weight, lines))
        out = jnp.dot(act[cut, :], second[...], preferred_element_type=F32)
        for n, (block, weight, lines) in enumerate(reads):
            rest = enc_ref[block, :].astype(F32) + weight * ring[lines, :].astype(F32)
            x_ref[block, :] = (rest + out[n * rows:(n + 1) * rows, :]).astype(BF16)
            copy = pltpu.make_async_copy(x_ref.at[block], out_hbm.at[block], io_sems.at[r * tile // rows + n])
            copy.start()
            stores.append(copy)
    for copy in stores:
        copy.wait()


def decode(owner, weights, ring_own, ring_near, back_own, back_near, grid_part, mesh_part, encoded, first, second):
    cells, depth = encoded.shape
    hidden = first.shape[1]
    rows = ring_own.shape[0]
    return pl.pallas_call(
        decode_kernel,
        out_shape=(
            jax.ShapeDtypeStruct((cells, depth), BF16),
            jax.ShapeDtypeStruct((rows, depth), BF16),
            kept(mesh_part.shape),
        ),
        in_specs=[ANY] + [VMEM] * 10,
        out_specs=(ANY, ANY, VMEM),
        input_output_aliases={7: 2},
        scratch_shapes=[
            pltpu.SMEM(owner.shape, jnp.int32),
            pltpu.VMEM((cells, depth), BF16),
            pltpu.VMEM((cells, hidden), BF16),
            pltpu.VMEM(((2 * REACH + 1) * rows, depth), BF16),
            pltpu.SemaphoreType.DMA((cells // rows + 2,)),
        ],
        compiler_params=pltpu.CompilerParams(vmem_limit_bytes=16 << 20),
        cost_estimate=pl.CostEstimate(
            flops=2 * cells * depth * hidden, bytes_accessed=4 * (cells + hidden) * depth, transcendentals=cells * hidden
        ),
        name="decode",
    )(*in_hbm(owner), weights, ring_own, ring_near, back_own, back_near, grid_part, mesh_part, encoded, first, second)[:2]


def on_device(
    grid, g2m_owner, g2m_weight, m2g_owner, m2g_weight, mesh_feat, neighbours,
    enc_w1, enc_w2, attn_gain, w_qkv, w_out, dec_w1, dec_w2,
):
    rows = mesh_feat.shape[0]
    nblocks = g2m_owner.shape[0]
    encoded, message, base, local, first = encode(
        g2m_owner, neighbours, g2m_weight.reshape(nblocks, rows), mesh_feat, grid, enc_w1, enc_w2, dec_w1
    )
    outgoing = outgoing_sums(base, swapped(message))
    sums = from_outward(outgoing, 1)
    grid_part, second = grid_hidden(encoded, first, dec_w2, outgoing)
    share, message = chip_share(local, sums, grid_part)
    own, pair, message = chip_states(share, swapped(message))
    near = from_outward(message, 1)
    far = from_outward(message, 2)
    behind = swapped(near[:rows])
    query, kv = project(pair, near, attn_gain, w_qkv[0])
    ring_own = attend_own(base, own, query, kv, behind, attn_gain, w_qkv[0], w_out[0])
    ring_near = attend_near(sums, near, query, kv, far, attn_gain, w_qkv[0], w_out[0], ring_own)
    back_own = swapped(ring_own)
    back_near = swapped(ring_near[:rows])
    mesh_part = mesh_hidden(back_own, ring_own, ring_near, first)
    return decode(
        m2g_owner, m2g_weight.reshape(nblocks, rows), ring_own, ring_near, back_own, back_near,
        grid_part, mesh_part, encoded, first, second,
    )


def solution(mesh):
    split = P(AXES, None)
    flat = P(AXES)
    in_specs = (split, flat, flat, flat, flat, split, split) + (P(),) * 7
    return jax.shard_map(
        on_device, mesh=mesh, in_specs=in_specs, out_specs=(split, split), check_vma=False
    )
```

```python
import functools

import jax
import jax.numpy as jnp
from jax import lax
from jax.experimental import pallas as pl
from jax.experimental.pallas import tpu as pltpu
from jax.sharding import PartitionSpec as P

HD = 128
REACH = 2
LOG2E = 1.4426950408889634
EXTRA = 16
LANES = 128
AXES = ("tile", "sub")
BF16 = jnp.bfloat16
F32 = jnp.float32
VMEM = pl.BlockSpec(memory_space=pltpu.VMEM)
SMEM = pl.BlockSpec(memory_space=pltpu.SMEM)
ANY = pl.BlockSpec(memory_space=pl.ANY)


def swapped(block):
    count = lax.axis_size(AXES)
    return lax.ppermute(block, AXES, [(i, i ^ 1) for i in range(count)])


def from_outward(block, chips):
    count = lax.axis_size(AXES)
    route = []
    for i in range(count):
        step = 2 * chips - 1
        route.append((i, (i + step if i % 2 else i - step) % count))
    return lax.ppermute(block, AXES, route)


def tiles_of(rows, columns):
    return min(rows, 1024), min(columns, 1024)


def outward_of():
    return 2 * lax.axis_index("sub") - 1


def offset_of(owner, mine, count):
    return lax.rem(owner - mine + REACH + count, count) - REACH


def kept(shape, dtype=BF16):
    return pltpu.VMEM(shape, dtype)


def in_hbm(*arrays):
    return [pltpu.with_memory_space_constraint(a, pltpu.HBM) for a in arrays]


def strips(depth):
    return [slice(k, k + LANES) for k in range(0, depth, LANES)]


def spread(ref, first, block):
    rows = block.shape[0]
    for k, cols in enumerate(strips(block.shape[1])):
        ref[first + k * rows:first + (k + 1) * rows, :] = block[:, cols].astype(BF16)


def hidden_layer(x_ref, first, act, tile, part, arrive, before):
    for j in range(first.shape[1] // part):
        before(j)
        cols = slice(j * part, (j + 1) * part)
        for r in range(x_ref.shape[0] // tile):
            if j == 0:
                arrive(r)
            cut = slice(r * tile, (r + 1) * tile)
            half = jnp.dot(x_ref[cut, :] * BF16(0.5), first[:, cols], preferred_element_type=F32)
            act[cut, cols] = (half * jnp.tanh(half) + half).astype(BF16)


def encode_kernel(
    owner_hbm, listed_hbm, weight_hbm, feat_hbm, x_hbm, first_hbm, second_hbm, next_hbm,
    enc_ref, msg_ref, base_ref, loc_ref, next_ref,
    owner, listed, weight_ref, feat_ref, first, second, act, total, sems, io_sems,
):
    rows, depth = feat_ref.shape
    tile, part = tiles_of(enc_ref.shape[0], first.shape[1])
    tiles, parts = enc_ref.shape[0] // tile, first.shape[1] // part
    loads = [
        pltpu.make_async_copy(x_hbm.at[pl.ds(r * tile, tile)], enc_ref.at[pl.ds(r * tile, tile)], io_sems.at[r])
        for r in range(tiles)
    ]
    ones, twos = [], []
    for j in range(parts):
        cut = pl.ds(j * part, part)
        ones.append(pltpu.make_async_copy(first_hbm.at[:, cut], first.at[:, cut], sems.at[0, j]))
        twos.append(pltpu.make_async_copy(second_hbm.at[cut], second.at[cut], sems.at[1, j]))
    small = [
        pltpu.make_async_copy(weight_hbm, weight_ref, io_sems.at[tiles]),
        pltpu.make_async_copy(feat_hbm, feat_ref, io_sems.at[tiles + 1]),
        pltpu.make_async_copy(owner_hbm, owner, io_sems.at[tiles + 2]),
        pltpu.make_async_copy(listed_hbm, listed, io_sems.at[tiles + 3]),
    ]
    later = pltpu.make_async_copy(next_hbm, next_ref, io_sems.at[tiles + 4])
    for copy in loads + ones + twos + small + [later]:
        copy.start()

    def arrive(r):
        if r == 0:
            for copy in loads:
                copy.wait()

    mine, count = lax.axis_index(AXES), lax.axis_size(AXES)
    outward = outward_of()
    total[...] = jnp.zeros_like(total)

    def before(j):
        due = ones[:1] if j == 0 else []
        if j == min(1, parts - 1):
            due = due + ones[1:] + twos + small
        for copy in due:
            copy.wait()

    hidden_layer(enc_ref, first, act, tile, part, arrive, before)
    columns = jnp.transpose(weight_ref[...])
    tile = min(tile, 256)
    for r in range(enc_ref.shape[0] // tile):
        cut = slice(r * tile, (r + 1) * tile)
        out = enc_ref[cut, :].astype(F32) + jnp.dot(act[cut, :], second[...], preferred_element_type=F32)
        enc_ref[cut, :] = out.astype(BF16)
        for b in range(r * tile // rows, (r + 1) * tile // rows):
            slot = outward * offset_of(owner[b], mine, count) + REACH
            total[slot] += columns[:, b:b + 1] * out[b * rows - r * tile:(b + 1) * rows - r * tile, :]
    absent = sum(-offset_of(listed[0, n], mine, count) for n in range(listed.shape[1])).astype(F32)
    spot = lax.broadcasted_iota(jnp.int32, (EXTRA, LANES), 1)
    lines = rows * depth // LANES
    spread(msg_ref, 0, total[0])
    msg_ref[lines:, :] = jnp.where(spot == 1, absent, 0.0).astype(BF16)
    spread(base_ref, 0, total[4])
    spread(base_ref, lines, total[3])
    base_ref[2 * lines:, :] = jnp.where(spot == 0, absent, 0.0).astype(BF16)
    loc_ref[:rows, :] = total[1]
    loc_ref[rows:, :] = total[2] + feat_ref[...].astype(F32)
    later.wait()


def encode(owner, listed, weights, feat, grid, first, second, following):
    cells, depth = grid.shape
    hidden = first.shape[1]
    rows = feat.shape[0]
    tile, part = tiles_of(cells, hidden)
    return pl.pallas_call(
        encode_kernel,
        out_shape=(
            kept((cells, depth)),
            kept((rows * depth // LANES + EXTRA, LANES)),
            kept((2 * rows * depth // LANES + EXTRA, LANES)),
            kept((2 * rows, depth), F32),
            kept(following.shape),
        ),
        in_specs=[ANY] * 8,
        out_specs=(VMEM,) * 5,
        scratch_shapes=[
            pltpu.SMEM(owner.shape, jnp.int32),
            pltpu.SMEM(listed.shape, jnp.int32),
            pltpu.VMEM(weights.shape, F32),
            pltpu.VMEM(feat.shape, BF16),
            pltpu.VMEM((depth, hidden), BF16),
            pltpu.VMEM((hidden, depth), BF16),
            pltpu.VMEM((cells, hidden), BF16),
            pltpu.VMEM((2 * REACH + 1, rows, depth), F32),
            pltpu.SemaphoreType.DMA((2, hidden // part)),
            pltpu.SemaphoreType.DMA((cells // tile + 5,)),
        ],
        compiler_params=pltpu.CompilerParams(vmem_limit_bytes=24 << 20),
        cost_estimate=pl.CostEstimate(
            flops=4 * cells * depth * hidden, bytes_accessed=4 * (cells + hidden) * depth, transcendentals=cells * hidden
        ),
        name="encode",
    )(*in_hbm(owner, listed, weights, feat, grid, first, second, following))


def outgoing_kernel(base_ref, arrived_ref, out_ref):
    rows = arrived_ref.shape[0] - EXTRA
    out_ref[:rows, :] = base_ref[:rows, :]
    out_ref[rows:, :] = (base_ref[rows:, :].astype(F32) + arrived_ref[...].astype(F32)).astype(BF16)


def outgoing_sums(base, arrived):
    return pl.pallas_call(
        outgoing_kernel, out_shape=kept(base.shape), in_specs=[VMEM] * 2, out_specs=VMEM,
        compiler_params=pltpu.CompilerParams(vmem_limit_bytes=4 << 20), name="outgoing_sums"
    )(base, arrived)


def share_kernel(loc_ref, arrived_ref, after, share_ref, msg_ref):
    del after
    rows, depth = loc_ref.shape[0] // 2, loc_ref.shape[1]
    for half in range(2):
        cut = slice(half * rows, (half + 1) * rows)
        for k, cols in enumerate(strips(depth)):
            line = (half * depth // LANES + k) * rows
            share_ref[cut, cols] = loc_ref[cut, cols] + arrived_ref[line:line + rows, :].astype(F32)
    msg_ref[:rows, :] = share_ref[rows:, :].astype(BF16)
    msg_ref[rows:, :] = share_ref[:rows, :].astype(BF16)


def chip_share(local, arrived, after):
    return pl.pallas_call(
        share_kernel,
        out_shape=(kept(local.shape, F32), kept(local.shape)),
        in_specs=[VMEM] * 2 + [ANY],
        out_specs=(VMEM,) * 2,
        compiler_params=pltpu.CompilerParams(vmem_limit_bytes=4 << 20),
        name="chip_share",
    )(local, arrived, after)


def state_kernel(share_ref, other_ref, own_ref, pair_ref, msg_ref):
    rows = own_ref.shape[0]
    own_ref[...] = share_ref[rows:, :] + other_ref[rows:, :].astype(F32)
    pair_ref[:rows, :] = (share_ref[:rows, :] + other_ref[:rows, :].astype(F32)).astype(BF16)
    pair_ref[rows:, :] = own_ref[...].astype(BF16)
    msg_ref[:rows, :] = pair_ref[rows:, :]
    msg_ref[rows:, :] = pair_ref[:rows, :]


def chip_states(share, other):
    rows, depth = share.shape[0] // 2, share.shape[1]
    return pl.pallas_call(
        state_kernel,
        out_shape=(kept((rows, depth), F32), kept(share.shape), kept(share.shape)),
        in_specs=[VMEM] * 2,
        out_specs=(VMEM,) * 3,
        compiler_params=pltpu.CompilerParams(vmem_limit_bytes=4 << 20),
        name="chip_states",
    )(share, other)


def normal(block, gain):
    state = block.astype(F32)
    scale = lax.rsqrt(jnp.mean(state * state, axis=-1, keepdims=True) + 1e-6)
    return (state * scale * gain).astype(BF16)


def project_kernel(pair_ref, near_ref, gain_ref, w_qkv, query_ref, kv_ref, normed):
    rows, depth = pair_ref.shape[0] // 2, pair_ref.shape[1]
    gain = gain_ref[...]
    normed[:2 * rows, :] = normal(pair_ref[...], gain)
    normed[2 * rows:, :] = normal(near_ref[...], gain)
    kv_ref[...] = jnp.dot(normed[...], w_qkv[:, depth:], preferred_element_type=F32).astype(BF16)
    query_ref[...] = jnp.dot(normed[rows:, :], w_qkv[:, :depth], preferred_element_type=F32).astype(BF16)


def project(pair, near, gain, w_qkv):
    rows, depth = pair.shape[0] // 2, pair.shape[1]
    return pl.pallas_call(
        project_kernel,
        out_shape=(kept((3 * rows, depth)), kept((4 * rows, 2 * depth))),
        in_specs=[VMEM] * 4,
        out_specs=(VMEM,) * 2,
        scratch_shapes=[pltpu.VMEM((4 * rows, depth), BF16)],
        compiler_params=pltpu.CompilerParams(vmem_limit_bytes=8 << 20),
        cost_estimate=pl.CostEstimate(
            flops=22 * rows * depth * depth, bytes_accessed=2 * rows * depth, transcendentals=0
        ),
        name="project",
    )(pair, near, gain, w_qkv)


def attention(items):
    units = [
        (n, slice(h * HD, (h + 1) * HD)) for n, (query, _, _) in enumerate(items) for h in range(query.shape[1] // HD)
    ]
    scores = [
        jnp.concatenate([
            lax.dot_general(
                items[n][0][:, cols], ref[first:first + size, cols], (((1,), (1,)), ((), ())), preferred_element_type=F32
            )
            for ref, first, size in items[n][1]
        ], axis=1)
        for n, cols in units
    ]
    scores = [jnp.where(items[n][2], score, -jnp.inf) for (n, _), score in zip(units, scores)]
    below = [(score - jnp.max(score, axis=-1, keepdims=True)) * (HD ** -0.5 * LOG2E) for score in scores]
    grown = [jnp.exp2(score.astype(BF16)) for score in below]
    heads = [[] for _ in items]
    for (n, cols), weights in zip(units, grown):
        query, window, _ = items[n]
        depth = query.shape[1]
        start, taken = 0, None
        for ref, first, size in window:
            value = ref[first:first + size, depth + cols.start:depth + cols.stop]
            value = jnp.concatenate([value, jnp.ones((size, HD), BF16)], axis=1)
            term = jnp.dot(weights[:, start:start + size], value, preferred_element_type=F32)
            taken = term if taken is None else taken + term
            start += size
        heads[n].append((taken[:, :HD] / taken[:, HD:]).astype(BF16))
    return [jnp.concatenate(parts, axis=1) for parts in heads]


def kept_lanes(rows, absent):
    block = (lax.broadcasted_iota(jnp.int32, (rows, (2 * REACH + 1) * rows), 1) // rows).astype(F32)
    return block != outward_of().astype(F32) * absent + REACH


def attend_own_kernel(base_ref, own_ref, query_ref, kv_ref, behind_ref, gain_ref, w_qkv, w_out, ring_ref, kv_behind):
    rows, depth = own_ref.shape
    kv_behind[...] = jnp.dot(
        normal(behind_ref[...], gain_ref[...]), w_qkv[:, depth:], preferred_element_type=F32
    ).astype(BF16)
    keep = kept_lanes(rows, base_ref[2 * rows * depth // LANES:, :].astype(F32)[0:1, 0:1])
    mixed = attention([(query_ref[:rows, :], [(kv_behind, 0, rows), (kv_ref, 0, 4 * rows)], keep)])[0]
    ring_ref[...] = (own_ref[...] + jnp.dot(mixed, w_out[...], preferred_element_type=F32)).astype(BF16)


def attend_near_kernel(
    sums_ref, near_ref, query_ref, kv_ref, far_ref, gain_ref, w_qkv, w_out, after, ring_ref, kv_far, mixed
):
    del after
    rows, depth = near_ref.shape[0] // 2, near_ref.shape[1]
    kv_far[...] = jnp.dot(
        normal(far_ref[...], gain_ref[...]), w_qkv[:, depth:], preferred_element_type=F32
    ).astype(BF16)
    windows = [
        [(kv_ref, 0, 4 * rows), (kv_far, 0, rows)],
        [(kv_ref, rows, 3 * rows), (kv_far, 0, 2 * rows)],
    ]
    items = []
    for n, window in enumerate(windows):
        keep = kept_lanes(rows, sums_ref[2 * rows * depth // LANES:, :].astype(F32)[0:1, n:n + 1])
        items.append((query_ref[(n + 1) * rows:(n + 2) * rows, :], window, keep))
    for n, block in enumerate(attention(items)):
        mixed[n * rows:(n + 1) * rows, :] = block
    added = jnp.dot(mixed[...], w_out[...], preferred_element_type=F32)
    ring_ref[...] = (near_ref[...].astype(F32) + added).astype(BF16)


def attend_own(base, own, query, kv, behind, gain, w_qkv, w_out):
    rows, depth = own.shape
    return pl.pallas_call(
        attend_own_kernel,
        out_shape=kept((rows, depth)),
        in_specs=[VMEM] * 8,
        out_specs=VMEM,
        scratch_shapes=[pltpu.VMEM((rows, 2 * depth), BF16)],
        compiler_params=pltpu.CompilerParams(vmem_limit_bytes=12 << 20),
        cost_estimate=pl.CostEstimate(
            flops=20 * rows * depth * depth, bytes_accessed=2 * rows * depth, transcendentals=0
        ),
        name="attend_own",
    )(base, own, query, kv, behind, gain, w_qkv, w_out)


def attend_near(sums, near, query, kv, far, gain, w_qkv, w_out, after):
    rows, depth = near.shape[0] // 2, near.shape[1]
    return pl.pallas_call(
        attend_near_kernel,
        out_shape=kept((2 * rows, depth)),
        in_specs=[VMEM] * 8 + [ANY],
        out_specs=VMEM,
        scratch_shapes=[pltpu.VMEM((2 * rows, 2 * depth), BF16), pltpu.VMEM((2 * rows, depth), BF16)],
        compiler_params=pltpu.CompilerParams(vmem_limit_bytes=12 << 20),
        cost_estimate=pl.CostEstimate(
            flops=40 * rows * depth * depth, bytes_accessed=2 * rows * depth, transcendentals=0
        ),
        name="attend_near",
    )(sums, near, query, kv, far, gain, w_qkv, w_out, after)


def halved(rows, first):
    return jnp.dot(rows * BF16(0.5), first, preferred_element_type=F32)


def grid_hidden_kernel(enc_ref, first, second_hbm, after, out_ref, second, sem):
    del after
    copy = pltpu.make_async_copy(second_hbm, second, sem)
    copy.start()
    tile, part = tiles_of(*out_ref.shape)
    for j in range(out_ref.shape[1] // part):
        cols = slice(j * part, (j + 1) * part)
        for r in range(out_ref.shape[0] // tile):
            cut = slice(r * tile, (r + 1) * tile)
            out_ref[cut, cols] = halved(enc_ref[cut, :], first[:, cols]).astype(BF16)
    copy.wait()


def grid_hidden(encoded, first, second, after):
    cells, depth = encoded.shape
    hidden = first.shape[1]
    return pl.pallas_call(
        grid_hidden_kernel,
        out_shape=(kept((cells, hidden)), kept(second.shape)),
        in_specs=[VMEM] * 2 + [ANY] * 2,
        out_specs=(VMEM, VMEM),
        scratch_shapes=[pltpu.SemaphoreType.DMA],
        compiler_params=pltpu.CompilerParams(vmem_limit_bytes=12 << 20),
        cost_estimate=pl.CostEstimate(
            flops=2 * cells * depth * hidden, bytes_accessed=2 * (cells + hidden) * depth, transcendentals=0
        ),
        name="grid_hidden",
    )(encoded, first, *in_hbm(second), after)


def mesh_hidden_kernel(back_own, ring_own, ring_near, first, out_ref):
    rows = ring_own.shape[0]
    out_ref[rows:REACH * rows, :] = halved(back_own[...], first[...]).astype(BF16)
    out_ref[REACH * rows:(REACH + 1) * rows, :] = halved(ring_own[...], first[...]).astype(BF16)
    out_ref[(REACH + 1) * rows:, :] = halved(ring_near[...], first[...]).astype(BF16)


def mesh_hidden(back_own, ring_own, ring_near, first):
    rows, depth = ring_own.shape
    return pl.pallas_call(
        mesh_hidden_kernel,
        out_shape=kept(((2 * REACH + 1) * rows, first.shape[1])),
        in_specs=[VMEM] * 4,
        out_specs=VMEM,
        compiler_params=pltpu.CompilerParams(vmem_limit_bytes=12 << 20),
        cost_estimate=pl.CostEstimate(
            flops=8 * rows * depth * first.shape[1], bytes_accessed=2 * rows * depth, transcendentals=0
        ),
        name="mesh_hidden",
    )(back_own, ring_own, ring_near, first)


def decode_kernel(
    owner_hbm, weight_ref, ring_own, ring_near, back_own, back_near, grid_ref, mesh_in, enc_ref, first, second,
    out_hbm, mesh_hbm, mesh_ref,
    owner, x_ref, act, ring, io_sems,
):
    del mesh_in
    rows = ring_own.shape[0]
    tile, part = tiles_of(x_ref.shape[0], first.shape[1])
    tile = min(tile, 256)
    tiles, parts = x_ref.shape[0] // tile, first.shape[1] // part
    stores = [pltpu.make_async_copy(ring_own, mesh_hbm, io_sems.at[x_ref.shape[0] // rows])]
    index = pltpu.make_async_copy(owner_hbm, owner, io_sems.at[x_ref.shape[0] // rows + 1])
    index.start()
    stores[0].start()
    mine, count = lax.axis_index(AXES), lax.axis_size(AXES)
    outward = outward_of()
    mesh_ref[:rows, :] = halved(back_near[...], first[...]).astype(BF16)
    ring[:rows, :] = back_near[...]
    ring[rows:2 * rows, :] = back_own[...]
    ring[2 * rows:3 * rows, :] = ring_own[...]
    ring[3 * rows:, :] = ring_near[...]
    columns = jnp.transpose(weight_ref[...])
    index.wait()
    for r in range(tiles):
        cut = slice(r * tile, (r + 1) * tile)
        reads = []
        for b in range(r * tile // rows, (r + 1) * tile // rows):
            slot = outward * offset_of(owner[b], mine, count) + REACH
            lines = pl.ds(pl.multiple_of(slot * rows, rows), rows)
            block = slice(b * rows, (b + 1) * rows)
            weight = columns[:, b:b + 1]
            narrow = weight.astype(BF16)
            for j in range(parts):
                cols = slice(j * part, (j + 1) * part)
                half = grid_ref[block, cols] + narrow * mesh_ref[lines, cols]
                act[block, cols] = half * jnp.tanh(half) + half
            reads.append((block, weight, lines))
        out = jnp.dot(act[cut, :], second[...], preferred_element_type=F32)
        for n, (block, weight, lines) in enumerate(reads):
            rest = enc_ref[block, :].astype(F32) + weight * ring[lines, :].astype(F32)
            x_ref[block, :] = (rest + out[n * rows:(n + 1) * rows, :]).astype(BF16)
            copy = pltpu.make_async_copy(x_ref.at[block], out_hbm.at[block], io_sems.at[r * tile // rows + n])
            copy.start()
            stores.append(copy)
    for copy in stores:
        copy.wait()


def decode(owner, weights, ring_own, ring_near, back_own, back_near, grid_part, mesh_part, encoded, first, second):
    cells, depth = encoded.shape
    hidden = first.shape[1]
    rows = ring_own.shape[0]
    return pl.pallas_call(
        decode_kernel,
        out_shape=(
            jax.ShapeDtypeStruct((cells, depth), BF16),
            jax.ShapeDtypeStruct((rows, depth), BF16),
            kept(mesh_part.shape),
        ),
        in_specs=[ANY] + [VMEM] * 10,
        out_specs=(ANY, ANY, VMEM),
        input_output_aliases={7: 2},
        scratch_shapes=[
            pltpu.SMEM(owner.shape, jnp.int32),
            pltpu.VMEM((cells, depth), BF16),
            pltpu.VMEM((cells, hidden), BF16),
            pltpu.VMEM(((2 * REACH + 1) * rows, depth), BF16),
            pltpu.SemaphoreType.DMA((cells // rows + 2,)),
        ],
        compiler_params=pltpu.CompilerParams(vmem_limit_bytes=16 << 20),
        cost_estimate=pl.CostEstimate(
            flops=2 * cells * depth * hidden, bytes_accessed=4 * (cells + hidden) * depth, transcendentals=cells * hidden
        ),
        name="decode",
    )(*in_hbm(owner), weights, ring_own, ring_near, back_own, back_near, grid_part, mesh_part, encoded, first, second)[:2]


def on_device(
    grid, g2m_owner, g2m_weight, m2g_owner, m2g_weight, mesh_feat, neighbours,
    enc_w1, enc_w2, attn_gain, w_qkv, w_out, dec_w1, dec_w2,
):
    rows = mesh_feat.shape[0]
    nblocks = g2m_owner.shape[0]
    encoded, message, base, local, first = encode(
        g2m_owner, neighbours, g2m_weight.reshape(nblocks, rows), mesh_feat, grid, enc_w1, enc_w2, dec_w1
    )
    outgoing = outgoing_sums(base, swapped(message))
    sums = from_outward(outgoing, 1)
    grid_part, second = grid_hidden(encoded, first, dec_w2, outgoing)
    share, message = chip_share(local, sums, grid_part)
    own, pair, message = chip_states(share, swapped(message))
    near = from_outward(message, 1)
    far = from_outward(message, 2)
    behind = swapped(near[:rows])
    query, kv = project(pair, near, attn_gain, w_qkv[0])
    ring_own = attend_own(base, own, query, kv, behind, attn_gain, w_qkv[0], w_out[0])
    ring_near = attend_near(sums, near, query, kv, far, attn_gain, w_qkv[0], w_out[0], ring_own)
    back_own = swapped(ring_own)
    back_near = swapped(ring_near[:rows])
    mesh_part = mesh_hidden(back_own, ring_own, ring_near, first)
    return decode(
        m2g_owner, m2g_weight.reshape(nblocks, rows), ring_own, ring_near, back_own, back_near,
        grid_part, mesh_part, encoded, first, second,
    )


def solution(mesh):
    split = P(AXES, None)
    flat = P(AXES)
    in_specs = (split, flat, flat, flat, flat, split, split) + (P(),) * 7
    return jax.shard_map(
        on_device, mesh=mesh, in_specs=in_specs, out_specs=(split, split), check_vma=False
    )
```

```python
import functools

import jax
import jax.numpy as jnp
from jax import lax
from jax.experimental import pallas as pl
from jax.experimental.pallas import tpu as pltpu
from jax.sharding import PartitionSpec as P

HD = 128
REACH = 2
LOG2E = 1.4426950408889634
EXTRA = 16
LANES = 128
AXES = ("tile", "sub")
BF16 = jnp.bfloat16
F32 = jnp.float32
VMEM = pl.BlockSpec(memory_space=pltpu.VMEM)
SMEM = pl.BlockSpec(memory_space=pltpu.SMEM)
ANY = pl.BlockSpec(memory_space=pl.ANY)


def swapped(block):
    count = lax.axis_size(AXES)
    return lax.ppermute(block, AXES, [(i, i ^ 1) for i in range(count)])


def from_outward(block, chips):
    count = lax.axis_size(AXES)
    route = []
    for i in range(count):
        step = 2 * chips - 1
        route.append((i, (i + step if i % 2 else i - step) % count))
    return lax.ppermute(block, AXES, route)


def tiles_of(rows, columns):
    return min(rows, 1024), min(columns, 1024)


def outward_of():
    return 2 * lax.axis_index("sub") - 1


def offset_of(owner, mine, count):
    return lax.rem(owner - mine + REACH + count, count) - REACH


def kept(shape, dtype=BF16):
    return pltpu.VMEM(shape, dtype)


def in_hbm(*arrays):
    return [pltpu.with_memory_space_constraint(a, pltpu.HBM) for a in arrays]


def strips(depth):
    return [slice(k, k + LANES) for k in range(0, depth, LANES)]


def spread(ref, first, block):
    rows = block.shape[0]
    for k, cols in enumerate(strips(block.shape[1])):
        ref[first + k * rows:first + (k + 1) * rows, :] = block[:, cols].astype(BF16)


def hidden_layer(x_ref, first, act, tile, part, arrive, before):
    for j in range(first.shape[1] // part):
        before(j)
        cols = slice(j * part, (j + 1) * part)
        for r in range(x_ref.shape[0] // tile):
            if j == 0:
                arrive(r)
            cut = slice(r * tile, (r + 1) * tile)
            half = jnp.dot(x_ref[cut, :] * BF16(0.5), first[:, cols], preferred_element_type=F32)
            act[cut, cols] = (half * jnp.tanh(half) + half).astype(BF16)


def encode_kernel(
    owner_hbm, listed_hbm, weight_hbm, feat_hbm, x_hbm, first_hbm, second_hbm, next_hbm,
    enc_ref, msg_ref, base_ref, loc_ref, next_ref,
    owner, listed, weight_ref, feat_ref, first, second, act, total, sems, io_sems,
):
    rows, depth = feat_ref.shape
    tile, part = tiles_of(enc_ref.shape[0], first.shape[1])
    tiles, parts = enc_ref.shape[0] // tile, first.shape[1] // part
    loads = [
        pltpu.make_async_copy(x_hbm.at[pl.ds(r * tile, tile)], enc_ref.at[pl.ds(r * tile, tile)], io_sems.at[r])
        for r in range(tiles)
    ]
    ones, twos = [], []
    for j in range(parts):
        cut = pl.ds(j * part, part)
        ones.append(pltpu.make_async_copy(first_hbm.at[:, cut], first.at[:, cut], sems.at[0, j]))
        twos.append(pltpu.make_async_copy(second_hbm.at[cut], second.at[cut], sems.at[1, j]))
    small = [
        pltpu.make_async_copy(weight_hbm, weight_ref, io_sems.at[tiles]),
        pltpu.make_async_copy(feat_hbm, feat_ref, io_sems.at[tiles + 1]),
        pltpu.make_async_copy(owner_hbm, owner, io_sems.at[tiles + 2]),
        pltpu.make_async_copy(listed_hbm, listed, io_sems.at[tiles + 3]),
    ]
    later = pltpu.make_async_copy(next_hbm, next_ref, io_sems.at[tiles + 4])
    for copy in loads + ones + twos + small + [later]:
        copy.start()

    def arrive(r):
        if r == 0:
            for copy in loads:
                copy.wait()

    mine, count = lax.axis_index(AXES), lax.axis_size(AXES)
    outward = outward_of()
    total[...] = jnp.zeros_like(total)

    def before(j):
        due = ones[:1] if j == 0 else []
        if j == min(1, parts - 1):
            due = due + ones[1:] + twos + small
        for copy in due:
            copy.wait()

    hidden_layer(enc_ref, first, act, tile, part, arrive, before)
    columns = jnp.transpose(weight_ref[...])
    tile = min(tile, 512)
    for r in range(enc_ref.shape[0] // tile):
        cut = slice(r * tile, (r + 1) * tile)
        out = enc_ref[cut, :].astype(F32) + jnp.dot(act[cut, :], second[...], preferred_element_type=F32)
        enc_ref[cut, :] = out.astype(BF16)
        for b in range(r * tile // rows, (r + 1) * tile // rows):
            slot = outward * offset_of(owner[b], mine, count) + REACH
            total[slot] += columns[:, b:b + 1] * out[b * rows - r * tile:(b + 1) * rows - r * tile, :]
    absent = sum(-offset_of(listed[0, n], mine, count) for n in range(listed.shape[1])).astype(F32)
    spot = lax.broadcasted_iota(jnp.int32, (EXTRA, LANES), 1)
    lines = rows * depth // LANES
    spread(msg_ref, 0, total[0])
    msg_ref[lines:, :] = jnp.where(spot == 1, absent, 0.0).astype(BF16)
    spread(base_ref, 0, total[4])
    spread(base_ref, lines, total[3])
    base_ref[2 * lines:, :] = jnp.where(spot == 0, absent, 0.0).astype(BF16)
    loc_ref[:rows, :] = total[1]
    loc_ref[rows:, :] = total[2] + feat_ref[...].astype(F32)
    later.wait()


def encode(owner, listed, weights, feat, grid, first, second, following):
    cells, depth = grid.shape
    hidden = first.shape[1]
    rows = feat.shape[0]
    tile, part = tiles_of(cells, hidden)
    return pl.pallas_call(
        encode_kernel,
        out_shape=(
            kept((cells, depth)),
            kept((rows * depth // LANES + EXTRA, LANES)),
            kept((2 * rows * depth // LANES + EXTRA, LANES)),
            kept((2 * rows, depth), F32),
            kept(following.shape),
        ),
        in_specs=[ANY] * 8,
        out_specs=(VMEM,) * 5,
        scratch_shapes=[
            pltpu.SMEM(owner.shape, jnp.int32),
            pltpu.SMEM(listed.shape, jnp.int32),
            pltpu.VMEM(weights.shape, F32),
            pltpu.VMEM(feat.shape, BF16),
            pltpu.VMEM((depth, hidden), BF16),
            pltpu.VMEM((hidden, depth), BF16),
            pltpu.VMEM((cells, hidden), BF16),
            pltpu.VMEM((2 * REACH + 1, rows, depth), F32),
            pltpu.SemaphoreType.DMA((2, hidden // part)),
            pltpu.SemaphoreType.DMA((cells // tile + 5,)),
        ],
        compiler_params=pltpu.CompilerParams(vmem_limit_bytes=24 << 20),
        cost_estimate=pl.CostEstimate(
            flops=4 * cells * depth * hidden, bytes_accessed=4 * (cells + hidden) * depth, transcendentals=cells * hidden
        ),
        name="encode",
    )(*in_hbm(owner, listed, weights, feat, grid, first, second, following))


def outgoing_kernel(base_ref, arrived_ref, out_ref):
    rows = arrived_ref.shape[0] - EXTRA
    out_ref[:rows, :] = base_ref[:rows, :]
    out_ref[rows:, :] = (base_ref[rows:, :].astype(F32) + arrived_ref[...].astype(F32)).astype(BF16)


def outgoing_sums(base, arrived):
    return pl.pallas_call(
        outgoing_kernel, out_shape=kept(base.shape), in_specs=[VMEM] * 2, out_specs=VMEM,
        compiler_params=pltpu.CompilerParams(vmem_limit_bytes=4 << 20), name="outgoing_sums"
    )(base, arrived)


def share_kernel(loc_ref, arrived_ref, after, share_ref, msg_ref):
    del after
    rows, depth = loc_ref.shape[0] // 2, loc_ref.shape[1]
    for half in range(2):
        cut = slice(half * rows, (half + 1) * rows)
        for k, cols in enumerate(strips(depth)):
            line = (half * depth // LANES + k) * rows
            share_ref[cut, cols] = loc_ref[cut, cols] + arrived_ref[line:line + rows, :].astype(F32)
    msg_ref[:rows, :] = share_ref[rows:, :].astype(BF16)
    msg_ref[rows:, :] = share_ref[:rows, :].astype(BF16)


def chip_share(local, arrived, after):
    return pl.pallas_call(
        share_kernel,
        out_shape=(kept(local.shape, F32), kept(local.shape)),
        in_specs=[VMEM] * 2 + [ANY],
        out_specs=(VMEM,) * 2,
        compiler_params=pltpu.CompilerParams(vmem_limit_bytes=4 << 20),
        name="chip_share",
    )(local, arrived, after)


def state_kernel(share_ref, other_ref, own_ref, pair_ref, msg_ref):
    rows = own_ref.shape[0]
    own_ref[...] = share_ref[rows:, :] + other_ref[rows:, :].astype(F32)
    pair_ref[:rows, :] = (share_ref[:rows, :] + other_ref[:rows, :].astype(F32)).astype(BF16)
    pair_ref[rows:, :] = own_ref[...].astype(BF16)
    msg_ref[:rows, :] = pair_ref[rows:, :]
    msg_ref[rows:, :] = pair_ref[:rows, :]


def chip_states(share, other):
    rows, depth = share.shape[0] // 2, share.shape[1]
    return pl.pallas_call(
        state_kernel,
        out_shape=(kept((rows, depth), F32), kept(share.shape), kept(share.shape)),
        in_specs=[VMEM] * 2,
        out_specs=(VMEM,) * 3,
        compiler_params=pltpu.CompilerParams(vmem_limit_bytes=4 << 20),
        name="chip_states",
    )(share, other)


def normal(block, gain):
    state = block.astype(F32)
    scale = lax.rsqrt(jnp.mean(state * state, axis=-1, keepdims=True) + 1e-6)
    return (state * scale * gain).astype(BF16)


def project_kernel(pair_ref, near_ref, gain_ref, w_qkv, query_ref, kv_ref, normed):
    rows, depth = pair_ref.shape[0] // 2, pair_ref.shape[1]
    gain = gain_ref[...]
    normed[:2 * rows, :] = normal(pair_ref[...], gain)
    normed[2 * rows:, :] = normal(near_ref[...], gain)
    kv_ref[...] = jnp.dot(normed[...], w_qkv[:, depth:], preferred_element_type=F32).astype(BF16)
    query_ref[...] = jnp.dot(normed[rows:, :], w_qkv[:, :depth], preferred_element_type=F32).astype(BF16)


def project(pair, near, gain, w_qkv):
    rows, depth = pair.shape[0] // 2, pair.shape[1]
    return pl.pallas_call(
        project_kernel,
        out_shape=(kept((3 * rows, depth)), kept((4 * rows, 2 * depth))),
        in_specs=[VMEM] * 4,
        out_specs=(VMEM,) * 2,
        scratch_shapes=[pltpu.VMEM((4 * rows, depth), BF16)],
        compiler_params=pltpu.CompilerParams(vmem_limit_bytes=8 << 20),
        cost_estimate=pl.CostEstimate(
            flops=22 * rows * depth * depth, bytes_accessed=2 * rows * depth, transcendentals=0
        ),
        name="project",
    )(pair, near, gain, w_qkv)


def attention(items):
    units = [
        (n, slice(h * HD, (h + 1) * HD)) for n, (query, _, _) in enumerate(items) for h in range(query.shape[1] // HD)
    ]
    scores = [
        jnp.concatenate([
            lax.dot_general(
                items[n][0][:, cols], ref[first:first + size, cols], (((1,), (1,)), ((), ())), preferred_element_type=F32
            )
            for ref, first, size in items[n][1]
        ], axis=1)
        for n, cols in units
    ]
    scores = [jnp.where(items[n][2], score, -jnp.inf) for (n, _), score in zip(units, scores)]
    below = [(score - jnp.max(score, axis=-1, keepdims=True)) * (HD ** -0.5 * LOG2E) for score in scores]
    grown = [jnp.exp2(score.astype(BF16)) for score in below]
    heads = [[] for _ in items]
    for (n, cols), weights in zip(units, grown):
        query, window, _ = items[n]
        depth = query.shape[1]
        start, taken = 0, None
        for ref, first, size in window:
            value = ref[first:first + size, depth + cols.start:depth + cols.stop]
            value = jnp.concatenate([value, jnp.ones((size, HD), BF16)], axis=1)
            term = jnp.dot(weights[:, start:start + size], value, preferred_element_type=F32)
            taken = term if taken is None else taken + term
            start += size
        heads[n].append((taken[:, :HD] / taken[:, HD:]).astype(BF16))
    return [jnp.concatenate(parts, axis=1) for parts in heads]


def kept_lanes(rows, absent):
    block = (lax.broadcasted_iota(jnp.int32, (rows, (2 * REACH + 1) * rows), 1) // rows).astype(F32)
    return block != outward_of().astype(F32) * absent + REACH


def attend_own_kernel(base_ref, own_ref, query_ref, kv_ref, behind_ref, gain_ref, w_qkv, w_out, ring_ref, kv_behind):
    rows, depth = own_ref.shape
    kv_behind[...] = jnp.dot(
        normal(behind_ref[...], gain_ref[...]), w_qkv[:, depth:], preferred_element_type=F32
    ).astype(BF16)
    keep = kept_lanes(rows, base_ref[2 * rows * depth // LANES:, :].astype(F32)[0:1, 0:1])
    mixed = attention([(query_ref[:rows, :], [(kv_behind, 0, rows), (kv_ref, 0, 4 * rows)], keep)])[0]
    ring_ref[...] = (own_ref[...] + jnp.dot(mixed, w_out[...], preferred_element_type=F32)).astype(BF16)


def attend_near_kernel(
    sums_ref, near_ref, query_ref, kv_ref, far_ref, gain_ref, w_qkv, w_out, after, ring_ref, kv_far, mixed
):
    del after
    rows, depth = near_ref.shape[0] // 2, near_ref.shape[1]
    kv_far[...] = jnp.dot(
        normal(far_ref[...], gain_ref[...]), w_qkv[:, depth:], preferred_element_type=F32
    ).astype(BF16)
    windows = [
        [(kv_ref, 0, 4 * rows), (kv_far, 0, rows)],
        [(kv_ref, rows, 3 * rows), (kv_far, 0, 2 * rows)],
    ]
    items = []
    for n, window in enumerate(windows):
        keep = kept_lanes(rows, sums_ref[2 * rows * depth // LANES:, :].astype(F32)[0:1, n:n + 1])
        items.append((query_ref[(n + 1) * rows:(n + 2) * rows, :], window, keep))
    for n, block in enumerate(attention(items)):
        mixed[n * rows:(n + 1) * rows, :] = block
    added = jnp.dot(mixed[...], w_out[...], preferred_element_type=F32)
    ring_ref[...] = (near_ref[...].astype(F32) + added).astype(BF16)


def attend_own(base, own, query, kv, behind, gain, w_qkv, w_out):
    rows, depth = own.shape
    return pl.pallas_call(
        attend_own_kernel,
        out_shape=kept((rows, depth)),
        in_specs=[VMEM] * 8,
        out_specs=VMEM,
        scratch_shapes=[pltpu.VMEM((rows, 2 * depth), BF16)],
        compiler_params=pltpu.CompilerParams(vmem_limit_bytes=12 << 20),
        cost_estimate=pl.CostEstimate(
            flops=20 * rows * depth * depth, bytes_accessed=2 * rows * depth, transcendentals=0
        ),
        name="attend_own",
    )(base, own, query, kv, behind, gain, w_qkv, w_out)


def attend_near(sums, near, query, kv, far, gain, w_qkv, w_out, after):
    rows, depth = near.shape[0] // 2, near.shape[1]
    return pl.pallas_call(
        attend_near_kernel,
        out_shape=kept((2 * rows, depth)),
        in_specs=[VMEM] * 8 + [ANY],
        out_specs=VMEM,
        scratch_shapes=[pltpu.VMEM((2 * rows, 2 * depth), BF16), pltpu.VMEM((2 * rows, depth), BF16)],
        compiler_params=pltpu.CompilerParams(vmem_limit_bytes=12 << 20),
        cost_estimate=pl.CostEstimate(
            flops=40 * rows * depth * depth, bytes_accessed=2 * rows * depth, transcendentals=0
        ),
        name="attend_near",
    )(sums, near, query, kv, far, gain, w_qkv, w_out, after)


def halved(rows, first):
    return jnp.dot(rows * BF16(0.5), first, preferred_element_type=F32)


def grid_hidden_kernel(enc_ref, first, second_hbm, after, out_ref, second, sem):
    del after
    copy = pltpu.make_async_copy(second_hbm, second, sem)
    copy.start()
    tile, part = tiles_of(*out_ref.shape)
    for j in range(out_ref.shape[1] // part):
        cols = slice(j * part, (j + 1) * part)
        for r in range(out_ref.shape[0] // tile):
            cut = slice(r * tile, (r + 1) * tile)
            out_ref[cut, cols] = halved(enc_ref[cut, :], first[:, cols]).astype(BF16)
    copy.wait()


def grid_hidden(encoded, first, second, after):
    cells, depth = encoded.shape
    hidden = first.shape[1]
    return pl.pallas_call(
        grid_hidden_kernel,
        out_shape=(kept((cells, hidden)), kept(second.shape)),
        in_specs=[VMEM] * 2 + [ANY] * 2,
        out_specs=(VMEM, VMEM),
        scratch_shapes=[pltpu.SemaphoreType.DMA],
        compiler_params=pltpu.CompilerParams(vmem_limit_bytes=12 << 20),
        cost_estimate=pl.CostEstimate(
            flops=2 * cells * depth * hidden, bytes_accessed=2 * (cells + hidden) * depth, transcendentals=0
        ),
        name="grid_hidden",
    )(encoded, first, *in_hbm(second), after)


def mesh_hidden_kernel(back_own, ring_own, ring_near, first, out_ref):
    rows = ring_own.shape[0]
    out_ref[rows:REACH * rows, :] = halved(back_own[...], first[...]).astype(BF16)
    out_ref[REACH * rows:(REACH + 1) * rows, :] = halved(ring_own[...], first[...]).astype(BF16)
    out_ref[(REACH + 1) * rows:, :] = halved(ring_near[...], first[...]).astype(BF16)


def mesh_hidden(back_own, ring_own, ring_near, first):
    rows, depth = ring_own.shape
    return pl.pallas_call(
        mesh_hidden_kernel,
        out_shape=kept(((2 * REACH + 1) * rows, first.shape[1])),
        in_specs=[VMEM] * 4,
        out_specs=VMEM,
        compiler_params=pltpu.CompilerParams(vmem_limit_bytes=12 << 20),
        cost_estimate=pl.CostEstimate(
            flops=8 * rows * depth * first.shape[1], bytes_accessed=2 * rows * depth, transcendentals=0
        ),
        name="mesh_hidden",
    )(back_own, ring_own, ring_near, first)


def decode_kernel(
    owner_hbm, weight_ref, ring_own, ring_near, back_own, back_near, grid_ref, mesh_in, enc_ref, first, second,
    out_hbm, mesh_hbm, mesh_ref,
    owner, x_ref, act, ring, io_sems,
):
    del mesh_in
    rows = ring_own.shape[0]
    tile, part = tiles_of(x_ref.shape[0], first.shape[1])
    tile = min(tile, 256)
    tiles, parts = x_ref.shape[0] // tile, first.shape[1] // part
    stores = [pltpu.make_async_copy(ring_own, mesh_hbm, io_sems.at[x_ref.shape[0] // rows])]
    index = pltpu.make_async_copy(owner_hbm, owner, io_sems.at[x_ref.shape[0] // rows + 1])
    index.start()
    stores[0].start()
    mine, count = lax.axis_index(AXES), lax.axis_size(AXES)
    outward = outward_of()
    mesh_ref[:rows, :] = halved(back_near[...], first[...]).astype(BF16)
    ring[:rows, :] = back_near[...]
    ring[rows:2 * rows, :] = back_own[...]
    ring[2 * rows:3 * rows, :] = ring_own[...]
    ring[3 * rows:, :] = ring_near[...]
    columns = jnp.transpose(weight_ref[...])
    index.wait()
    for r in range(tiles):
        cut = slice(r * tile, (r + 1) * tile)
        reads = []
        for b in range(r * tile // rows, (r + 1) * tile // rows):
            slot = outward * offset_of(owner[b], mine, count) + REACH
            lines = pl.ds(pl.multiple_of(slot * rows, rows), rows)
            block = slice(b * rows, (b + 1) * rows)
            weight = columns[:, b:b + 1]
            narrow = weight.astype(BF16)
            for j in range(parts):
                cols = slice(j * part, (j + 1) * part)
                half = grid_ref[block, cols] + narrow * mesh_ref[lines, cols]
                act[block, cols] = half * jnp.tanh(half) + half
            reads.append((block, weight, lines))
        out = jnp.dot(act[cut, :], second[...], preferred_element_type=F32)
        for n, (block, weight, lines) in enumerate(reads):
            rest = enc_ref[block, :].astype(F32) + weight * ring[lines, :].astype(F32)
            x_ref[block, :] = (rest + out[n * rows:(n + 1) * rows, :]).astype(BF16)
            copy = pltpu.make_async_copy(x_ref.at[block], out_hbm.at[block], io_sems.at[r * tile // rows + n])
            copy.start()
            stores.append(copy)
    for copy in stores:
        copy.wait()


def decode(owner, weights, ring_own, ring_near, back_own, back_near, grid_part, mesh_part, encoded, first, second):
    cells, depth = encoded.shape
    hidden = first.shape[1]
    rows = ring_own.shape[0]
    return pl.pallas_call(
        decode_kernel,
        out_shape=(
            jax.ShapeDtypeStruct((cells, depth), BF16),
            jax.ShapeDtypeStruct((rows, depth), BF16),
            kept(mesh_part.shape),
        ),
        in_specs=[ANY] + [VMEM] * 10,
        out_specs=(ANY, ANY, VMEM),
        input_output_aliases={7: 2},
        scratch_shapes=[
            pltpu.SMEM(owner.shape, jnp.int32),
            pltpu.VMEM((cells, depth), BF16),
            pltpu.VMEM((cells, hidden), BF16),
            pltpu.VMEM(((2 * REACH + 1) * rows, depth), BF16),
            pltpu.SemaphoreType.DMA((cells // rows + 2,)),
        ],
        compiler_params=pltpu.CompilerParams(vmem_limit_bytes=16 << 20),
        cost_estimate=pl.CostEstimate(
            flops=2 * cells * depth * hidden, bytes_accessed=4 * (cells + hidden) * depth, transcendentals=cells * hidden
        ),
        name="decode",
    )(*in_hbm(owner), weights, ring_own, ring_near, back_own, back_near, grid_part, mesh_part, encoded, first, second)[:2]


def on_device(
    grid, g2m_owner, g2m_weight, m2g_owner, m2g_weight, mesh_feat, neighbours,
    enc_w1, enc_w2, attn_gain, w_qkv, w_out, dec_w1, dec_w2,
):
    rows = mesh_feat.shape[0]
    nblocks = g2m_owner.shape[0]
    encoded, message, base, local, first = encode(
        g2m_owner, neighbours, g2m_weight.reshape(nblocks, rows), mesh_feat, grid, enc_w1, enc_w2, dec_w1
    )
    outgoing = outgoing_sums(base, swapped(message))
    sums = from_outward(outgoing, 1)
    grid_part, second = grid_hidden(encoded, first, dec_w2, outgoing)
    share, message = chip_share(local, sums, grid_part)
    own, pair, message = chip_states(share, swapped(message))
    near = from_outward(message, 1)
    far = from_outward(message, 2)
    behind = swapped(near[:rows])
    query, kv = project(pair, near, attn_gain, w_qkv[0])
    ring_own = attend_own(base, own, query, kv, behind, attn_gain, w_qkv[0], w_out[0])
    ring_near = attend_near(sums, near, query, kv, far, attn_gain, w_qkv[0], w_out[0], ring_own)
    back_own = swapped(ring_own)
    back_near = swapped(ring_near[:rows])
    mesh_part = mesh_hidden(back_own, ring_own, ring_near, first)
    return decode(
        m2g_owner, m2g_weight.reshape(nblocks, rows), ring_own, ring_near, back_own, back_near,
        grid_part, mesh_part, encoded, first, second,
    )


def solution(mesh):
    split = P(AXES, None)
    flat = P(AXES)
    in_specs = (split, flat, flat, flat, flat, split, split) + (P(),) * 7
    return jax.shard_map(
        on_device, mesh=mesh, in_specs=in_specs, out_specs=(split, split), check_vma=False
    )
```

```python
import functools

import jax
import jax.numpy as jnp
from jax import lax
from jax.experimental import pallas as pl
from jax.experimental.pallas import tpu as pltpu
from jax.sharding import PartitionSpec as P

HD = 128
REACH = 2
LOG2E = 1.4426950408889634
EXTRA = 16
LANES = 128
AXES = ("tile", "sub")
BF16 = jnp.bfloat16
F32 = jnp.float32
VMEM = pl.BlockSpec(memory_space=pltpu.VMEM)
SMEM = pl.BlockSpec(memory_space=pltpu.SMEM)
ANY = pl.BlockSpec(memory_space=pl.ANY)


def swapped(block):
    count = lax.axis_size(AXES)
    return lax.ppermute(block, AXES, [(i, i ^ 1) for i in range(count)])


def from_outward(block, chips):
    count = lax.axis_size(AXES)
    route = []
    for i in range(count):
        step = 2 * chips - 1
        route.append((i, (i + step if i % 2 else i - step) % count))
    return lax.ppermute(block, AXES, route)


def tiles_of(rows, columns):
    return min(rows, 1024), min(columns, 1024)


def outward_of():
    return 2 * lax.axis_index("sub") - 1


def offset_of(owner, mine, count):
    return lax.rem(owner - mine + REACH + count, count) - REACH


def kept(shape, dtype=BF16):
    return pltpu.VMEM(shape, dtype)


def in_hbm(*arrays):
    return [pltpu.with_memory_space_constraint(a, pltpu.HBM) for a in arrays]


def strips(depth):
    return [slice(k, k + LANES) for k in range(0, depth, LANES)]


def spread(ref, first, block):
    rows = block.shape[0]
    for k, cols in enumerate(strips(block.shape[1])):
        ref[first + k * rows:first + (k + 1) * rows, :] = block[:, cols].astype(BF16)


def hidden_layer(x_ref, first, act, tile, part, arrive, before):
    for j in range(first.shape[1] // part):
        before(j)
        cols = slice(j * part, (j + 1) * part)
        for r in range(x_ref.shape[0] // tile):
            if j == 0:
                arrive(r)
            cut = slice(r * tile, (r + 1) * tile)
            half = jnp.dot(x_ref[cut, :] * BF16(0.5), first[:, cols], preferred_element_type=F32)
            act[cut, cols] = (half * jnp.tanh(half) + half).astype(BF16)


def encode_kernel(
    owner_hbm, listed_hbm, weight_hbm, feat_hbm, x_hbm, first_hbm, second_hbm, next_hbm,
    enc_ref, msg_ref, base_ref, loc_ref, next_ref,
    owner, listed, weight_ref, feat_ref, first, second, act, total, sems, io_sems,
):
    rows, depth = feat_ref.shape
    tile, part = tiles_of(enc_ref.shape[0], first.shape[1])
    tiles, parts = enc_ref.shape[0] // tile, first.shape[1] // part
    loads = [
        pltpu.make_async_copy(x_hbm.at[pl.ds(r * tile, tile)], enc_ref.at[pl.ds(r * tile, tile)], io_sems.at[r])
        for r in range(tiles)
    ]
    ones, twos = [], []
    for j in range(parts):
        cut = pl.ds(j * part, part)
        ones.append(pltpu.make_async_copy(first_hbm.at[:, cut], first.at[:, cut], sems.at[0, j]))
        twos.append(pltpu.make_async_copy(second_hbm.at[cut], second.at[cut], sems.at[1, j]))
    small = [
        pltpu.make_async_copy(weight_hbm, weight_ref, io_sems.at[tiles]),
        pltpu.make_async_copy(feat_hbm, feat_ref, io_sems.at[tiles + 1]),
        pltpu.make_async_copy(owner_hbm, owner, io_sems.at[tiles + 2]),
        pltpu.make_async_copy(listed_hbm, listed, io_sems.at[tiles + 3]),
    ]
    later = pltpu.make_async_copy(next_hbm, next_ref, io_sems.at[tiles + 4])
    for copy in loads + ones + twos + small + [later]:
        copy.start()

    def arrive(r):
        if r == 0:
            for copy in loads:
                copy.wait()

    mine, count = lax.axis_index(AXES), lax.axis_size(AXES)
    outward = outward_of()
    total[...] = jnp.zeros_like(total)

    def before(j):
        due = ones[:1] if j == 0 else []
        if j == min(1, parts - 1):
            due = due + ones[1:] + twos + small
        for copy in due:
            copy.wait()

    hidden_layer(enc_ref, first, act, tile, part, arrive, before)
    columns = jnp.transpose(weight_ref[...])
    tile = min(tile, 512)
    for r in range(enc_ref.shape[0] // tile):
        cut = slice(r * tile, (r + 1) * tile)
        out = enc_ref[cut, :].astype(F32) + jnp.dot(act[cut, :], second[...], preferred_element_type=F32)
        enc_ref[cut, :] = out.astype(BF16)
        for b in range(r * tile // rows, (r + 1) * tile // rows):
            slot = outward * offset_of(owner[b], mine, count) + REACH
            total[slot] += columns[:, b:b + 1] * out[b * rows - r * tile:(b + 1) * rows - r * tile, :]
    absent = sum(-offset_of(listed[0, n], mine, count) for n in range(listed.shape[1])).astype(F32)
    spot = lax.broadcasted_iota(jnp.int32, (EXTRA, LANES), 1)
    lines = rows * depth // LANES
    spread(msg_ref, 0, total[0])
    msg_ref[lines:, :] = jnp.where(spot == 1, absent, 0.0).astype(BF16)
    spread(base_ref, 0, total[4])
    spread(base_ref, lines, total[3])
    base_ref[2 * lines:, :] = jnp.where(spot == 0, absent, 0.0).astype(BF16)
    loc_ref[:rows, :] = total[1]
    loc_ref[rows:, :] = total[2] + feat_ref[...].astype(F32)
    later.wait()


def encode(owner, listed, weights, feat, grid, first, second, following):
    cells, depth = grid.shape
    hidden = first.shape[1]
    rows = feat.shape[0]
    tile, part = tiles_of(cells, hidden)
    return pl.pallas_call(
        encode_kernel,
        out_shape=(
            kept((cells, depth)),
            kept((rows * depth // LANES + EXTRA, LANES)),
            kept((2 * rows * depth // LANES + EXTRA, LANES)),
            kept((2 * rows, depth), F32),
            kept(following.shape),
        ),
        in_specs=[ANY] * 8,
        out_specs=(VMEM,) * 5,
        scratch_shapes=[
            pltpu.SMEM(owner.shape, jnp.int32),
            pltpu.SMEM(listed.shape, jnp.int32),
            pltpu.VMEM(weights.shape, F32),
            pltpu.VMEM(feat.shape, BF16),
            pltpu.VMEM((depth, hidden), BF16),
            pltpu.VMEM((hidden, depth), BF16),
            pltpu.VMEM((cells, hidden), BF16),
            pltpu.VMEM((2 * REACH + 1, rows, depth), F32),
            pltpu.SemaphoreType.DMA((2, hidden // part)),
            pltpu.SemaphoreType.DMA((cells // tile + 5,)),
        ],
        compiler_params=pltpu.CompilerParams(vmem_limit_bytes=24 << 20),
        cost_estimate=pl.CostEstimate(
            flops=4 * cells * depth * hidden, bytes_accessed=4 * (cells + hidden) * depth, transcendentals=cells * hidden
        ),
        name="encode",
    )(*in_hbm(owner, listed, weights, feat, grid, first, second, following))


def outgoing_kernel(base_ref, arrived_ref, out_ref):
    rows = arrived_ref.shape[0] - EXTRA
    out_ref[:rows, :] = base_ref[:rows, :]
    out_ref[rows:, :] = (base_ref[rows:, :].astype(F32) + arrived_ref[...].astype(F32)).astype(BF16)


def outgoing_sums(base, arrived):
    return pl.pallas_call(
        outgoing_kernel, out_shape=kept(base.shape), in_specs=[VMEM] * 2, out_specs=VMEM,
        compiler_params=pltpu.CompilerParams(vmem_limit_bytes=4 << 20), name="outgoing_sums"
    )(base, arrived)


def share_kernel(loc_ref, arrived_ref, after, share_ref, msg_ref):
    del after
    rows, depth = loc_ref.shape[0] // 2, loc_ref.shape[1]
    for half in range(2):
        cut = slice(half * rows, (half + 1) * rows)
        for k, cols in enumerate(strips(depth)):
            line = (half * depth // LANES + k) * rows
            share_ref[cut, cols] = loc_ref[cut, cols] + arrived_ref[line:line + rows, :].astype(F32)
    msg_ref[:rows, :] = share_ref[rows:, :].astype(BF16)
    msg_ref[rows:, :] = share_ref[:rows, :].astype(BF16)


def chip_share(local, arrived, after):
    return pl.pallas_call(
        share_kernel,
        out_shape=(kept(local.shape, F32), kept(local.shape)),
        in_specs=[VMEM] * 2 + [ANY],
        out_specs=(VMEM,) * 2,
        compiler_params=pltpu.CompilerParams(vmem_limit_bytes=4 << 20),
        name="chip_share",
    )(local, arrived, after)


def state_kernel(share_ref, other_ref, own_ref, pair_ref, msg_ref):
    rows = own_ref.shape[0]
    own_ref[...] = share_ref[rows:, :] + other_ref[rows:, :].astype(F32)
    pair_ref[:rows, :] = (share_ref[:rows, :] + other_ref[:rows, :].astype(F32)).astype(BF16)
    pair_ref[rows:, :] = own_ref[...].astype(BF16)
    msg_ref[:rows, :] = pair_ref[rows:, :]
    msg_ref[rows:, :] = pair_ref[:rows, :]


def chip_states(share, other):
    rows, depth = share.shape[0] // 2, share.shape[1]
    return pl.pallas_call(
        state_kernel,
        out_shape=(kept((rows, depth), F32), kept(share.shape), kept(share.shape)),
        in_specs=[VMEM] * 2,
        out_specs=(VMEM,) * 3,
        compiler_params=pltpu.CompilerParams(vmem_limit_bytes=4 << 20),
        name="chip_states",
    )(share, other)


def normal(block, gain):
    state = block.astype(F32)
    scale = lax.rsqrt(jnp.mean(state * state, axis=-1, keepdims=True) + 1e-6)
    return (state * scale * gain).astype(BF16)


def project_kernel(pair_ref, near_ref, gain_ref, w_qkv, query_ref, kv_ref, normed):
    rows, depth = pair_ref.shape[0] // 2, pair_ref.shape[1]
    gain = gain_ref[...]
    normed[:2 * rows, :] = normal(pair_ref[...], gain)
    normed[2 * rows:, :] = normal(near_ref[...], gain)
    kv_ref[...] = jnp.dot(normed[...], w_qkv[:, depth:], preferred_element_type=F32).astype(BF16)
    query_ref[...] = jnp.dot(normed[rows:, :], w_qkv[:, :depth], preferred_element_type=F32).astype(BF16)


def project(pair, near, gain, w_qkv):
    rows, depth = pair.shape[0] // 2, pair.shape[1]
    return pl.pallas_call(
        project_kernel,
        out_shape=(kept((3 * rows, depth)), kept((4 * rows, 2 * depth))),
        in_specs=[VMEM] * 4,
        out_specs=(VMEM,) * 2,
        scratch_shapes=[pltpu.VMEM((4 * rows, depth), BF16)],
        compiler_params=pltpu.CompilerParams(vmem_limit_bytes=8 << 20),
        cost_estimate=pl.CostEstimate(
            flops=22 * rows * depth * depth, bytes_accessed=2 * rows * depth, transcendentals=0
        ),
        name="project",
    )(pair, near, gain, w_qkv)


def attention(items):
    units = [
        (n, slice(h * HD, (h + 1) * HD)) for n, (query, _, _) in enumerate(items) for h in range(query.shape[1] // HD)
    ]
    scores = [
        jnp.concatenate([
            lax.dot_general(
                items[n][0][:, cols], ref[first:first + size, cols], (((1,), (1,)), ((), ())), preferred_element_type=F32
            )
            for ref, first, size in items[n][1]
        ], axis=1)
        for n, cols in units
    ]
    scores = [jnp.where(items[n][2], score, -jnp.inf) for (n, _), score in zip(units, scores)]
    below = [(score - jnp.max(score, axis=-1, keepdims=True)) * (HD ** -0.5 * LOG2E) for score in scores]
    grown = [jnp.exp2(score.astype(BF16)) for score in below]
    heads = [[] for _ in items]
    for (n, cols), weights in zip(units, grown):
        query, window, _ = items[n]
        depth = query.shape[1]
        start, taken = 0, None
        for ref, first, size in window:
            value = ref[first:first + size, depth + cols.start:depth + cols.stop]
            value = jnp.concatenate([value, jnp.ones((size, HD), BF16)], axis=1)
            term = jnp.dot(weights[:, start:start + size], value, preferred_element_type=F32)
            taken = term if taken is None else taken + term
            start += size
        heads[n].append((taken[:, :HD] / taken[:, HD:]).astype(BF16))
    return [jnp.concatenate(parts, axis=1) for parts in heads]


def kept_lanes(rows, absent):
    block = (lax.broadcasted_iota(jnp.int32, (rows, (2 * REACH + 1) * rows), 1) // rows).astype(F32)
    return block != outward_of().astype(F32) * absent + REACH


def attend_own_kernel(base_ref, own_ref, query_ref, kv_ref, behind_ref, gain_ref, w_qkv, w_out, ring_ref, kv_behind):
    rows, depth = own_ref.shape
    kv_behind[...] = jnp.dot(
        normal(behind_ref[...], gain_ref[...]), w_qkv[:, depth:], preferred_element_type=F32
    ).astype(BF16)
    keep = kept_lanes(rows, base_ref[2 * rows * depth // LANES:, :].astype(F32)[0:1, 0:1])
    mixed = attention([(query_ref[:rows, :], [(kv_behind, 0, rows), (kv_ref, 0, 4 * rows)], keep)])[0]
    ring_ref[...] = (own_ref[...] + jnp.dot(mixed, w_out[...], preferred_element_type=F32)).astype(BF16)


def attend_near_kernel(
    sums_ref, near_ref, query_ref, kv_ref, far_ref, gain_ref, w_qkv, w_out, after, ring_ref, kv_far, mixed
):
    del after
    rows, depth = near_ref.shape[0] // 2, near_ref.shape[1]
    kv_far[...] = jnp.dot(
        normal(far_ref[...], gain_ref[...]), w_qkv[:, depth:], preferred_element_type=F32
    ).astype(BF16)
    windows = [
        [(kv_ref, 0, 4 * rows), (kv_far, 0, rows)],
        [(kv_ref, rows, 3 * rows), (kv_far, 0, 2 * rows)],
    ]
    items = []
    for n, window in enumerate(windows):
        keep = kept_lanes(rows, sums_ref[2 * rows * depth // LANES:, :].astype(F32)[0:1, n:n + 1])
        items.append((query_ref[(n + 1) * rows:(n + 2) * rows, :], window, keep))
    for n, block in enumerate(attention(items)):
        mixed[n * rows:(n + 1) * rows, :] = block
    added = jnp.dot(mixed[...], w_out[...], preferred_element_type=F32)
    ring_ref[...] = (near_ref[...].astype(F32) + added).astype(BF16)


def attend_own(base, own, query, kv, behind, gain, w_qkv, w_out):
    rows, depth = own.shape
    return pl.pallas_call(
        attend_own_kernel,
        out_shape=kept((rows, depth)),
        in_specs=[VMEM] * 8,
        out_specs=VMEM,
        scratch_shapes=[pltpu.VMEM((rows, 2 * depth), BF16)],
        compiler_params=pltpu.CompilerParams(vmem_limit_bytes=12 << 20),
        cost_estimate=pl.CostEstimate(
            flops=20 * rows * depth * depth, bytes_accessed=2 * rows * depth, transcendentals=0
        ),
        name="attend_own",
    )(base, own, query, kv, behind, gain, w_qkv, w_out)


def attend_near(sums, near, query, kv, far, gain, w_qkv, w_out, after):
    rows, depth = near.shape[0] // 2, near.shape[1]
    return pl.pallas_call(
        attend_near_kernel,
        out_shape=kept((2 * rows, depth)),
        in_specs=[VMEM] * 8 + [ANY],
        out_specs=VMEM,
        scratch_shapes=[pltpu.VMEM((2 * rows, 2 * depth), BF16), pltpu.VMEM((2 * rows, depth), BF16)],
        compiler_params=pltpu.CompilerParams(vmem_limit_bytes=12 << 20),
        cost_estimate=pl.CostEstimate(
            flops=40 * rows * depth * depth, bytes_accessed=2 * rows * depth, transcendentals=0
        ),
        name="attend_near",
    )(sums, near, query, kv, far, gain, w_qkv, w_out, after)


def halved(rows, first):
    return jnp.dot(rows * BF16(0.5), first, preferred_element_type=F32)


def grid_hidden_kernel(enc_ref, first, second_hbm, after, out_ref, second, sem):
    del after
    copy = pltpu.make_async_copy(second_hbm, second, sem)
    copy.start()
    tile, part = tiles_of(*out_ref.shape)
    for j in range(out_ref.shape[1] // part):
        cols = slice(j * part, (j + 1) * part)
        for r in range(out_ref.shape[0] // tile):
            cut = slice(r * tile, (r + 1) * tile)
            out_ref[cut, cols] = halved(enc_ref[cut, :], first[:, cols]).astype(BF16)
    copy.wait()


def grid_hidden(encoded, first, second, after):
    cells, depth = encoded.shape
    hidden = first.shape[1]
    return pl.pallas_call(
        grid_hidden_kernel,
        out_shape=(kept((cells, hidden)), kept(second.shape)),
        in_specs=[VMEM] * 2 + [ANY] * 2,
        out_specs=(VMEM, VMEM),
        scratch_shapes=[pltpu.SemaphoreType.DMA],
        compiler_params=pltpu.CompilerParams(vmem_limit_bytes=12 << 20),
        cost_estimate=pl.CostEstimate(
            flops=2 * cells * depth * hidden, bytes_accessed=2 * (cells + hidden) * depth, transcendentals=0
        ),
        name="grid_hidden",
    )(encoded, first, *in_hbm(second), after)


def mesh_hidden_kernel(back_own, ring_own, ring_near, first, out_ref):
    rows = ring_own.shape[0]
    out_ref[rows:REACH * rows, :] = halved(back_own[...], first[...]).astype(BF16)
    out_ref[REACH * rows:(REACH + 1) * rows, :] = halved(ring_own[...], first[...]).astype(BF16)
    out_ref[(REACH + 1) * rows:, :] = halved(ring_near[...], first[...]).astype(BF16)


def mesh_hidden(back_own, ring_own, ring_near, first):
    rows, depth = ring_own.shape
    return pl.pallas_call(
        mesh_hidden_kernel,
        out_shape=kept(((2 * REACH + 1) * rows, first.shape[1])),
        in_specs=[VMEM] * 4,
        out_specs=VMEM,
        compiler_params=pltpu.CompilerParams(vmem_limit_bytes=12 << 20),
        cost_estimate=pl.CostEstimate(
            flops=8 * rows * depth * first.shape[1], bytes_accessed=2 * rows * depth, transcendentals=0
        ),
        name="mesh_hidden",
    )(back_own, ring_own, ring_near, first)


def decode_kernel(
    owner_hbm, weight_ref, ring_own, ring_near, back_own, back_near, grid_ref, mesh_in, enc_ref, first, second,
    out_hbm, mesh_hbm, mesh_ref,
    owner, x_ref, act, ring, io_sems,
):
    del mesh_in
    rows = ring_own.shape[0]
    tile, part = tiles_of(x_ref.shape[0], first.shape[1])
    tile = min(tile, 256)
    tiles, parts = x_ref.shape[0] // tile, first.shape[1] // part
    stores = [pltpu.make_async_copy(ring_own, mesh_hbm, io_sems.at[x_ref.shape[0] // rows])]
    index = pltpu.make_async_copy(owner_hbm, owner, io_sems.at[x_ref.shape[0] // rows + 1])
    index.start()
    stores[0].start()
    mine, count = lax.axis_index(AXES), lax.axis_size(AXES)
    outward = outward_of()
    mesh_ref[:rows, :] = halved(back_near[...], first[...]).astype(BF16)
    columns = jnp.transpose(weight_ref[...])
    index.wait()
    for r in range(tiles):
        cut = slice(r * tile, (r + 1) * tile)
        reads = []
        for b in range(r * tile // rows, (r + 1) * tile // rows):
            slot = outward * offset_of(owner[b], mine, count) + REACH
            lines = pl.ds(pl.multiple_of(slot * rows, rows), rows)
            block = slice(b * rows, (b + 1) * rows)
            weight = columns[:, b:b + 1]
            narrow = weight.astype(BF16)
            for j in range(parts):
                cols = slice(j * part, (j + 1) * part)
                half = grid_ref[block, cols] + narrow * mesh_ref[lines, cols]
                act[block, cols] = half * jnp.tanh(half) + half
            reads.append((block, weight, lines))
        out = jnp.dot(act[cut, :], second[...], preferred_element_type=F32)
        if r == 0:
            ring[:rows, :] = back_near[...]
            ring[rows:2 * rows, :] = back_own[...]
            ring[2 * rows:3 * rows, :] = ring_own[...]
            ring[3 * rows:, :] = ring_near[...]
        for n, (block, weight, lines) in enumerate(reads):
            rest = enc_ref[block, :].astype(F32) + weight * ring[lines, :].astype(F32)
            x_ref[block, :] = (rest + out[n * rows:(n + 1) * rows, :]).astype(BF16)
            copy = pltpu.make_async_copy(x_ref.at[block], out_hbm.at[block], io_sems.at[r * tile // rows + n])
            copy.start()
            stores.append(copy)
    for copy in stores:
        copy.wait()


def decode(owner, weights, ring_own, ring_near, back_own, back_near, grid_part, mesh_part, encoded, first, second):
    cells, depth = encoded.shape
    hidden = first.shape[1]
    rows = ring_own.shape[0]
    return pl.pallas_call(
        decode_kernel,
        out_shape=(
            jax.ShapeDtypeStruct((cells, depth), BF16),
            jax.ShapeDtypeStruct((rows, depth), BF16),
            kept(mesh_part.shape),
        ),
        in_specs=[ANY] + [VMEM] * 10,
        out_specs=(ANY, ANY, VMEM),
        input_output_aliases={7: 2},
        scratch_shapes=[
            pltpu.SMEM(owner.shape, jnp.int32),
            pltpu.VMEM((cells, depth), BF16),
            pltpu.VMEM((cells, hidden), BF16),
            pltpu.VMEM(((2 * REACH + 1) * rows, depth), BF16),
            pltpu.SemaphoreType.DMA((cells // rows + 2,)),
        ],
        compiler_params=pltpu.CompilerParams(vmem_limit_bytes=16 << 20),
        cost_estimate=pl.CostEstimate(
            flops=2 * cells * depth * hidden, bytes_accessed=4 * (cells + hidden) * depth, transcendentals=cells * hidden
        ),
        name="decode",
    )(*in_hbm(owner), weights, ring_own, ring_near, back_own, back_near, grid_part, mesh_part, encoded, first, second)[:2]


def on_device(
    grid, g2m_owner, g2m_weight, m2g_owner, m2g_weight, mesh_feat, neighbours,
    enc_w1, enc_w2, attn_gain, w_qkv, w_out, dec_w1, dec_w2,
):
    rows = mesh_feat.shape[0]
    nblocks = g2m_owner.shape[0]
    encoded, message, base, local, first = encode(
        g2m_owner, neighbours, g2m_weight.reshape(nblocks, rows), mesh_feat, grid, enc_w1, enc_w2, dec_w1
    )
    outgoing = outgoing_sums(base, swapped(message))
    sums = from_outward(outgoing, 1)
    grid_part, second = grid_hidden(encoded, first, dec_w2, outgoing)
    share, message = chip_share(local, sums, grid_part)
    own, pair, message = chip_states(share, swapped(message))
    near = from_outward(message, 1)
    far = from_outward(message, 2)
    behind = swapped(near[:rows])
    query, kv = project(pair, near, attn_gain, w_qkv[0])
    ring_own = attend_own(base, own, query, kv, behind, attn_gain, w_qkv[0], w_out[0])
    ring_near = attend_near(sums, near, query, kv, far, attn_gain, w_qkv[0], w_out[0], ring_own)
    back_own = swapped(ring_own)
    back_near = swapped(ring_near[:rows])
    mesh_part = mesh_hidden(back_own, ring_own, ring_near, first)
    return decode(
        m2g_owner, m2g_weight.reshape(nblocks, rows), ring_own, ring_near, back_own, back_near,
        grid_part, mesh_part, encoded, first, second,
    )


def solution(mesh):
    split = P(AXES, None)
    flat = P(AXES)
    in_specs = (split, flat, flat, flat, flat, split, split) + (P(),) * 7
    return jax.shard_map(
        on_device, mesh=mesh, in_specs=in_specs, out_specs=(split, split), check_vma=False
    )
```
